32 devices in a mesh: rep: 4 (over y, x), blk: 8 (over z, core).
Axes of the slice: x: 2, y: 2, z: 4, core: 2. Of those that a mesh axis runs over, the one named last changes fastest.
Arguments:
- item_factors: bfloat16 [16384, 256], P('blk')
- ratings: bfloat16 [8192, 2048], P(('rep', 'blk')), may hold values from 0.049804688 to 2
- block_ids: int32 [64, 16], P(('rep', 'blk')), may hold values from 0 to 127, as said below
- live_counts: int32 [64], P(('rep', 'blk')), may hold values from 1 to 16, as said below
- owner_rows: int32 [8192], P(('rep', 'blk')), may hold values from 0 to 8191, as said below
Outputs:
- user_factors: float32 [8192, 256], P(('rep', 'blk'))
The draws below stay inside these ranges and needn't reach their ends.
Inputs may be any that keep to these rules, and one draw needn't show every extreme that they name: `block_ids`: slot s of every row batch names a block of item panel s // 2, that is a number from (s // 2) * 16 to that plus 2048 // 128 - 1; the slots of one batch name different blocks. `live_counts`: the first row batch of every device has all 16 slots live. `owner_rows`: A permutation of the users; of the 256 users of any device, exactly 8 land in the rows of each device.
All inputs are finite; a program needn't handle non-finite values.
Results may differ from the reference program's by a relative error of at most 0.0039.
Values may be sent and summed in bfloat16 or wider, within the bound.
No kernel may reach another device: no remote copies, remote signals or barrier semaphores. Data moves between devices by JAX's collectives and lax.ppermute only.
A program may use at most 128 MiB of HBM per device.

```python
import math
import jax
import jax.numpy as jnp
from jax import lax

F = 256
BS = 128
RB = 128
NPER = 2
ITERS = 8
ITEM_DEV = 2048
U_DEV = 256
NB = 16
K = 2048
BATCHES = 2
USERS = 8192
NBAT = 64
ITEMS = 16384


def draw_item_factors(key, part):
    first, second = jax.random.split(jax.random.fold_in(key, 11), 2)
    panel_index = (jnp.arange(ITEMS) // ITEM_DEV).astype(jnp.float32)
    panel_total = max(ITEMS // ITEM_DEV - 1, 1)
    panel_scale = (0.5 * jnp.exp(math.log(4.0) * panel_index / panel_total))[:, None]
    base = jax.random.normal(first, (ITEMS, F), jnp.float32)
    column = jnp.exp(jax.random.uniform(second, (1, F), jnp.float32, math.log(0.15), math.log(1.5)))
    return (base * column * panel_scale * ITEMS ** (-0.5)).astype(jnp.bfloat16)


def draw_block_ids(key, part):
    owners = NB // NPER
    per_panel = ITEM_DEV // BS
    keys = jax.random.split(jax.random.fold_in(key, 22), NBAT * owners)
    picks = jax.vmap(lambda single: jax.random.permutation(single, per_panel)[:NPER])(keys)
    picks = picks.astype(jnp.int32).reshape(NBAT, owners, NPER)
    offsets = (jnp.arange(owners, dtype=jnp.int32) * per_panel)[None, :, None]
    return (picks + offsets).reshape(NBAT, NB).astype(jnp.int32)


def draw_live_counts(key, part):
    counts = jax.random.randint(jax.random.fold_in(key, 33), (NBAT,), 1, NB + 1, jnp.int32)
    first_batch = jnp.arange(NBAT, dtype=jnp.int32) % BATCHES == 0
    return jnp.where(first_batch, NB, counts).astype(jnp.int32)


def draw_owner_rows(key, part):
    devices = USERS // U_DEV
    quota = U_DEV // devices
    first, second = jax.random.split(jax.random.fold_in(key, 44))
    local_perm = jax.vmap(lambda single: jax.random.permutation(single, U_DEV))(jax.random.split(first, devices)).astype(jnp.int32)
    slot_perm = jax.vmap(lambda single: jax.random.permutation(single, U_DEV))(jax.random.split(second, devices)).astype(jnp.int32)
    position = jnp.arange(U_DEV, dtype=jnp.int32)
    target_dev = position % devices
    source = jnp.arange(devices, dtype=jnp.int32)[:, None]
    slot = source * quota + (position // devices)[None, :]
    target = target_dev[None, :] * U_DEV + slot_perm[target_dev[None, :], slot]
    result = jax.vmap(lambda order, values: jnp.zeros((U_DEV,), jnp.int32).at[order].set(values))(local_perm, target.astype(jnp.int32))
    return result.reshape(USERS).astype(jnp.int32)


def levels(stream_key, dims, cuts, smallest, top_value):
    def one(dim, shards_of):
        heights = jax.random.uniform(jax.random.fold_in(jax.random.fold_in(stream_key, 6), dim), (shards_of,), jnp.float32, smallest / len(cuts), top_value / len(cuts))
        return jnp.repeat(jnp.exp(heights), dims[dim] // shards_of).reshape((-1,) + (1,) * (len(dims) - dim - 1))

    factor_of = one(*cuts[0])
    for cut in cuts[1:]:
        factor_of = factor_of * one(*cut)
    return factor_of


def setup_inputs(seed: int = 0) -> dict:
    seeds = jax.random.split(jax.random.key(seed), 6)
    return {
        "item_factors": draw_item_factors(jax.random.fold_in(seeds[5], 71), 0),
        "ratings": jnp.clip(jnp.exp(math.log(2.0) - 3.6927934 * jax.random.uniform(seeds[1], (USERS, K), jnp.float32) ** levels(seeds[1], (USERS, K), ((0, 32),), -0.2, 0.2)), 0.049804688, 2.0).astype(jnp.bfloat16),
        "block_ids": draw_block_ids(jax.random.fold_in(seeds[5], 71), 0),
        "live_counts": draw_live_counts(jax.random.fold_in(seeds[5], 71), 0),
        "owner_rows": draw_owner_rows(jax.random.fold_in(seeds[5], 71), 0),
    }


conf_scale = 6.0
ridge_term = 0.5


def solve_batch(panel_rows, weight, target, gram_matrix):
    prec_high = lax.Precision.HIGHEST
    factor_rows = panel_rows.astype(jnp.float32)
    target_proj = jnp.dot(target, factor_rows, precision=prec_high)

    def operate(vector):
        projected = jnp.dot(vector, factor_rows.T, precision=prec_high) * weight
        return (jnp.dot(vector, gram_matrix, precision=prec_high)
                + jnp.dot(projected, factor_rows, precision=prec_high) + ridge_term * vector)

    solution = jnp.zeros_like(target_proj)
    residual = target_proj
    direction = target_proj
    norm_now = jnp.sum(residual * residual, axis=1, keepdims=True)
    for step in range(ITERS):
        image = operate(direction)
        step_size = norm_now / jnp.sum(direction * image, axis=1, keepdims=True)
        solution = solution + step_size * direction
        residual = residual - step_size * image
        norm_next = jnp.sum(residual * residual, axis=1, keepdims=True)
        direction = residual + (norm_next / norm_now) * direction
        norm_now = norm_next
    return solution


def reference(item_factors, ratings, block_ids, live_counts, owner_rows):
    gram_matrix = jnp.dot(item_factors.T, item_factors, preferred_element_type=jnp.float32)
    block_table = item_factors.reshape(ITEMS // BS, BS, F)
    slot_of_column = (jnp.arange(K) // BS).astype(jnp.int32)

    def one_batch(inputs):
        batch_ids, batch_live, batch_ratings = inputs
        panel_rows = block_table[batch_ids].reshape(K, F)
        is_live = (slot_of_column < batch_live).astype(jnp.float32)[None, :]
        weight = conf_scale * batch_ratings.astype(jnp.float32) * is_live
        target = is_live + weight
        return solve_batch(panel_rows, weight, target, gram_matrix)

    solved = lax.map(one_batch, (block_ids, live_counts, ratings.reshape(NBAT, RB, K)))
    solved = solved.reshape(USERS, F)
    return jnp.zeros((USERS, F), jnp.float32).at[owner_rows].set(solved)
```

```python
import functools
import jax
import jax.numpy as jnp
from jax import lax
from jax.experimental import pallas as pl
from jax.experimental.pallas import tpu as pltpu
from jax.sharding import PartitionSpec as P

ITERS = 8
WIDE_ITERS = 2
VMEM_BYTES = 56 * 1024 * 1024

conf_scale = 6.0
ridge_term = 0.5


def dot32(left, right, dims=((1,), (0,))):
    return lax.dot_general(left, right, (dims, ((), ())), preferred_element_type=jnp.float32)


def halves(value):
    high = value.astype(jnp.bfloat16)
    low = (value - high.astype(jnp.float32)).astype(jnp.bfloat16)
    return high, low


def stage_kernel(layout, block_size, batch_count, per_panel, first, *refs):
    where_ref, ids_ref = refs[:2]
    refs = refs[2:]
    panels, refs = refs[: len(layout)], refs[len(layout):]
    if not first:
        gram_in, refs = refs[0], refs[1:]
    gram_ref, rows_ref, cols_ref = refs
    core, rep, chip = where_ref[0], where_ref[1], where_ref[2]
    total = None if first else gram_in[...]
    for ref in panels:
        width = ref.shape[-1]
        flat = ref[...].reshape(-1, width)
        term = dot32(flat, flat, ((0,), (0,)))
        total = term if total is None else total + term
    gram_ref[...] = total
    slots = 2 * per_panel
    for batch in range(batch_count):
        for side in range(2):
            parity = core if side == 0 else 1 - core
            for pick in range(per_panel):
                local = parity * per_panel + pick
                block = ids_ref[batch, chip * slots + local]
                groups = {}
                for ref, (ref_side, part, start) in zip(panels, layout):
                    if ref_side == side:
                        groups.setdefault(part, []).append((start, ref))
                for part, held in groups.items():
                    size = held[0][1].shape[1]
                    within = lax.rem(block, sum(ref.shape[0] for _, ref in held))
                    value = None
                    for start, ref in sorted(held, key=lambda pair: pair[0]):
                        index = jnp.clip(within - start, 0, ref.shape[0] - 1)
                        piece = ref[index]
                        value = piece if value is None else jnp.where(within >= start, piece, value)
                    offset = local * block_size
                    if size < block_size:
                        offset = offset + (rep ^ part) * size
                    rows_ref[batch, pl.ds(pl.multiple_of(offset, size), size), :] = value
        cols_ref[batch] = rows_ref[batch].T


def solve_kernel(chips, block_size, batch_count, *refs):
    where_ref, live_ref, place_ref, ratings_ref, gram_ref = refs[:5]
    rows_refs = refs[5:5 + chips]
    cols_refs = refs[5 + chips:5 + 2 * chips]
    send_ref = refs[5 + 2 * chips]
    weight, gram_high, gram_low, x_s, r_s, p_s, n_s = refs[6 + 2 * chips:]
    chip = where_ref[2]
    users = ratings_ref.shape[0] // batch_count
    span = ratings_ref.shape[1] // chips
    gram = gram_ref[...]
    high, low = halves(gram)
    gram_high[...] = high
    gram_low[...] = low

    for batch in range(batch_count):
        total = None
        for k in range(chips):
            source = lax.rem(chip - k + chips, chips)
            start = pl.multiple_of(source * span, span)
            rated = ratings_ref[batch * users:(batch + 1) * users, pl.ds(start, span)].astype(jnp.float32)
            column = start + lax.broadcasted_iota(jnp.int32, (users, span), 1)
            is_live = (column < live_ref[batch] * block_size).astype(jnp.float32)
            scaled = conf_scale * rated * is_live
            weight[batch, :, k * span:(k + 1) * span] = scaled
            high, low = halves(is_live + scaled)
            term = dot32(jnp.concatenate([high, low], axis=0), rows_refs[k][batch])
            total = term if total is None else total + term
        target_proj = total[:users] + total[users:]
        x_s[batch] = jnp.zeros_like(target_proj)
        r_s[batch] = target_proj
        p_s[batch] = target_proj
        n_s[batch] = jnp.sum(target_proj * target_proj, axis=1, keepdims=True)

    def step(wide):
        def body(_, carry):
            for batch in range(batch_count):
                direction = p_s[batch]
                high, low = halves(direction)
                both = jnp.concatenate([high, low], axis=0)
                moving = both if wide else high
                total = None
                for k in range(chips):
                    projected = dot32(moving, cols_refs[k][batch])
                    if wide:
                        projected = projected[:users] + projected[users:]
                    projected = projected * weight[batch, :, k * span:(k + 1) * span]
                    if wide:
                        back = jnp.concatenate(halves(projected), axis=0)
                    else:
                        back = projected.astype(jnp.bfloat16)
                    term = dot32(back, rows_refs[k][batch])
                    total = term if total is None else total + term
                if wide:
                    total = total[:users] + total[users:]
                gram_part = dot32(both, gram_high[...])
                image = (
                    gram_part[:users] + gram_part[users:] + dot32(high, gram_low[...])
                    + total + ridge_term * direction
                )
                norm_now = n_s[batch]
                step_size = norm_now / jnp.sum(direction * image, axis=1, keepdims=True)
                x_s[batch] = x_s[batch] + step_size * direction
                residual = r_s[batch] - step_size * image
                r_s[batch] = residual
                norm_next = jnp.sum(residual * residual, axis=1, keepdims=True)
                p_s[batch] = residual + norm_next / norm_now * direction
                n_s[batch] = norm_next
            return carry

        return body

    lax.fori_loop(0, WIDE_ITERS, step(True), 0)
    lax.fori_loop(WIDE_ITERS, ITERS, step(False), 0)
    for batch in range(batch_count):
        for user in range(users):
            send_ref[pl.ds(place_ref[batch * users + user], 1), :] = x_s[batch, user:user + 1, :]


def place_kernel(slot_ref, got_ref, out_ref):
    for row in range(got_ref.shape[0]):
        out_ref[pl.ds(slot_ref[row], 1), :] = got_ref[row:row + 1, :]


def smem():
    return pl.BlockSpec(memory_space=pltpu.SMEM)


def vmem():
    return pl.BlockSpec(memory_space=pltpu.VMEM)


PARAMS = pltpu.CompilerParams(vmem_limit_bytes=VMEM_BYTES)


def on_device(item_factors, ratings, block_ids, live_counts, owner_rows):
    item_local, width = item_factors.shape
    users_here, columns = ratings.shape
    batch_count, slot_count = block_ids.shape
    batch_rows = users_here // batch_count
    block_size = columns // slot_count
    panel_count = lax.axis_size("blk")
    rep_count = lax.axis_size("rep")
    device_count = rep_count * panel_count
    quota = users_here // device_count
    chips = panel_count // 2
    per_panel = slot_count // panel_count
    blocks = item_local // block_size
    part_rows = block_size // rep_count
    rep = lax.axis_index("rep")
    blk = lax.axis_index("blk")

    def over_blk(array, target):
        return lax.ppermute(array, "blk", [(b, target(b)) for b in range(panel_count)])

    def over_rep(array, part):
        return lax.ppermute(array, "rep", [(r, r ^ part) for r in range(rep_count)])

    def other_core(array):
        return over_blk(array, lambda b: b ^ 1)

    whole = item_factors.reshape(blocks, block_size, width)
    piece = lax.dynamic_slice(whole, (0, rep * part_rows, 0), (blocks, part_rows, width))

    owners = lax.all_gather(owner_rows, ("rep", "blk"), axis=0, tiled=False)
    me = rep * panel_count + blk
    before = (jnp.arange(users_here)[:, None] < jnp.arange(users_here)[None, :]).astype(jnp.bfloat16)
    mine = (owners // users_here) == me
    mine_rank = dot32(mine.astype(jnp.bfloat16), before).astype(jnp.int32)
    chosen = mine[:, None, :] & (mine_rank[:, None, :] == jnp.arange(quota)[None, :, None])
    slots = jnp.sum(jnp.where(chosen, (owners % users_here)[:, None, :], 0), axis=2).reshape(-1)
    target_dev = owner_rows // users_here
    goes = target_dev[None, :] == jnp.arange(device_count)[:, None]
    goes_rank = dot32(goes.astype(jnp.bfloat16), before).astype(jnp.int32)
    place = target_dev * quota + jnp.sum(jnp.where(goes, goes_rank, 0), axis=0)

    gram = None
    rows_list, cols_list = [], []
    for k in range(chips):
        if k == 0:
            own = [(0, 0, whole)]
        else:
            piece = over_blk(piece, lambda b: (b + 2) % panel_count)
            own = [(0, 0, piece)]
            if rep_count == 4:
                near = over_rep(piece, 1)
                next_ = over_rep(piece, 2)
                half = blocks // 2
                own += [(1, 0, near), (2, 0, next_)]
                own += [(3, 0, over_rep(next_[:half], 1)), (3, half, over_rep(near[half:], 2))]
            else:
                own += [(part, 0, over_rep(piece, part)) for part in range(1, rep_count)]
        layout = tuple((0, part, start) for part, start, _ in own)
        layout += tuple((1, part, start) for part, start, _ in own)
        arrays = [array for _, _, array in own]
        arrays += [other_core(array) for array in arrays]
        where = jnp.stack([blk % 2, rep, (blk // 2 - k) % chips]).astype(jnp.int32)
        span = 2 * per_panel * block_size
        operands = [where, block_ids] + arrays + ([] if gram is None else [gram])
        gram, rows, cols = pl.pallas_call(
            functools.partial(stage_kernel, layout, block_size, batch_count, per_panel, gram is None),
            out_shape=(
                jax.ShapeDtypeStruct((width, width), jnp.float32),
                jax.ShapeDtypeStruct((batch_count, span, width), jnp.bfloat16),
                jax.ShapeDtypeStruct((batch_count, width, span), jnp.bfloat16),
            ),
            in_specs=[smem(), smem()] + [vmem()] * (len(operands) - 2),
            out_specs=(vmem(), vmem(), vmem()),
            compiler_params=PARAMS,
            cost_estimate=pl.CostEstimate(
                flops=4 * item_local * width * width, bytes_accessed=8 * item_local * width, transcendentals=0
            ),
            name="stage",
        )(*operands)
        rows_list.append(rows)
        cols_list.append(cols)

    where = jnp.stack([blk % 2, rep, blk // 2]).astype(jnp.int32)
    state = pltpu.VMEM((batch_count, batch_rows, width), jnp.float32)
    send_rows = pl.pallas_call(
        functools.partial(solve_kernel, chips, block_size, batch_count),
        out_shape=jax.ShapeDtypeStruct((users_here, width), jnp.float32),
        in_specs=[smem(), smem(), smem()] + [vmem()] * (2 + 2 * chips),
        out_specs=vmem(),
        scratch_shapes=[
            pltpu.VMEM((batch_count, batch_rows, columns), jnp.float32),
            pltpu.VMEM((width, width), jnp.bfloat16),
            pltpu.VMEM((width, width), jnp.bfloat16),
            state, state, state,
            pltpu.VMEM((batch_count, batch_rows, 1), jnp.float32),
        ],
        compiler_params=PARAMS,
        cost_estimate=pl.CostEstimate(
            flops=12 * 4 * users_here * columns * width, bytes_accessed=8 * columns * width, transcendentals=0
        ),
        name="solve",
    )(where, live_counts, place, ratings, gram, *rows_list, *cols_list)

    got_rows = lax.all_to_all(
        send_rows.reshape(device_count, quota, width), ("rep", "blk"), split_axis=0, concat_axis=0, tiled=True
    )
    return pl.pallas_call(
        place_kernel,
        out_shape=jax.ShapeDtypeStruct((users_here, width), jnp.float32),
        in_specs=[smem(), vmem()],
        out_specs=vmem(),
        compiler_params=PARAMS,
        name="place",
    )(slots, got_rows.reshape(users_here, width))


def solution(mesh):
    placed = (
        P("blk", None),
        P(("rep", "blk"), None),
        P(("rep", "blk"), None),
        P(("rep", "blk")),
        P(("rep", "blk")),
    )
    return jax.shard_map(
        on_device, mesh=mesh, in_specs=placed, out_specs=P(("rep", "blk"), None), check_vma=False
    )
```

```python
import functools
import jax
import jax.numpy as jnp
from jax import lax
from jax.experimental import pallas as pl
from jax.experimental.pallas import tpu as pltpu
from jax.sharding import PartitionSpec as P

ITERS = 8
WIDE_ITERS = 2

conf_scale = 6.0
ridge_term = 0.5


def dot32(left, right, dims=((1,), (0,))):
    return lax.dot_general(left, right, (dims, ((), ())), preferred_element_type=jnp.float32)


def halves(value):
    high = value.astype(jnp.bfloat16)
    low = (value - high.astype(jnp.float32)).astype(jnp.bfloat16)
    return high, low


def local_slots(core, per_panel):
    for side in range(2):
        parity = core if side == 0 else 1 - core
        for pick in range(per_panel):
            yield side, parity * per_panel + pick


def select_kernel(batch_count, per_panel, quota, where_ref, note_ref, own_ref, other_ref, *out_refs):
    core, rep, chip, blk, panels = (where_ref[i] for i in range(5))
    slots = 2 * per_panel
    slot_count = panels * per_panel
    blocks = own_ref.shape[0]
    for part, out_ref in enumerate(out_refs):
        row = (rep ^ part) * panels + blk
        for batch in range(batch_count):
            for side, local in local_slots(core, per_panel):
                block = note_ref[row, quota + batch * slot_count + chip * slots + local]
                held = other_ref if side else own_ref
                out_ref[batch * slots + local] = held[lax.rem(block, blocks)]


def join_kernel(batch_count, per_panel, *refs):
    where_ref, *part_refs, rows_ref, cols_ref = refs
    rep = where_ref[1]
    size = part_refs[0].shape[1]
    block_size = size * len(part_refs)
    slots = 2 * per_panel
    for batch in range(batch_count):
        for part, ref in enumerate(part_refs):
            for local in range(slots):
                offset = pl.multiple_of(local * block_size + (rep ^ part) * size, size)
                rows_ref[batch, pl.ds(offset, size), :] = ref[batch * slots + local]
        cols_ref[batch] = rows_ref[batch].T


def pick_kernel(batch_count, per_panel, where_ref, ids_ref, own_ref, other_ref, rows_ref, cols_ref):
    core, chip = where_ref[0], where_ref[2]
    slots = 2 * per_panel
    blocks, block_size, _ = own_ref.shape
    for batch in range(batch_count):
        for side, local in local_slots(core, per_panel):
            block = ids_ref[batch, chip * slots + local]
            held = other_ref if side else own_ref
            offset = pl.multiple_of(local * block_size, block_size)
            rows_ref[batch, pl.ds(offset, block_size), :] = held[lax.rem(block, blocks)]
        cols_ref[batch] = rows_ref[batch].T


def solve_kernel(chips, reps, block_size, batch_count, *refs):
    where_ref, live_ref, place_ref, ratings_ref = refs[:4]
    gram_refs, refs = refs[4:4 + reps], refs[4 + reps:]
    rows_refs, cols_refs, refs = refs[:chips], refs[chips:2 * chips], refs[2 * chips:]
    send_ref, weight, gram_high, gram_low, x_s, r_s, p_s, n_s = refs
    rep, chip = where_ref[1], where_ref[2]
    users = ratings_ref.shape[0] // batch_count
    span = ratings_ref.shape[1] // chips
    batches = range(batch_count)
    for part, ref in enumerate(gram_refs):
        size = ref.shape[0]
        offset = pl.multiple_of((rep ^ part) * size, size)
        high, low = halves(ref[...])
        gram_high[pl.ds(offset, size), :] = high
        gram_low[pl.ds(offset, size), :] = low

    totals = [None] * batch_count
    for k in range(chips):
        source = lax.rem(chip - k + chips, chips)
        start = pl.multiple_of(source * span, span)
        column = start + lax.broadcasted_iota(jnp.int32, (users, span), 1)
        for batch in batches:
            rated = ratings_ref[batch * users:(batch + 1) * users, pl.ds(start, span)].astype(jnp.float32)
            is_live = (column < live_ref[batch] * block_size).astype(jnp.float32)
            scaled = conf_scale * rated * is_live
            weight[batch, :, k * span:(k + 1) * span] = scaled
            both = jnp.concatenate(halves(is_live + scaled), axis=0)
            term = dot32(both, rows_refs[k][batch])
            totals[batch] = term if totals[batch] is None else totals[batch] + term
    for batch in batches:
        target_proj = totals[batch][:users] + totals[batch][users:]
        x_s[batch] = jnp.zeros_like(target_proj)
        r_s[batch] = target_proj
        p_s[batch] = target_proj
        n_s[batch] = jnp.sum(target_proj * target_proj, axis=1, keepdims=True)

    def step(wide):
        def body(_, carry):
            highs, boths, totals = [], [], [None] * batch_count
            for batch in batches:
                high, low = halves(p_s[batch])
                highs.append(high)
                boths.append(jnp.concatenate([high, low], axis=0))
            for k in range(chips):
                for batch in batches:
                    projected = dot32(boths[batch] if wide else highs[batch], cols_refs[k][batch])
                    if wide:
                        projected = projected[:users] + projected[users:]
                    projected = projected * weight[batch, :, k * span:(k + 1) * span]
                    if wide:
                        back = jnp.concatenate(halves(projected), axis=0)
                    else:
                        back = projected.astype(jnp.bfloat16)
                    term = dot32(back, rows_refs[k][batch])
                    totals[batch] = term if totals[batch] is None else totals[batch] + term
            for batch in batches:
                total = totals[batch]
                if wide:
                    total = total[:users] + total[users:]
                direction = p_s[batch]
                gram_part = dot32(boths[batch], gram_high[...])
                image = (
                    gram_part[:users] + gram_part[users:] + dot32(highs[batch], gram_low[...])
                    + total + ridge_term * direction
                )
                norm_now = n_s[batch]
                step_size = norm_now / jnp.sum(direction * image, axis=1, keepdims=True)
                x_s[batch] = x_s[batch] + step_size * direction
                residual = r_s[batch] - step_size * image
                r_s[batch] = residual
                norm_next = jnp.sum(residual * residual, axis=1, keepdims=True)
                p_s[batch] = residual + norm_next / norm_now * direction
                n_s[batch] = norm_next
            return carry

        return body

    lax.fori_loop(0, WIDE_ITERS, step(True), 0)
    lax.fori_loop(WIDE_ITERS, ITERS, step(False), 0)
    for batch in batches:
        for user in range(users):
            send_ref[pl.ds(place_ref[batch * users + user], 1), :] = x_s[batch, user:user + 1, :]


def place_kernel(note_ref, got_ref, out_ref):
    for source in range(got_ref.shape[0]):
        for row in range(got_ref.shape[1]):
            out_ref[pl.ds(note_ref[source, row], 1), :] = got_ref[source, row:row + 1, :]


def smem():
    return pl.BlockSpec(memory_space=pltpu.SMEM)


def vmem():
    return pl.BlockSpec(memory_space=pltpu.VMEM)


def call(body, name, small, large, out_shape, mebibytes, flops, scratch=()):
    operands = (*small, *large)
    moved = sum(array.size * array.dtype.itemsize for array in operands)
    return pl.pallas_call(
        body,
        out_shape=out_shape,
        in_specs=[smem()] * len(small) + [vmem()] * len(large),
        out_specs=jax.tree.map(lambda _: vmem(), out_shape),
        scratch_shapes=list(scratch),
        compiler_params=pltpu.CompilerParams(vmem_limit_bytes=mebibytes * 1024 * 1024),
        cost_estimate=pl.CostEstimate(flops=flops, bytes_accessed=moved, transcendentals=0),
        name=name,
    )(*operands)


def on_device(item_factors, ratings, block_ids, live_counts, owner_rows):
    item_local, width = item_factors.shape
    users_here, columns = ratings.shape
    batch_count, slot_count = block_ids.shape
    batch_rows = users_here // batch_count
    block_size = columns // slot_count
    panel_count = lax.axis_size("blk")
    rep_count = lax.axis_size("rep")
    device_count = rep_count * panel_count
    quota = users_here // device_count
    chips = panel_count // 2
    per_panel = slot_count // panel_count
    blocks = item_local // block_size
    part_rows = block_size // rep_count
    span = 2 * per_panel * block_size
    rep = lax.axis_index("rep")
    blk = lax.axis_index("blk")

    def over_blk(array, target):
        return lax.ppermute(array, "blk", [(b, target(b)) for b in range(panel_count)])

    def over_rep(array, part):
        return lax.ppermute(array, "rep", [(r, r ^ part) for r in range(rep_count)])

    def other_core(array):
        return over_blk(array, lambda b: b ^ 1)

    whole = item_factors.reshape(blocks, block_size, width)
    piece = lax.dynamic_slice(whole, (0, rep * part_rows, 0), (blocks, part_rows, width))

    before = (jnp.arange(users_here)[:, None] < jnp.arange(users_here)[None, :]).astype(jnp.bfloat16)
    target_dev = owner_rows // users_here
    goes = target_dev[None, :] == jnp.arange(device_count)[:, None]
    goes_rank = dot32(goes.astype(jnp.bfloat16), before).astype(jnp.int32)
    place = target_dev * quota + jnp.sum(jnp.where(goes, goes_rank, 0), axis=0)
    chosen = goes[:, None, :] & (goes_rank[:, None, :] == jnp.arange(quota)[None, :, None])
    slots = jnp.sum(jnp.where(chosen, (owner_rows % users_here)[None, None, :], 0), axis=2)
    ids_row = jnp.broadcast_to(block_ids.reshape(1, -1), (device_count, block_ids.size))
    note = lax.all_to_all(
        jnp.concatenate([slots, ids_row], axis=1), ("rep", "blk"), split_axis=0, concat_axis=0, tiled=True
    )

    local_gram = dot32(item_factors, item_factors, ((0,), (0,)))
    gram_rows = width // rep_count
    gram = lax.dynamic_slice(local_gram, (rep * gram_rows, 0), (gram_rows, width))
    bit = 1
    while bit < panel_count:
        gram = gram + over_blk(gram, lambda b: b ^ bit)
        bit *= 2
    grams = [gram] + [over_rep(gram, part) for part in range(1, rep_count)]

    rows_list, cols_list = [], []
    joined = (
        jax.ShapeDtypeStruct((batch_count, span, width), jnp.bfloat16),
        jax.ShapeDtypeStruct((batch_count, width, span), jnp.bfloat16),
    )
    picked = jax.ShapeDtypeStruct((batch_count * 2 * per_panel, part_rows, width), jnp.bfloat16)
    for k in range(chips):
        where = jnp.stack([blk % 2, rep, (blk // 2 - k) % chips, blk, panel_count]).astype(jnp.int32)
        if k == 0:
            home = where
            rows, cols = call(
                functools.partial(pick_kernel, batch_count, per_panel), "pick",
                [where, block_ids], [whole, other_core(whole)], joined, 16, 1 << 20,
            )
        else:
            piece = over_blk(piece, lambda b: (b + 2) % panel_count)
            chosen_parts = call(
                functools.partial(select_kernel, batch_count, per_panel, quota), "select",
                [where, note], [piece, other_core(piece)], (picked,) * rep_count, 8, 1 << 20,
            )
            parts = [chosen_parts[0]] + [over_rep(chosen_parts[part], part) for part in range(1, rep_count)]
            rows, cols = call(
                functools.partial(join_kernel, batch_count, per_panel), "join",
                [where], parts, joined, 8, 1 << 20,
            )
        rows_list.append(rows)
        cols_list.append(cols)

    state = pltpu.VMEM((batch_count, batch_rows, width), jnp.float32)
    half = pltpu.VMEM((width, width), jnp.bfloat16)
    send_rows = call(
        functools.partial(solve_kernel, chips, rep_count, block_size, batch_count), "solve",
        [home, live_counts, place], [ratings, *grams, *rows_list, *cols_list],
        jax.ShapeDtypeStruct((users_here, width), jnp.float32), 40,
        12 * 4 * users_here * columns * width,
        [
            pltpu.VMEM((batch_count, batch_rows, columns), jnp.float32), half, half,
            state, state, state, pltpu.VMEM((batch_count, batch_rows, 1), jnp.float32),
        ],
    )
    got_rows = lax.all_to_all(
        send_rows.reshape(device_count, quota, width), ("rep", "blk"), split_axis=0, concat_axis=0, tiled=True
    )
    return call(
        place_kernel, "place", [note], [got_rows],
        jax.ShapeDtypeStruct((users_here, width), jnp.float32), 8, 1 << 20,
    )


def solution(mesh):
    placed = (
        P("blk", None),
        P(("rep", "blk"), None),
        P(("rep", "blk"), None),
        P(("rep", "blk")),
        P(("rep", "blk")),
    )
    return jax.shard_map(
        on_device, mesh=mesh, in_specs=placed, out_specs=P(("rep", "blk"), None), check_vma=False
    )
```

```python
import functools
import jax
import jax.numpy as jnp
from jax import lax
from jax.experimental import pallas as pl
from jax.experimental.pallas import tpu as pltpu
from jax.sharding import PartitionSpec as P

ITERS = 8
WIDE_ITERS = 2

conf_scale = 6.0
ridge_term = 0.5


def dot32(left, right, dims=((1,), (0,))):
    return lax.dot_general(left, right, (dims, ((), ())), preferred_element_type=jnp.float32)


def halves(value):
    high = value.astype(jnp.bfloat16)
    low = (value - high.astype(jnp.float32)).astype(jnp.bfloat16)
    return high, low


def local_slots(core, per_panel):
    for side in range(2):
        parity = core if side == 0 else 1 - core
        for pick in range(per_panel):
            yield side, parity * per_panel + pick


def position(chips, back):
    blk = lax.axis_index("blk")
    return lax.rem(blk, 2), lax.axis_index("rep"), blk, lax.rem(lax.div(blk, 2) + chips - back, chips)


def select_kernel(chips, back, batch_count, per_panel, quota, note_ref, own_ref, other_ref, *out_refs):
    core, rep, blk, chip = position(chips, back)
    panels = 2 * chips
    slots = 2 * per_panel
    slot_count = panels * per_panel
    blocks = own_ref.shape[0]
    for part, out_ref in enumerate(out_refs):
        row = (rep ^ part) * panels + blk
        for batch in range(batch_count):
            for side, local in local_slots(core, per_panel):
                block = note_ref[row, quota + batch * slot_count + chip * slots + local]
                held = other_ref if side else own_ref
                out_ref[batch * slots + local] = held[lax.rem(block, blocks)]


def join_kernel(batch_count, per_panel, *refs):
    *part_refs, rows_ref, cols_ref = refs
    rep = lax.axis_index("rep")
    size = part_refs[0].shape[1]
    block_size = size * len(part_refs)
    slots = 2 * per_panel
    for batch in range(batch_count):
        for part, ref in enumerate(part_refs):
            for local in range(slots):
                offset = pl.multiple_of(local * block_size + (rep ^ part) * size, size)
                rows_ref[batch, pl.ds(offset, size), :] = ref[batch * slots + local]
        cols_ref[batch] = rows_ref[batch].T


def pick_kernel(chips, batch_count, per_panel, quota, note_ref, own_ref, other_ref, rows_ref, cols_ref):
    core, rep, blk, chip = position(chips, 0)
    row = rep * 2 * chips + blk
    slot_count = 2 * chips * per_panel
    slots = 2 * per_panel
    blocks, block_size, _ = own_ref.shape
    for batch in range(batch_count):
        for side, local in local_slots(core, per_panel):
            block = note_ref[row, quota + batch * slot_count + chip * slots + local]
            held = other_ref if side else own_ref
            offset = pl.multiple_of(local * block_size, block_size)
            rows_ref[batch, pl.ds(offset, block_size), :] = held[lax.rem(block, blocks)]
        cols_ref[batch] = rows_ref[batch].T


def solve_kernel(chips, reps, block_size, batch_count, *refs):
    note_ref, place_ref, ratings_ref = refs[:3]
    gram_refs, refs = refs[3:3 + reps], refs[3 + reps:]
    rows_refs, cols_refs, refs = refs[:chips], refs[chips:2 * chips], refs[2 * chips:]
    send_ref, weight, gram_high, gram_low, x_s, r_s, p_s, n_s = refs
    _, rep, blk, chip = position(chips, 0)
    live_at = note_ref.shape[1] - batch_count
    users = ratings_ref.shape[0] // batch_count
    span = ratings_ref.shape[1] // chips
    batches = range(batch_count)
    for part, ref in enumerate(gram_refs):
        size = ref.shape[0]
        offset = pl.multiple_of((rep ^ part) * size, size)
        high, low = halves(ref[...])
        gram_high[pl.ds(offset, size), :] = high
        gram_low[pl.ds(offset, size), :] = low

    totals = [None] * batch_count
    for k in range(chips):
        source = lax.rem(chip - k + chips, chips)
        start = pl.multiple_of(source * span, span)
        column = start + lax.broadcasted_iota(jnp.int32, (users, span), 1)
        for batch in batches:
            rated = ratings_ref[batch * users:(batch + 1) * users, pl.ds(start, span)].astype(jnp.float32)
            is_live = (column < note_ref[rep * 2 * chips + blk, live_at + batch] * block_size).astype(jnp.float32)
            scaled = conf_scale * rated * is_live
            weight[batch, :, k * span:(k + 1) * span] = scaled
            both = jnp.concatenate(halves(is_live + scaled), axis=0)
            term = dot32(both, rows_refs[k][batch])
            totals[batch] = term if totals[batch] is None else totals[batch] + term
    for batch in batches:
        target_proj = totals[batch][:users] + totals[batch][users:]
        x_s[batch] = jnp.zeros_like(target_proj)
        r_s[batch] = target_proj
        p_s[batch] = target_proj
        n_s[batch] = jnp.sum(target_proj * target_proj, axis=1, keepdims=True)

    def step(wide):
        def body(_, carry):
            highs, boths, totals = [], [], [None] * batch_count
            for batch in batches:
                high, low = halves(p_s[batch])
                highs.append(high)
                boths.append(jnp.concatenate([high, low], axis=0))
            for k in range(chips):
                for batch in batches:
                    projected = dot32(boths[batch] if wide else highs[batch], cols_refs[k][batch])
                    if wide:
                        projected = projected[:users] + projected[users:]
                    projected = projected * weight[batch, :, k * span:(k + 1) * span]
                    if wide:
                        back = jnp.concatenate(halves(projected), axis=0)
                    else:
                        back = projected.astype(jnp.bfloat16)
                    term = dot32(back, rows_refs[k][batch])
                    totals[batch] = term if totals[batch] is None else totals[batch] + term
            for batch in batches:
                total = totals[batch]
                if wide:
                    total = total[:users] + total[users:]
                direction = p_s[batch]
                gram_part = dot32(boths[batch], gram_high[...])
                image = (
                    gram_part[:users] + gram_part[users:] + dot32(highs[batch], gram_low[...])
                    + total + ridge_term * direction
                )
                norm_now = n_s[batch]
                step_size = norm_now / jnp.sum(direction * image, axis=1, keepdims=True)
                x_s[batch] = x_s[batch] + step_size * direction
                residual = r_s[batch] - step_size * image
                r_s[batch] = residual
                norm_next = jnp.sum(residual * residual, axis=1, keepdims=True)
                p_s[batch] = residual + norm_next / norm_now * direction
                n_s[batch] = norm_next
            return carry

        return body

    lax.fori_loop(0, WIDE_ITERS, step(True), 0)
    lax.fori_loop(WIDE_ITERS, ITERS, step(False), 0)
    for batch in batches:
        for user in range(users):
            send_ref[pl.ds(place_ref[batch * users + user], 1), :] = x_s[batch, user:user + 1, :]


def place_kernel(note_ref, got_ref, out_ref):
    for source in range(got_ref.shape[0]):
        for row in range(got_ref.shape[1]):
            out_ref[pl.ds(note_ref[source, row], 1), :] = got_ref[source, row:row + 1, :]


def smem():
    return pl.BlockSpec(memory_space=pltpu.SMEM)


def vmem():
    return pl.BlockSpec(memory_space=pltpu.VMEM)


def call(body, name, small, large, out_shape, mebibytes, flops, scratch=()):
    operands = (*small, *large)
    moved = sum(array.size * array.dtype.itemsize for array in operands)
    return pl.pallas_call(
        body,
        out_shape=out_shape,
        in_specs=[smem()] * len(small) + [vmem()] * len(large),
        out_specs=jax.tree.map(lambda _: vmem(), out_shape),
        scratch_shapes=list(scratch),
        compiler_params=pltpu.CompilerParams(vmem_limit_bytes=mebibytes * 1024 * 1024),
        cost_estimate=pl.CostEstimate(flops=flops, bytes_accessed=moved, transcendentals=0),
        name=name,
    )(*operands)


def on_device(item_factors, ratings, block_ids, live_counts, owner_rows):
    item_local, width = item_factors.shape
    users_here, columns = ratings.shape
    batch_count, slot_count = block_ids.shape
    batch_rows = users_here // batch_count
    block_size = columns // slot_count
    panel_count = lax.axis_size("blk")
    rep_count = lax.axis_size("rep")
    device_count = rep_count * panel_count
    quota = users_here // device_count
    chips = panel_count // 2
    per_panel = slot_count // panel_count
    blocks = item_local // block_size
    part_rows = block_size // rep_count
    span = 2 * per_panel * block_size
    rep = lax.axis_index("rep")

    def over_blk(array, target):
        return lax.ppermute(array, "blk", [(b, target(b)) for b in range(panel_count)])

    def over_rep(array, part):
        return lax.ppermute(array, "rep", [(r, r ^ part) for r in range(rep_count)])

    def other_core(array):
        return over_blk(array, lambda b: b ^ 1)

    whole = item_factors.reshape(blocks, block_size, width)
    piece = lax.dynamic_slice(whole, (0, rep * part_rows, 0), (blocks, part_rows, width))

    before = (jnp.arange(users_here)[:, None] < jnp.arange(users_here)[None, :]).astype(jnp.bfloat16)
    target_dev = owner_rows // users_here
    goes = target_dev[None, :] == jnp.arange(device_count)[:, None]
    goes_rank = dot32(goes.astype(jnp.bfloat16), before).astype(jnp.int32)
    place = target_dev * quota + jnp.sum(jnp.where(goes, goes_rank, 0), axis=0)
    chosen = goes[:, None, :] & (goes_rank[:, None, :] == jnp.arange(quota)[None, :, None])
    slots = jnp.sum(jnp.where(chosen, (owner_rows % users_here)[None, None, :], 0), axis=2)
    known = jnp.concatenate([block_ids.reshape(-1), live_counts])
    known = jnp.broadcast_to(known[None, :], (device_count, known.size))
    note = lax.all_to_all(
        jnp.concatenate([slots, known], axis=1), ("rep", "blk"), split_axis=0, concat_axis=0, tiled=True
    )

    other_whole = other_core(whole)
    after = lax.optimization_barrier
    pieces = [over_blk(piece, lambda b: (b + 2) % panel_count)]
    pieces[0], note = after((pieces[0], note))
    for _ in range(2, chips):
        pieces.append(over_blk(pieces[-1], lambda b: (b + 2) % panel_count))

    gram_rows = width // rep_count
    gram = sum(
        dot32(lax.dynamic_slice(panel.reshape(-1, width), (0, rep * gram_rows), (item_local, gram_rows)),
              panel.reshape(-1, width), ((0,), (0,)))
        for panel in (whole, other_whole)
    )
    bit = 2
    while bit < panel_count:
        gram = gram + over_blk(gram, lambda b: b ^ bit)
        bit *= 2
    grams = [gram] + [over_rep(gram, part) for part in range(1, rep_count)]

    joined = (
        jax.ShapeDtypeStruct((batch_count, span, width), jnp.bfloat16),
        jax.ShapeDtypeStruct((batch_count, width, span), jnp.bfloat16),
    )
    picked = jax.ShapeDtypeStruct((batch_count * 2 * per_panel, part_rows, width), jnp.bfloat16)
    tables = [call(
        functools.partial(pick_kernel, chips, batch_count, per_panel, quota), "pick",
        [note], [whole, other_whole], joined, 16, 1 << 20,
    )]
    chosen = None
    for k in range(1, chips):
        piece = pieces[k - 1]
        if k == 2:
            piece, chosen, tables[0] = after((piece, chosen, tables[0]))
        elif k > 2:
            piece, chosen, tables[k - 2] = after((piece, chosen, tables[k - 2]))
        if k == chips - 1:
            piece, grams = after((piece, grams))
        if k > 1:
            parts = [chosen[0]] + [over_rep(chosen[part], part) for part in range(1, rep_count)]
            tables.append(call(
                functools.partial(join_kernel, batch_count, per_panel), "join", [], parts, joined, 8, 1 << 20,
            ))
        chosen = call(
            functools.partial(select_kernel, chips, k, batch_count, per_panel, quota), "select",
            [note], [piece, other_core(piece)], (picked,) * rep_count, 8, 1 << 20,
        )
    parts = [chosen[0]] + [over_rep(chosen[part], part) for part in range(1, rep_count)]
    tables.append(call(
        functools.partial(join_kernel, batch_count, per_panel), "join", [], parts, joined, 8, 1 << 20,
    ))
    rows_list, cols_list = [rows for rows, _ in tables], [cols for _, cols in tables]

    state = pltpu.VMEM((batch_count, batch_rows, width), jnp.float32)
    half = pltpu.VMEM((width, width), jnp.bfloat16)
    send_rows = call(
        functools.partial(solve_kernel, chips, rep_count, block_size, batch_count), "solve",
        [note, place], [ratings, *grams, *rows_list, *cols_list],
        jax.ShapeDtypeStruct((users_here, width), jnp.float32), 40,
        12 * 4 * users_here * columns * width,
        [
            pltpu.VMEM((batch_count, batch_rows, columns), jnp.float32), half, half,
            state, state, state, pltpu.VMEM((batch_count, batch_rows, 1), jnp.float32),
        ],
    )
    got_rows = lax.all_to_all(
        send_rows.reshape(device_count, quota, width), ("rep", "blk"), split_axis=0, concat_axis=0, tiled=True
    )
    return call(
        place_kernel, "place", [note], [got_rows],
        jax.ShapeDtypeStruct((users_here, width), jnp.float32), 8, 1 << 20,
    )


def solution(mesh):
    placed = (
        P("blk", None),
        P(("rep", "blk"), None),
        P(("rep", "blk"), None),
        P(("rep", "blk")),
        P(("rep", "blk")),
    )
    return jax.shard_map(
        on_device, mesh=mesh, in_specs=placed, out_specs=P(("rep", "blk"), None), check_vma=False
    )
```

```python
import functools
import jax
import jax.numpy as jnp
from jax import lax
from jax.experimental import pallas as pl
from jax.experimental.pallas import tpu as pltpu
from jax.sharding import PartitionSpec as P

ITERS = 8
WIDE_ITERS = 2

conf_scale = 6.0
ridge_term = 0.5


def dot32(left, right, dims=((1,), (0,))):
    return lax.dot_general(left, right, (dims, ((), ())), preferred_element_type=jnp.float32)


def halves(value):
    high = value.astype(jnp.bfloat16)
    low = (value - high.astype(jnp.float32)).astype(jnp.bfloat16)
    return high, low


def local_slots(core, per_panel):
    for side in range(2):
        parity = core if side == 0 else 1 - core
        for pick in range(per_panel):
            yield side, parity * per_panel + pick


def position(chips, back):
    blk = lax.axis_index("blk")
    return lax.rem(blk, 2), lax.rem(lax.div(blk, 2) + chips - back, chips)


def select_kernel(chips, back, reps, batch_count, per_panel, *refs):
    ids_refs, (own_ref, other_ref), refs = refs[:reps], refs[reps:reps + 2], refs[reps + 2:]
    gram_refs, out_refs = refs[:-reps], refs[-reps:]
    named, size = batch_count * 2 * per_panel, own_ref.shape[1]
    for gram_ref in gram_refs:
        gram = jnp.concatenate(halves(gram_ref[...]), axis=0)
        for out_ref in out_refs:
            out_ref[named:] = gram.reshape(-1, size, gram.shape[1])
    core, chip = position(chips, back)
    slots = 2 * per_panel
    blocks = own_ref.shape[0]
    for ids_ref, out_ref in zip(ids_refs, out_refs):
        for batch in range(batch_count):
            for side, local in local_slots(core, per_panel):
                block = ids_ref[batch, chip * slots + local]
                held = other_ref if side else own_ref
                out_ref[batch * slots + local] = held[lax.rem(block, blocks)]


def join_kernel(reps, batch_count, per_panel, *refs):
    part_refs, rows_ref, cols_ref, *gram_refs = refs[:reps], *refs[reps:]
    rep = lax.axis_index("rep")
    size = part_refs[0].shape[1]
    block_size = size * len(part_refs)
    slots = 2 * per_panel
    for batch in range(batch_count):
        for part, ref in enumerate(part_refs):
            for local in range(slots):
                offset = pl.multiple_of(local * block_size + (rep ^ part) * size, size)
                rows_ref[batch, pl.ds(offset, size), :] = ref[batch * slots + local]
        cols_ref[batch] = rows_ref[batch].T
    for part, ref in enumerate(part_refs):
        count = (ref.shape[0] - batch_count * slots) // 2
        for i, gram_ref in enumerate(gram_refs):
            start = batch_count * slots + i * count
            offset = pl.multiple_of((rep ^ part) * size * count, size * count)
            half = ref[start:start + count].reshape(size * count, ref.shape[2])
            gram_ref[pl.ds(offset, size * count), :] = half


def pick_kernel(chips, batch_count, per_panel, ids_ref, own_ref, other_ref, rows_ref, cols_ref):
    core, chip = position(chips, 0)
    slots = 2 * per_panel
    blocks, block_size, _ = own_ref.shape
    for batch in range(batch_count):
        for side, local in local_slots(core, per_panel):
            block = ids_ref[batch, chip * slots + local]
            held = other_ref if side else own_ref
            offset = pl.multiple_of(local * block_size, block_size)
            rows_ref[batch, pl.ds(offset, block_size), :] = held[lax.rem(block, blocks)]
        cols_ref[batch] = rows_ref[batch].T


def solve_kernel(chips, block_size, batch_count, *refs):
    live_ref, place_ref, ratings_ref, gram_high, gram_low = refs[:5]
    refs = refs[5:]
    rows_refs, cols_refs, refs = refs[:chips], refs[chips:2 * chips], refs[2 * chips:]
    send_ref, weight, x_s, r_s, p_s, n_s = refs
    _, chip = position(chips, 0)
    users = ratings_ref.shape[0] // batch_count
    span = ratings_ref.shape[1] // chips
    batches = range(batch_count)
    totals = [None] * batch_count
    for k in range(chips):
        source = lax.rem(chip - k + chips, chips)
        start = pl.multiple_of(source * span, span)
        column = start + lax.broadcasted_iota(jnp.int32, (users, span), 1)
        for batch in batches:
            rated = ratings_ref[batch * users:(batch + 1) * users, pl.ds(start, span)].astype(jnp.float32)
            is_live = (column < live_ref[batch] * block_size).astype(jnp.float32)
            scaled = conf_scale * rated * is_live
            weight[batch, :, k * span:(k + 1) * span] = scaled
            both = jnp.concatenate(halves(is_live + scaled), axis=0)
            term = dot32(both, rows_refs[k][batch])
            totals[batch] = term if totals[batch] is None else totals[batch] + term
    for batch in batches:
        target_proj = totals[batch][:users] + totals[batch][users:]
        x_s[batch] = jnp.zeros_like(target_proj)
        r_s[batch] = target_proj
        p_s[batch] = target_proj
        n_s[batch] = jnp.sum(target_proj * target_proj, axis=1, keepdims=True)

    def step(wide):
        def body(_, carry):
            highs, boths, totals = [], [], [None] * batch_count
            for batch in batches:
                high, low = halves(p_s[batch])
                highs.append(high)
                boths.append(jnp.concatenate([high, low], axis=0))
            for k in range(chips):
                for batch in batches:
                    projected = dot32(boths[batch] if wide else highs[batch], cols_refs[k][batch])
                    if wide:
                        projected = projected[:users] + projected[users:]
                    projected = projected * weight[batch, :, k * span:(k + 1) * span]
                    if wide:
                        back = jnp.concatenate(halves(projected), axis=0)
                    else:
                        back = projected.astype(jnp.bfloat16)
                    term = dot32(back, rows_refs[k][batch])
                    totals[batch] = term if totals[batch] is None else totals[batch] + term
            for batch in batches:
                total = totals[batch]
                if wide:
                    total = total[:users] + total[users:]
                direction = p_s[batch]
                gram_part = dot32(boths[batch], gram_high[...])
                image = (
                    gram_part[:users] + gram_part[users:] + dot32(highs[batch], gram_low[...])
                    + total + ridge_term * direction
                )
                norm_now = n_s[batch]
                step_size = norm_now / jnp.sum(direction * image, axis=1, keepdims=True)
                x_s[batch] = x_s[batch] + step_size * direction
                residual = r_s[batch] - step_size * image
                r_s[batch] = residual
                norm_next = jnp.sum(residual * residual, axis=1, keepdims=True)
                p_s[batch] = residual + norm_next / norm_now * direction
                n_s[batch] = norm_next
            return carry

        return body

    lax.fori_loop(0, WIDE_ITERS, step(True), 0)
    lax.fori_loop(WIDE_ITERS, ITERS, step(False), 0)
    for batch in batches:
        for user in range(users):
            send_ref[pl.ds(place_ref[batch * users + user], 1), :] = x_s[batch, user:user + 1, :]


def place_kernel(slot_ref, got_ref, out_ref):
    for source in range(got_ref.shape[0]):
        for row in range(got_ref.shape[1]):
            out_ref[pl.ds(slot_ref[source, row], 1), :] = got_ref[source, row:row + 1, :]


def smem():
    return pl.BlockSpec(memory_space=pltpu.SMEM)


def vmem():
    return pl.BlockSpec(memory_space=pltpu.VMEM)


def call(body, name, small, large, out_shape, mebibytes, flops, scratch=()):
    operands = (*small, *large)
    moved = sum(array.size * array.dtype.itemsize for array in operands)
    return pl.pallas_call(
        body,
        out_shape=out_shape,
        in_specs=[smem()] * len(small) + [vmem()] * len(large),
        out_specs=jax.tree.map(lambda _: vmem(), out_shape),
        scratch_shapes=list(scratch),
        compiler_params=pltpu.CompilerParams(vmem_limit_bytes=mebibytes * 1024 * 1024),
        cost_estimate=pl.CostEstimate(flops=flops, bytes_accessed=moved, transcendentals=0),
        name=name,
    )(*operands)


def on_device(item_factors, ratings, block_ids, live_counts, owner_rows):
    item_local, width = item_factors.shape
    users_here, columns = ratings.shape
    batch_count, slot_count = block_ids.shape
    batch_rows = users_here // batch_count
    block_size = columns // slot_count
    panel_count = lax.axis_size("blk")
    rep_count = lax.axis_size("rep")
    device_count = rep_count * panel_count
    quota = users_here // device_count
    chips = panel_count // 2
    per_panel = slot_count // panel_count
    blocks = item_local // block_size
    part_rows = block_size // rep_count
    span = 2 * per_panel * block_size
    rep = lax.axis_index("rep")

    def over_blk(array, target):
        return lax.ppermute(array, "blk", [(b, target(b)) for b in range(panel_count)])

    def over_rep(array, part):
        return lax.ppermute(array, "rep", [(r, r ^ part) for r in range(rep_count)])

    def other_core(array):
        return over_blk(array, lambda b: b ^ 1)

    whole = item_factors.reshape(blocks, block_size, width)
    piece = lax.dynamic_slice(whole, (0, rep * part_rows, 0), (blocks, part_rows, width))

    after = lax.optimization_barrier
    other_whole = other_core(whole)
    pieces = [over_blk(piece, lambda b: (b + 2) % panel_count)]
    ids = [block_ids] + [over_rep(block_ids, part) for part in range(1, rep_count)]

    before = (jnp.arange(users_here)[:, None] < jnp.arange(users_here)[None, :]).astype(jnp.bfloat16)
    target_dev = owner_rows // users_here
    goes = target_dev[None, :] == jnp.arange(device_count)[:, None]
    goes_rank = dot32(goes.astype(jnp.bfloat16), before).astype(jnp.int32)
    place = target_dev * quota + jnp.sum(jnp.where(goes, goes_rank, 0), axis=0)
    sent = goes[:, None, :] & (goes_rank[:, None, :] == jnp.arange(quota)[None, :, None])
    slots = jnp.sum(jnp.where(sent, (owner_rows % users_here)[None, None, :], 0), axis=2)

    gram_rows = width // rep_count
    gram = sum(
        dot32(lax.dynamic_slice(panel.reshape(-1, width), (0, rep * gram_rows), (item_local, gram_rows)),
              panel.reshape(-1, width), ((0,), (0,)))
        for panel in (whole, other_whole)
    )
    bit = 2

    tables = [call(
        functools.partial(pick_kernel, chips, batch_count, per_panel), "pick",
        [block_ids], [whole, other_whole],
        (
            jax.ShapeDtypeStruct((batch_count, span, width), jnp.bfloat16),
            jax.ShapeDtypeStruct((batch_count, width, span), jnp.bfloat16),
        ), 16, 1 << 20,
    )]
    named = batch_count * 2 * per_panel
    gram_step = max(1, chips - 2)
    gram_blocks = 2 * gram_rows // part_rows

    def join(parts, with_gram):
        shapes = (
            jax.ShapeDtypeStruct((batch_count, span, width), jnp.bfloat16),
            jax.ShapeDtypeStruct((batch_count, width, span), jnp.bfloat16),
        ) + (jax.ShapeDtypeStruct((width, width), jnp.bfloat16),) * (2 * with_gram)
        return call(
            functools.partial(join_kernel, rep_count, batch_count, per_panel), "join", [], parts, shapes, 8, 1 << 20
        )

    parts = None
    for k in range(1, chips):
        piece = pieces[k - 1]
        if k < chips - 1:
            if bit < panel_count:
                gram = gram + over_blk(gram, lambda b: b ^ bit)
                bit *= 2
            moving, gram = after((piece, gram))
            if k > 1:
                moving, chosen = after((moving, chosen))
            pieces.append(over_blk(moving, lambda b: (b + 2) % panel_count))
        while k == gram_step and bit < panel_count:
            gram = gram + over_blk(gram, lambda b: b ^ bit)
            bit *= 2
        if k > 1:
            piece, chosen = after((piece, chosen))
            parts = [chosen[0]] + [over_rep(chosen[part], part) for part in range(1, rep_count)]
        if k == chips - 1:
            piece, tables[0] = after((piece, tables[0]))
        pair = [piece, other_core(piece)]
        if k > 1:
            pair, parts = after((pair, parts))
            tables.append(join(parts, k - 1 == gram_step))
        with_gram = k == gram_step
        picked = jax.ShapeDtypeStruct((named + with_gram * gram_blocks, part_rows, width), jnp.bfloat16)
        chosen = call(
            functools.partial(select_kernel, chips, k, rep_count, batch_count, per_panel), "select",
            ids, pair + [gram] * with_gram, (picked,) * rep_count, 8, 1 << 20,
        )
    slots, chosen = after((slots, chosen))
    slots = lax.all_to_all(slots, ("rep", "blk"), split_axis=0, concat_axis=0, tiled=True)
    parts = [chosen[0]] + [over_rep(chosen[part], part) for part in range(1, rep_count)]
    parts, slots = after((parts, slots))
    tables.append(join(parts, chips - 1 == gram_step))
    rows_list, cols_list = [table[0] for table in tables], [table[1] for table in tables]
    gram_high, gram_low = tables[gram_step][2:]

    state = pltpu.VMEM((batch_count, batch_rows, width), jnp.float32)
    send_rows = call(
        functools.partial(solve_kernel, chips, block_size, batch_count), "solve",
        [live_counts, place], [ratings, gram_high, gram_low, *rows_list, *cols_list],
        jax.ShapeDtypeStruct((users_here, width), jnp.float32), 40,
        12 * 4 * users_here * columns * width,
        [
            pltpu.VMEM((batch_count, batch_rows, columns), jnp.float32),
            state, state, state, pltpu.VMEM((batch_count, batch_rows, 1), jnp.float32),
        ],
    )
    got_rows = lax.all_to_all(
        send_rows.reshape(device_count, quota, width), ("rep", "blk"), split_axis=0, concat_axis=0, tiled=True
    )
    return call(
        place_kernel, "place", [slots], [got_rows],
        jax.ShapeDtypeStruct((users_here, width), jnp.float32), 8, 1 << 20,
    )


def solution(mesh):
    placed = (
        P("blk", None),
        P(("rep", "blk"), None),
        P(("rep", "blk"), None),
        P(("rep", "blk")),
        P(("rep", "blk")),
    )
    return jax.shard_map(
        on_device, mesh=mesh, in_specs=placed, out_specs=P(("rep", "blk"), None), check_vma=False
    )
```

```python
import functools
import math
import jax
import jax.numpy as jnp
from jax import lax
from jax.experimental import pallas as pl
from jax.experimental.pallas import tpu as pltpu
from jax.sharding import PartitionSpec as P

ITERS = 8
WIDE_ITERS = 2
SPARE_VMEM = 6 * 1024 * 1024

conf_scale = 6.0
ridge_term = 0.5


def dot32(left, right, dims=((1,), (0,))):
    return lax.dot_general(left, right, (dims, ((), ())), preferred_element_type=jnp.float32)


def halves(value):
    high = value.astype(jnp.bfloat16)
    low = (value - high.astype(jnp.float32)).astype(jnp.bfloat16)
    return high, low


def local_slots(core, per_panel):
    for side in range(2):
        parity = core if side == 0 else 1 - core
        for pick in range(per_panel):
            yield side, parity * per_panel + pick


def position(chips, back):
    blk = lax.axis_index("blk")
    return lax.rem(blk, 2), lax.rem(lax.div(blk, 2) + chips - back, chips)


def select_kernel(chips, back, reps, batch_count, per_panel, ids_ref, own_ref, other_ref, *refs):
    *gram_refs, out_ref = refs
    core, chip = position(chips, back)
    slots = 2 * per_panel
    blocks, size, _ = own_ref.shape
    count = out_ref.shape[0] // reps
    for rep in range(reps):
        for batch in range(batch_count):
            for side, local in local_slots(core, per_panel):
                block = ids_ref[rep * batch_count + batch, chip * slots + local]
                held = other_ref if side else own_ref
                out_ref[rep * count + batch * slots + local] = held[lax.rem(block, blocks)]
        for gram_ref in gram_refs:
            gram = jnp.concatenate(halves(gram_ref[...]), axis=0)
            start = rep * count + batch_count * slots
            out_ref[start:(rep + 1) * count] = gram.reshape(-1, size, gram.shape[1])


def join_kernel(reps, batch_count, per_panel, parts_ref, rows_ref, cols_ref, *gram_refs):
    count, size = parts_ref.shape[0] // reps, parts_ref.shape[1]
    slots = 2 * per_panel
    for batch in range(batch_count):
        for rep in range(reps):
            for local in range(slots):
                offset = (local * reps + rep) * size
                rows_ref[batch, offset:offset + size, :] = parts_ref[rep * count + batch * slots + local]
        cols_ref[batch] = rows_ref[batch].T
    for rep in range(reps):
        extra = count - batch_count * slots
        half = extra // 2
        for i, gram_ref in enumerate(gram_refs):
            start = rep * count + batch_count * slots + i * half
            rows = parts_ref[start:start + half].reshape(size * half, parts_ref.shape[2])
            gram_ref[rep * size * half:(rep + 1) * size * half, :] = rows


def pick_kernel(chips, batch_count, per_panel, ids_ref, own_ref, other_ref, rows_ref, cols_ref):
    core, chip = position(chips, 0)
    slots = 2 * per_panel
    blocks, block_size, _ = own_ref.shape
    for batch in range(batch_count):
        for side, local in local_slots(core, per_panel):
            block = ids_ref[batch, chip * slots + local]
            held = other_ref if side else own_ref
            offset = pl.multiple_of(local * block_size, block_size)
            rows_ref[batch, pl.ds(offset, block_size), :] = held[lax.rem(block, blocks)]
        cols_ref[batch] = rows_ref[batch].T


def solve_kernel(chips, block_size, batch_count, *refs):
    live_ref, place_ref, ratings_ref, gram_high, gram_low = refs[:5]
    refs = refs[5:]
    rows_refs, cols_refs, refs = refs[:chips], refs[chips:2 * chips], refs[2 * chips:]
    send_ref, weight, x_s, r_s, p_s, n_s = refs
    _, chip = position(chips, 0)
    users = ratings_ref.shape[0] // batch_count
    span = ratings_ref.shape[1] // chips
    batches = range(batch_count)
    totals = [None] * batch_count
    for k in range(chips):
        source = lax.rem(chip - k + chips, chips)
        start = pl.multiple_of(source * span, span)
        column = start + lax.broadcasted_iota(jnp.int32, (users, span), 1)
        for batch in batches:
            rated = ratings_ref[batch * users:(batch + 1) * users, pl.ds(start, span)].astype(jnp.float32)
            is_live = (column < live_ref[batch] * block_size).astype(jnp.float32)
            scaled = conf_scale * rated * is_live
            weight[batch, :, k * span:(k + 1) * span] = scaled
            both = jnp.concatenate(halves(is_live + scaled), axis=0)
            term = dot32(both, rows_refs[k][batch])
            totals[batch] = term if totals[batch] is None else totals[batch] + term
    for batch in batches:
        target_proj = totals[batch][:users] + totals[batch][users:]
        x_s[batch] = jnp.zeros_like(target_proj)
        r_s[batch] = target_proj
        p_s[batch] = target_proj
        n_s[batch] = jnp.sum(target_proj * target_proj, axis=1, keepdims=True)

    def step(wide):
        def body(_, carry):
            highs, boths, totals = [], [], [None] * batch_count
            for batch in batches:
                high, low = halves(p_s[batch])
                highs.append(high)
                boths.append(jnp.concatenate([high, low], axis=0))
            for k in range(chips):
                for batch in batches:
                    projected = dot32(boths[batch] if wide else highs[batch], cols_refs[k][batch])
                    if wide:
                        projected = projected[:users] + projected[users:]
                    projected = projected * weight[batch, :, k * span:(k + 1) * span]
                    if wide:
                        back = jnp.concatenate(halves(projected), axis=0)
                    else:
                        back = projected.astype(jnp.bfloat16)
                    term = dot32(back, rows_refs[k][batch])
                    totals[batch] = term if totals[batch] is None else totals[batch] + term
            for batch in batches:
                total = totals[batch]
                if wide:
                    total = total[:users] + total[users:]
                direction = p_s[batch]
                gram_part = dot32(boths[batch], gram_high[...])
                image = (
                    gram_part[:users] + gram_part[users:] + dot32(highs[batch], gram_low[...])
                    + total + ridge_term * direction
                )
                norm_now = n_s[batch]
                step_size = norm_now / jnp.sum(direction * image, axis=1, keepdims=True)
                x_s[batch] = x_s[batch] + step_size * direction
                residual = r_s[batch] - step_size * image
                r_s[batch] = residual
                norm_next = jnp.sum(residual * residual, axis=1, keepdims=True)
                p_s[batch] = residual + norm_next / norm_now * direction
                n_s[batch] = norm_next
            return carry

        return body

    lax.fori_loop(0, WIDE_ITERS, step(True), 0)
    lax.fori_loop(WIDE_ITERS, ITERS, step(False), 0)
    for batch in batches:
        for user in range(users):
            send_ref[pl.ds(place_ref[batch * users + user], 1), :] = x_s[batch, user:user + 1, :]


def place_kernel(slot_ref, got_ref, out_ref):
    for source in range(got_ref.shape[0]):
        for row in range(got_ref.shape[1]):
            out_ref[pl.ds(slot_ref[source, row], 1), :] = got_ref[source, row:row + 1, :]


def smem():
    return pl.BlockSpec(memory_space=pltpu.SMEM)


def vmem():
    return pl.BlockSpec(memory_space=pltpu.VMEM)


def call(body, name, small, large, out_shape, flops, scratch=()):
    operands = (*small, *large)
    moved = sum(array.size * array.dtype.itemsize for array in (*operands, *jax.tree.leaves(out_shape)))
    kept = sum(math.prod(array.shape) * 4 for array in scratch)
    return pl.pallas_call(
        body,
        out_shape=out_shape,
        in_specs=[smem()] * len(small) + [vmem()] * len(large),
        out_specs=jax.tree.map(lambda _: vmem(), out_shape),
        scratch_shapes=list(scratch),
        compiler_params=pltpu.CompilerParams(vmem_limit_bytes=moved + kept + SPARE_VMEM),
        cost_estimate=pl.CostEstimate(flops=flops, bytes_accessed=moved, transcendentals=0),
        name=name,
    )(*operands)


def on_device(item_factors, ratings, block_ids, live_counts, owner_rows):
    item_local, width = item_factors.shape
    users_here, columns = ratings.shape
    batch_count, slot_count = block_ids.shape
    batch_rows = users_here // batch_count
    block_size = columns // slot_count
    panel_count = lax.axis_size("blk")
    rep_count = lax.axis_size("rep")
    device_count = rep_count * panel_count
    quota = users_here // device_count
    chips = panel_count // 2
    per_panel = slot_count // panel_count
    blocks = item_local // block_size
    part_rows = block_size // rep_count
    span = 2 * per_panel * block_size
    rep = lax.axis_index("rep")

    def over_blk(array, target):
        return lax.ppermute(array, "blk", [(b, target(b)) for b in range(panel_count)])

    def in_plane(array):
        return lax.all_to_all(array, "rep", split_axis=0, concat_axis=0, tiled=True)

    def other_core(array):
        return over_blk(array, lambda b: b ^ 1)

    whole = item_factors.reshape(blocks, block_size, width)
    piece = lax.dynamic_slice(whole, (0, rep * part_rows, 0), (blocks, part_rows, width))

    after = lax.optimization_barrier
    other_whole = other_core(whole)
    pieces = [over_blk(piece, lambda b: (b + 2) % panel_count)]
    ids = in_plane(jnp.tile(block_ids, (rep_count, 1)))
    pieces[0], ids = after((pieces[0], ids))

    before = (jnp.arange(users_here)[:, None] < jnp.arange(users_here)[None, :]).astype(jnp.bfloat16)
    target_dev = owner_rows // users_here
    goes = target_dev[None, :] == jnp.arange(device_count)[:, None]
    goes_rank = dot32(goes.astype(jnp.bfloat16), before).astype(jnp.int32)
    place = target_dev * quota + jnp.sum(jnp.where(goes, goes_rank, 0), axis=0)
    sent = goes[:, None, :] & (goes_rank[:, None, :] == jnp.arange(quota)[None, :, None])
    slots = jnp.sum(jnp.where(sent, (owner_rows % users_here)[None, None, :], 0), axis=2)

    gram_rows = width // rep_count
    gram = sum(
        dot32(lax.dynamic_slice(panel.reshape(-1, width), (0, rep * gram_rows), (item_local, gram_rows)),
              panel.reshape(-1, width), ((0,), (0,)))
        for panel in (whole, other_whole)
    )
    bit = 2

    tables = [call(
        functools.partial(pick_kernel, chips, batch_count, per_panel), "pick",
        [block_ids], [whole, other_whole],
        (
            jax.ShapeDtypeStruct((batch_count, span, width), jnp.bfloat16),
            jax.ShapeDtypeStruct((batch_count, width, span), jnp.bfloat16),
        ), 1 << 20,
    )]
    named = batch_count * 2 * per_panel
    gram_step = max(1, chips - 2)
    gram_blocks = 2 * gram_rows // part_rows

    def join(parts, with_gram):
        shapes = (
            jax.ShapeDtypeStruct((batch_count, span, width), jnp.bfloat16),
            jax.ShapeDtypeStruct((batch_count, width, span), jnp.bfloat16),
        ) + (jax.ShapeDtypeStruct((width, width), jnp.bfloat16),) * (2 * with_gram)
        return call(
            functools.partial(join_kernel, rep_count, batch_count, per_panel), "join", [], [parts], shapes, 1 << 20
        )

    for k in range(1, chips):
        piece = pieces[k - 1]
        if k < chips - 1:
            if bit < panel_count:
                gram = gram + over_blk(gram, lambda b: b ^ bit)
                bit *= 2
            moving, gram = after((piece, gram))
            if k > 1:
                moving, chosen = after((moving, chosen))
            pieces.append(over_blk(moving, lambda b: (b + 2) % panel_count))
        while k == gram_step and bit < panel_count:
            gram = gram + over_blk(gram, lambda b: b ^ bit)
            bit *= 2
        if k == 1:
            slots, piece = after((slots, piece))
            slots = lax.all_to_all(slots, ("rep", "blk"), split_axis=0, concat_axis=0, tiled=True)
        if k > 1:
            piece, chosen, slots = after((piece, chosen, slots))
            parts = in_plane(chosen)
        if k == chips - 1:
            piece, tables[0] = after((piece, tables[0]))
        pair = [piece, other_core(piece)]
        if k > 1:
            pair, parts = after((pair, parts))
            tables.append(join(parts, k - 1 == gram_step))
        with_gram = k == gram_step
        chosen = call(
            functools.partial(select_kernel, chips, k, rep_count, batch_count, per_panel), "select",
            [ids], pair + [gram] * with_gram,
            jax.ShapeDtypeStruct((rep_count * (named + with_gram * gram_blocks), part_rows, width), jnp.bfloat16),
            1 << 20,
        )
    tables.append(join(in_plane(chosen), chips - 1 == gram_step))
    rows_list, cols_list = [table[0] for table in tables], [table[1] for table in tables]
    gram_high, gram_low = tables[gram_step][2:]

    state = pltpu.VMEM((batch_count, batch_rows, width), jnp.float32)
    send_rows = call(
        functools.partial(solve_kernel, chips, block_size, batch_count), "solve",
        [live_counts, place], [ratings, gram_high, gram_low, *rows_list, *cols_list],
        jax.ShapeDtypeStruct((users_here, width), jnp.float32),
        12 * 4 * users_here * columns * width,
        [
            pltpu.VMEM((batch_count, batch_rows, columns), jnp.float32),
            state, state, state, pltpu.VMEM((batch_count, batch_rows, 1), jnp.float32),
        ],
    )
    got_rows = lax.all_to_all(
        send_rows.reshape(device_count, quota, width), ("rep", "blk"), split_axis=0, concat_axis=0, tiled=True
    )
    return call(
        place_kernel, "place", [slots], [got_rows],
        jax.ShapeDtypeStruct((users_here, width), jnp.float32), 1 << 20,
    )


def solution(mesh):
    placed = (
        P("blk", None),
        P(("rep", "blk"), None),
        P(("rep", "blk"), None),
        P(("rep", "blk")),
        P(("rep", "blk")),
    )
    return jax.shard_map(
        on_device, mesh=mesh, in_specs=placed, out_specs=P(("rep", "blk"), None), check_vma=False
    )
```

```python
import functools
import math
import jax
import jax.numpy as jnp
from jax import lax
from jax.experimental import pallas as pl
from jax.experimental.pallas import tpu as pltpu
from jax.sharding import PartitionSpec as P

ITERS = 8
WIDE_ITERS = 2
SPARE_VMEM = 6 * 1024 * 1024

conf_scale = 6.0
ridge_term = 0.5


def dot32(left, right, dims=((1,), (0,))):
    return lax.dot_general(left, right, (dims, ((), ())), preferred_element_type=jnp.float32)


def halves(value):
    high = value.astype(jnp.bfloat16)
    low = (value - high.astype(jnp.float32)).astype(jnp.bfloat16)
    return high, low


def local_slots(core, per_panel):
    for side in range(2):
        parity = core if side == 0 else 1 - core
        for pick in range(per_panel):
            yield side, parity * per_panel + pick


def position(chips, back):
    blk = lax.axis_index("blk")
    return lax.rem(blk, 2), lax.rem(lax.div(blk, 2) + chips - back, chips)


def select_kernel(chips, steps, batch_count, per_panel, quota, note_ref, *refs):
    panel_refs, refs = refs[:2 * len(steps)], refs[2 * len(steps):]
    gram_refs = [ref for ref in refs if ref.dtype == jnp.float32]
    out_refs = refs[len(gram_refs):]
    rep, panels = lax.axis_index("rep"), 2 * chips
    slots, slot_count = 2 * per_panel, panels * per_panel
    blocks, size, _ = panel_refs[0].shape
    named = batch_count * slots
    for part, out_ref in enumerate(out_refs):
        row = (rep ^ part) * panels + lax.axis_index("blk")
        for i, back in enumerate(steps):
            core, chip = position(chips, back)
            for batch in range(batch_count):
                for side, local in local_slots(core, per_panel):
                    block = note_ref[row, quota + batch * slot_count + chip * slots + local]
                    out_ref[i * named + batch * slots + local] = panel_refs[2 * i + side][lax.rem(block, blocks)]
        for gram_ref in gram_refs:
            gram = jnp.concatenate(halves(gram_ref[...]), axis=0)
            out_ref[len(steps) * named:] = gram.reshape(-1, size, gram.shape[1])


def join_kernel(reps, steps, batch_count, per_panel, *refs):
    part_refs, (rows_ref, cols_ref, *gram_refs) = refs[:reps], refs[reps:]
    rep = lax.axis_index("rep")
    size = part_refs[0].shape[1]
    slots = 2 * per_panel
    named = batch_count * slots
    for part, ref in enumerate(part_refs):
        for i in range(len(steps)):
            for batch in range(batch_count):
                for local in range(slots):
                    offset = (i * slots + local) * reps * size + (rep ^ part) * size
                    rows_ref[batch, pl.ds(pl.multiple_of(offset, size), size), :] = ref[
                        i * named + batch * slots + local
                    ]
        extra = ref.shape[0] - len(steps) * named
        half = extra // 2
        for i, gram_ref in enumerate(gram_refs):
            start = len(steps) * named + i * half
            offset = pl.multiple_of((rep ^ part) * size * half, size * half)
            gram_ref[pl.ds(offset, size * half), :] = ref[start:start + half].reshape(size * half, ref.shape[2])
    for batch in range(batch_count):
        cols_ref[batch] = rows_ref[batch].T


def pick_kernel(chips, batch_count, per_panel, ids_ref, own_ref, other_ref, rows_ref, cols_ref):
    core, chip = position(chips, 0)
    slots = 2 * per_panel
    blocks, block_size, _ = own_ref.shape
    for batch in range(batch_count):
        for side, local in local_slots(core, per_panel):
            block = ids_ref[batch, chip * slots + local]
            held = other_ref if side else own_ref
            offset = pl.multiple_of(local * block_size, block_size)
            rows_ref[batch, pl.ds(offset, block_size), :] = held[lax.rem(block, blocks)]
        cols_ref[batch] = rows_ref[batch].T


def solve_kernel(chips, block_size, batch_count, *refs):
    live_ref, place_ref, ratings_ref, gram_high, gram_low = refs[:5]
    refs = refs[5:]
    tables = (len(refs) - 6) // 2
    rows_refs, cols_refs, refs = refs[:tables], refs[tables:2 * tables], refs[2 * tables:]
    send_ref, weight, x_s, r_s, p_s, n_s = refs
    users = ratings_ref.shape[0] // batch_count
    span = ratings_ref.shape[1] // chips
    batches = range(batch_count)
    chunks = []
    for table, ref in enumerate(rows_refs):
        chunks += [(table, first) for first in range(0, ref.shape[1], span)]

    totals = [None] * batch_count
    for back, (table, first) in enumerate(chunks):
        _, chip = position(chips, back)
        start = pl.multiple_of(chip * span, span)
        index = start + lax.broadcasted_iota(jnp.int32, (users, span), 1)
        for batch in batches:
            rated = ratings_ref[batch * users:(batch + 1) * users, pl.ds(start, span)].astype(jnp.float32)
            is_live = (index < live_ref[batch] * block_size).astype(jnp.float32)
            scaled = conf_scale * rated * is_live
            weight[batch, :, back * span:(back + 1) * span] = scaled
            both = jnp.concatenate(halves(is_live + scaled), axis=0)
            term = dot32(both, rows_refs[table][batch, first:first + span])
            totals[batch] = term if totals[batch] is None else totals[batch] + term
    for batch in batches:
        target_proj = totals[batch][:users] + totals[batch][users:]
        x_s[batch] = jnp.zeros_like(target_proj)
        r_s[batch] = target_proj
        p_s[batch] = target_proj
        n_s[batch] = jnp.sum(target_proj * target_proj, axis=1, keepdims=True)

    def step(wide):
        def body(_, carry):
            highs, boths, totals = [], [], [None] * batch_count
            for batch in batches:
                high, low = halves(p_s[batch])
                highs.append(high)
                boths.append(jnp.concatenate([high, low], axis=0))
            for k, (table, first) in enumerate(chunks):
                for batch in batches:
                    moving = boths[batch] if wide else highs[batch]
                    projected = dot32(moving, cols_refs[table][batch, :, first:first + span])
                    if wide:
                        projected = projected[:users] + projected[users:]
                    projected = projected * weight[batch, :, k * span:(k + 1) * span]
                    if wide:
                        back = jnp.concatenate(halves(projected), axis=0)
                    else:
                        back = projected.astype(jnp.bfloat16)
                    term = dot32(back, rows_refs[table][batch, first:first + span])
                    totals[batch] = term if totals[batch] is None else totals[batch] + term
            for batch in batches:
                total = totals[batch]
                if wide:
                    total = total[:users] + total[users:]
                direction = p_s[batch]
                gram_part = dot32(boths[batch], gram_high[...])
                image = (
                    gram_part[:users] + gram_part[users:] + dot32(highs[batch], gram_low[...])
                    + total + ridge_term * direction
                )
                norm_now = n_s[batch]
                step_size = norm_now / jnp.sum(direction * image, axis=1, keepdims=True)
                x_s[batch] = x_s[batch] + step_size * direction
                residual = r_s[batch] - step_size * image
                r_s[batch] = residual
                norm_next = jnp.sum(residual * residual, axis=1, keepdims=True)
                p_s[batch] = residual + norm_next / norm_now * direction
                n_s[batch] = norm_next
            return carry

        return body

    lax.fori_loop(0, WIDE_ITERS, step(True), 0)
    lax.fori_loop(WIDE_ITERS, ITERS, step(False), 0)
    for batch in batches:
        for user in range(users):
            send_ref[pl.ds(place_ref[batch * users + user], 1), :] = x_s[batch, user:user + 1, :]


def place_kernel(note_ref, got_ref, out_ref):
    for source in range(got_ref.shape[0]):
        for row in range(got_ref.shape[1]):
            out_ref[pl.ds(note_ref[source, row], 1), :] = got_ref[source, row:row + 1, :]


def smem():
    return pl.BlockSpec(memory_space=pltpu.SMEM)


def vmem():
    return pl.BlockSpec(memory_space=pltpu.VMEM)


def call(body, name, small, large, out_shape, flops, scratch=()):
    operands = (*small, *large)
    moved = sum(array.size * array.dtype.itemsize for array in (*operands, *jax.tree.leaves(out_shape)))
    kept = sum(math.prod(array.shape) * 4 for array in scratch)
    return pl.pallas_call(
        body,
        out_shape=out_shape,
        in_specs=[smem()] * len(small) + [vmem()] * len(large),
        out_specs=jax.tree.map(lambda _: vmem(), out_shape),
        scratch_shapes=list(scratch),
        compiler_params=pltpu.CompilerParams(vmem_limit_bytes=moved + kept + SPARE_VMEM),
        cost_estimate=pl.CostEstimate(flops=flops, bytes_accessed=moved, transcendentals=0),
        name=name,
    )(*operands)


def on_device(item_factors, ratings, block_ids, live_counts, owner_rows):
    item_local, width = item_factors.shape
    users_here, columns = ratings.shape
    batch_count, slot_count = block_ids.shape
    batch_rows = users_here // batch_count
    block_size = columns // slot_count
    panel_count = lax.axis_size("blk")
    rep_count = lax.axis_size("rep")
    device_count = rep_count * panel_count
    quota = users_here // device_count
    chips = panel_count // 2
    per_panel = slot_count // panel_count
    blocks = item_local // block_size
    part_rows = block_size // rep_count
    span = 2 * per_panel * block_size
    rep = lax.axis_index("rep")

    def over_blk(array, target):
        return lax.ppermute(array, "blk", [(b, target(b)) for b in range(panel_count)])

    def over_rep(array, part):
        return lax.ppermute(array, "rep", [(r, r ^ part) for r in range(rep_count)])

    def other_core(array):
        return over_blk(array, lambda b: b ^ 1)

    whole = item_factors.reshape(blocks, block_size, width)
    piece = lax.dynamic_slice(whole, (0, rep * part_rows, 0), (blocks, part_rows, width))

    after = lax.optimization_barrier
    other_whole = other_core(whole)
    pieces = [over_blk(piece, lambda b: (b + 2) % panel_count)]

    before = (jnp.arange(users_here)[:, None] < jnp.arange(users_here)[None, :]).astype(jnp.bfloat16)
    target_dev = owner_rows // users_here
    goes = target_dev[None, :] == jnp.arange(device_count)[:, None]
    goes_rank = dot32(goes.astype(jnp.bfloat16), before).astype(jnp.int32)
    sent = goes[:, None, :] & (goes_rank[:, None, :] == jnp.arange(quota)[None, :, None])
    slots = jnp.sum(jnp.where(sent, (owner_rows % users_here)[None, None, :], 0), axis=2)
    known = jnp.broadcast_to(block_ids.reshape(1, -1), (device_count, block_ids.size))
    note = lax.all_to_all(
        jnp.concatenate([slots, known], axis=1), ("rep", "blk"), split_axis=0, concat_axis=0, tiled=True
    )
    place = target_dev * quota + jnp.sum(jnp.where(goes, goes_rank, 0), axis=0)

    gram_rows = width // rep_count
    early, _ = after((item_factors, pieces[0]))
    gram = sum(
        dot32(lax.dynamic_slice(panel, (0, rep * gram_rows), (item_local, gram_rows)), panel, ((0,), (0,)))
        for panel in (early, other_whole.reshape(item_local, width))
    )
    bit = 2
    for k in range(2, chips):
        if k > 2 and bit < panel_count:
            gram = gram + over_blk(gram, lambda b: b ^ bit)
            bit *= 2
            pieces[-1], gram = after((pieces[-1], gram))
        pieces.append(over_blk(pieces[-1], lambda b: (b + 2) % panel_count))
    while bit < panel_count:
        gram = gram + over_blk(gram, lambda b: b ^ bit)
        bit *= 2

    def table_shape(steps):
        rows = len(steps) * span
        return (
            jax.ShapeDtypeStruct((batch_count, rows, width), jnp.bfloat16),
            jax.ShapeDtypeStruct((batch_count, width, rows), jnp.bfloat16),
        )

    tables = [call(
        functools.partial(pick_kernel, chips, batch_count, per_panel), "pick",
        [block_ids], [whole, other_whole], table_shape([0]), 1 << 20,
    )]

    stages = [list(range(k, min(k + 2, chips))) for k in range(1, chips, 2)]
    chosen = None
    for steps in stages:
        pairs = []
        for k in steps:
            piece = pieces[k - 1]
            if k == 1:
                piece, note = after((piece, note))
            if chosen is not None:
                piece, chosen, tables[0] = after((piece, chosen, tables[0]))
            pairs += [piece, other_core(piece)]
        if chosen is not None:
            parts = [chosen[0]] + [over_rep(chosen[part], part) for part in range(1, rep_count)]
            tables.append(call(
                functools.partial(join_kernel, rep_count, held, batch_count, per_panel), "join",
                [], parts, table_shape(held), 1 << 20,
            ))
        last = steps is stages[-1]
        count = len(steps) * batch_count * 2 * per_panel + last * (2 * gram_rows // part_rows)
        picked = jax.ShapeDtypeStruct((count, part_rows, width), jnp.bfloat16)
        chosen = call(
            functools.partial(select_kernel, chips, steps, batch_count, per_panel, quota), "select",
            [note], pairs + [gram] * last, (picked,) * rep_count, 1 << 20,
        )
        held = steps
    parts = [chosen[0]] + [over_rep(chosen[part], part) for part in range(1, rep_count)]
    grams = (jax.ShapeDtypeStruct((width, width), jnp.bfloat16),) * 2
    *table, gram_high, gram_low = call(
        functools.partial(join_kernel, rep_count, held, batch_count, per_panel), "join",
        [], parts, table_shape(held) + grams, 1 << 20,
    )
    tables.append(table)
    rows_list, cols_list = [table[0] for table in tables], [table[1] for table in tables]

    state = pltpu.VMEM((batch_count, batch_rows, width), jnp.float32)
    send_rows = call(
        functools.partial(solve_kernel, chips, block_size, batch_count), "solve",
        [live_counts, place], [ratings, gram_high, gram_low, *rows_list, *cols_list],
        jax.ShapeDtypeStruct((users_here, width), jnp.float32),
        12 * 4 * users_here * columns * width,
        [
            pltpu.VMEM((batch_count, batch_rows, columns), jnp.float32),
            state, state, state, pltpu.VMEM((batch_count, batch_rows, 1), jnp.float32),
        ],
    )
    got_rows = lax.all_to_all(
        send_rows.reshape(device_count, quota, width), ("rep", "blk"), split_axis=0, concat_axis=0, tiled=True
    )
    return call(
        place_kernel, "place", [note], [got_rows],
        jax.ShapeDtypeStruct((users_here, width), jnp.float32), 1 << 20,
    )


def solution(mesh):
    placed = (
        P("blk", None),
        P(("rep", "blk"), None),
        P(("rep", "blk"), None),
        P(("rep", "blk")),
        P(("rep", "blk")),
    )
    return jax.shard_map(
        on_device, mesh=mesh, in_specs=placed, out_specs=P(("rep", "blk"), None), check_vma=False
    )
```

```python
import functools
import math
import jax
import jax.numpy as jnp
from jax import lax
from jax.experimental import pallas as pl
from jax.experimental.pallas import tpu as pltpu
from jax.sharding import PartitionSpec as P

ITERS = 8
WIDE_ITERS = 2
LANES = 128
SPARE_VMEM = 6 * 1024 * 1024

conf_scale = 6.0
ridge_term = 0.5


def dot32(left, right, dims=((1,), (0,))):
    return lax.dot_general(left, right, (dims, ((), ())), preferred_element_type=jnp.float32)


def halves(value):
    high = value.astype(jnp.bfloat16)
    low = (value - high.astype(jnp.float32)).astype(jnp.bfloat16)
    return high, low


def local_slots(core, per_panel):
    for side in range(2):
        parity = core if side == 0 else 1 - core
        for pick in range(per_panel):
            yield side, parity * per_panel + pick


def position(chips, back):
    blk = lax.axis_index("blk")
    return lax.rem(blk, 2), lax.rem(lax.div(blk, 2) + chips - back, chips)


def select_kernel(chips, reps, steps, batch_count, per_panel, *refs):
    ids_refs, refs = refs[:reps], refs[reps:]
    panel_refs, refs = refs[:2 * len(steps)], refs[2 * len(steps):]
    gram_refs = [ref for ref in refs if ref.dtype == jnp.float32]
    out_refs = refs[len(gram_refs):]
    slots = 2 * per_panel
    blocks, size, _ = panel_refs[0].shape
    named = batch_count * slots
    for ids_ref, out_ref in zip(ids_refs, out_refs):
        for i, back in enumerate(steps):
            core, chip = position(chips, back)
            for batch in range(batch_count):
                for side, local in local_slots(core, per_panel):
                    block = ids_ref[batch, chip * slots + local]
                    out_ref[i * named + batch * slots + local] = panel_refs[2 * i + side][lax.rem(block, blocks)]
        for gram_ref in gram_refs:
            gram = jnp.concatenate(halves(gram_ref[...]), axis=0)
            out_ref[len(steps) * named:] = gram.reshape(-1, size, gram.shape[1])


def join_kernel(reps, steps, batch_count, per_panel, *refs):
    part_refs, (rows_ref, cols_ref, *gram_refs) = refs[:reps], refs[reps:]
    rep = lax.axis_index("rep")
    size = part_refs[0].shape[1]
    slots = 2 * per_panel
    named = batch_count * slots
    for part, ref in enumerate(part_refs):
        for i in range(len(steps)):
            for batch in range(batch_count):
                for local in range(slots):
                    offset = (i * slots + local) * reps * size + (rep ^ part) * size
                    rows_ref[batch, pl.ds(pl.multiple_of(offset, size), size), :] = ref[
                        i * named + batch * slots + local
                    ]
        extra = ref.shape[0] - len(steps) * named
        half = extra // 2
        for i, gram_ref in enumerate(gram_refs):
            start = len(steps) * named + i * half
            offset = pl.multiple_of((rep ^ part) * size * half, size * half)
            gram_ref[pl.ds(offset, size * half), :] = ref[start:start + half].reshape(size * half, ref.shape[2])
    for batch in range(batch_count):
        cols_ref[batch] = rows_ref[batch].T


def pick_kernel(chips, batch_count, per_panel, ids_ref, own_ref, other_ref, rows_ref, cols_ref):
    core, chip = position(chips, 0)
    slots = 2 * per_panel
    blocks, block_size, _ = own_ref.shape
    for batch in range(batch_count):
        for side, local in local_slots(core, per_panel):
            block = ids_ref[batch, chip * slots + local]
            held = other_ref if side else own_ref
            offset = pl.multiple_of(local * block_size, block_size)
            rows_ref[batch, pl.ds(offset, block_size), :] = held[lax.rem(block, blocks)]
        cols_ref[batch] = rows_ref[batch].T


def solve_kernel(chips, steps, block_size, batch_count, *refs):
    live_ref, place_ref, ratings_ref, slots_ref, gram_high, gram_low = refs[:6]
    refs = refs[6:]
    tables = (len(refs) - 6) // 2
    rows_refs, cols_refs, refs = refs[:tables], refs[tables:2 * tables], refs[2 * tables:]
    send_ref, weight, x_s, r_s, p_s, n_s = refs
    users = ratings_ref.shape[0] // batch_count
    span = ratings_ref.shape[1] // chips
    batches = range(batch_count)
    chunks = []
    for table, ref in enumerate(rows_refs):
        chunks += [(table, first) for first in range(0, ref.shape[1], span)]

    totals = [None] * batch_count
    for k, (table, first) in enumerate(chunks):
        _, chip = position(chips, steps[k])
        start = pl.multiple_of(chip * span, span)
        index = start + lax.broadcasted_iota(jnp.int32, (users, span), 1)
        for batch in batches:
            rated = ratings_ref[batch * users:(batch + 1) * users, pl.ds(start, span)].astype(jnp.float32)
            is_live = (index < live_ref[batch] * block_size).astype(jnp.float32)
            scaled = conf_scale * rated * is_live
            weight[batch, :, k * span:(k + 1) * span] = scaled
            both = jnp.concatenate(halves(is_live + scaled), axis=0)
            term = dot32(both, rows_refs[table][batch, first:first + span])
            totals[batch] = term if totals[batch] is None else totals[batch] + term
    for batch in batches:
        target_proj = totals[batch][:users] + totals[batch][users:]
        x_s[batch] = jnp.zeros_like(target_proj)
        r_s[batch] = target_proj
        p_s[batch] = target_proj
        n_s[batch] = jnp.sum(target_proj * target_proj, axis=1, keepdims=True)

    def step(wide):
        def body(_, carry):
            highs, boths, totals = [], [], [None] * batch_count
            for batch in batches:
                high, low = halves(p_s[batch])
                highs.append(high)
                boths.append(jnp.concatenate([high, low], axis=0))
            for k, (table, first) in enumerate(chunks):
                for batch in batches:
                    moving = boths[batch] if wide else highs[batch]
                    projected = dot32(moving, cols_refs[table][batch, :, first:first + span])
                    if wide:
                        projected = projected[:users] + projected[users:]
                    projected = projected * weight[batch, :, k * span:(k + 1) * span]
                    if wide:
                        back = jnp.concatenate(halves(projected), axis=0)
                    else:
                        back = projected.astype(jnp.bfloat16)
                    term = dot32(back, rows_refs[table][batch, first:first + span])
                    totals[batch] = term if totals[batch] is None else totals[batch] + term
            for batch in batches:
                total = totals[batch]
                if wide:
                    total = total[:users] + total[users:]
                direction = p_s[batch]
                gram_part = dot32(boths[batch], gram_high[...])
                image = (
                    gram_part[:users] + gram_part[users:] + dot32(highs[batch], gram_low[...])
                    + total + ridge_term * direction
                )
                norm_now = n_s[batch]
                step_size = norm_now / jnp.sum(direction * image, axis=1, keepdims=True)
                x_s[batch] = x_s[batch] + step_size * direction
                residual = r_s[batch] - step_size * image
                r_s[batch] = residual
                norm_next = jnp.sum(residual * residual, axis=1, keepdims=True)
                p_s[batch] = residual + norm_next / norm_now * direction
                n_s[batch] = norm_next
            return carry

        return body

    lax.fori_loop(0, WIDE_ITERS, step(True), 0)
    lax.fori_loop(WIDE_ITERS, ITERS, step(False), 0)
    width = x_s.shape[2]
    quota = batch_count * users // send_ref.shape[0]
    send_ref[:, :, quota * width:] = slots_ref[...]
    for batch in batches:
        for user in range(users):
            place = place_ref[batch * users + user]
            lanes = pl.ds(pl.multiple_of(lax.rem(place, quota) * width, width), width)
            send_ref[lax.div(place, quota), :, lanes] = x_s[batch, user:user + 1, :]


def place_kernel(got_ref, out_ref, slots, sem):
    width = out_ref.shape[1]
    quota = out_ref.shape[0] // got_ref.shape[0]
    copy = pltpu.make_async_copy(got_ref.at[:, :, pl.ds(quota * width, LANES)], slots, sem)
    copy.start()
    copy.wait()
    for source in range(got_ref.shape[0]):
        for row in range(quota):
            slot = slots[source, 0, row].astype(jnp.int32)
            out_ref[pl.ds(slot, 1), :] = got_ref[source, :, row * width:(row + 1) * width]


def smem():
    return pl.BlockSpec(memory_space=pltpu.SMEM)


def vmem():
    return pl.BlockSpec(memory_space=pltpu.VMEM)


def call(body, name, small, large, out_shape, flops, scratch=()):
    operands = (*small, *large)
    moved = sum(array.size * array.dtype.itemsize for array in (*operands, *jax.tree.leaves(out_shape)))
    kept = sum(math.prod(array.shape) * 4 for array in scratch if hasattr(array, "shape"))
    return pl.pallas_call(
        body,
        out_shape=out_shape,
        in_specs=[smem()] * len(small) + [vmem()] * len(large),
        out_specs=jax.tree.map(lambda _: vmem(), out_shape),
        scratch_shapes=list(scratch),
        compiler_params=pltpu.CompilerParams(vmem_limit_bytes=moved + kept + SPARE_VMEM),
        cost_estimate=pl.CostEstimate(flops=flops, bytes_accessed=moved, transcendentals=0),
        name=name,
    )(*operands)


def on_device(item_factors, ratings, block_ids, live_counts, owner_rows):
    item_local, width = item_factors.shape
    users_here, columns = ratings.shape
    batch_count, slot_count = block_ids.shape
    batch_rows = users_here // batch_count
    block_size = columns // slot_count
    panel_count = lax.axis_size("blk")
    rep_count = lax.axis_size("rep")
    device_count = rep_count * panel_count
    quota = users_here // device_count
    chips = panel_count // 2
    per_panel = slot_count // panel_count
    blocks = item_local // block_size
    part_rows = block_size // rep_count
    span = 2 * per_panel * block_size
    rep = lax.axis_index("rep")

    def over_blk(array, target):
        return lax.ppermute(array, "blk", [(b, target(b)) for b in range(panel_count)])

    def over_rep(array, part):
        return lax.ppermute(array, "rep", [(r, r ^ part) for r in range(rep_count)])

    def other_core(array):
        return over_blk(array, lambda b: b ^ 1)

    whole = item_factors.reshape(blocks, block_size, width)
    piece = lax.dynamic_slice(whole, (0, rep * part_rows, 0), (blocks, part_rows, width))

    after = lax.optimization_barrier
    other_whole = other_core(whole)
    pieces = {0: piece}
    turn = chips // 2
    for k in range(1, turn + 1):
        pieces[k] = over_blk(pieces[k - 1], lambda b: (b + 2) % panel_count)
        if k < chips - k:
            pieces[chips - k] = over_blk(pieces[(chips - k + 1) % chips], lambda b: (b - 2) % panel_count)
    ids = [block_ids] + [over_rep(block_ids, part) for part in range(1, rep_count)]

    before = (jnp.arange(users_here)[:, None] < jnp.arange(users_here)[None, :]).astype(jnp.bfloat16)
    target_dev = owner_rows // users_here
    goes = target_dev[None, :] == jnp.arange(device_count)[:, None]
    goes_rank = dot32(goes.astype(jnp.bfloat16), before).astype(jnp.int32)
    sent = goes[:, None, :] & (goes_rank[:, None, :] == jnp.arange(quota)[None, :, None])
    slots = jnp.sum(jnp.where(sent, (owner_rows % users_here)[None, None, :], 0), axis=2)
    slots = jnp.pad(slots.astype(jnp.float32), ((0, 0), (0, LANES - quota)))[:, None, :]
    place = target_dev * quota + jnp.sum(jnp.where(goes, goes_rank, 0), axis=0)

    gram_rows = width // rep_count
    gram = sum(
        dot32(lax.dynamic_slice(panel, (0, rep * gram_rows), (item_local, gram_rows)), panel, ((0,), (0,)))
        for panel in (item_factors, other_whole.reshape(item_local, width))
    )
    gram = gram + over_blk(gram, lambda b: b ^ 2)

    def table_shape(steps):
        rows = len(steps) * span
        return (
            jax.ShapeDtypeStruct((batch_count, rows, width), jnp.bfloat16),
            jax.ShapeDtypeStruct((batch_count, width, rows), jnp.bfloat16),
        )

    tables = [call(
        functools.partial(pick_kernel, chips, batch_count, per_panel), "pick",
        [block_ids], [whole, other_whole], table_shape([0]), 1 << 20,
    )]

    near_first = sorted(range(1, chips), key=lambda k: min(k, chips - k))
    stages = [near_first[i:i + 2] for i in range(0, chips - 1, 2)]
    chosen = None
    for steps in stages:
        pairs = []
        for k in steps:
            piece = pieces[k]
            if chosen is not None:
                piece, chosen, tables[0], gram = after((piece, chosen, tables[0], gram))
            pairs += [piece, other_core(piece)]
        if chosen is not None:
            parts = [chosen[0]] + [over_rep(chosen[part], part) for part in range(1, rep_count)]
            tables.append(call(
                functools.partial(join_kernel, rep_count, held, batch_count, per_panel), "join",
                [], parts, table_shape(held), 1 << 20,
            ))
        last = steps is stages[-1]
        bit = 4
        while last and bit < panel_count:
            gram = gram + over_blk(gram, lambda b: b ^ bit)
            bit *= 2
        count = len(steps) * batch_count * 2 * per_panel + last * (2 * gram_rows // part_rows)
        picked = jax.ShapeDtypeStruct((count, part_rows, width), jnp.bfloat16)
        chosen = call(
            functools.partial(select_kernel, chips, rep_count, steps, batch_count, per_panel), "select",
            ids, pairs + [gram] * last, (picked,) * rep_count, 1 << 20,
        )
        held = steps
    parts = [chosen[0]] + [over_rep(chosen[part], part) for part in range(1, rep_count)]
    grams = (jax.ShapeDtypeStruct((width, width), jnp.bfloat16),) * 2
    *table, gram_high, gram_low = call(
        functools.partial(join_kernel, rep_count, held, batch_count, per_panel), "join",
        [], parts, table_shape(held) + grams, 1 << 20,
    )
    tables.append(table)
    rows_list, cols_list = [table[0] for table in tables], [table[1] for table in tables]

    state = pltpu.VMEM((batch_count, batch_rows, width), jnp.float32)
    lanes = quota * width + LANES
    send_rows = call(
        functools.partial(solve_kernel, chips, [0] + near_first, block_size, batch_count), "solve",
        [live_counts, place], [ratings, slots, gram_high, gram_low, *rows_list, *cols_list],
        jax.ShapeDtypeStruct((device_count, 1, lanes), jnp.float32),
        12 * 4 * users_here * columns * width,
        [
            pltpu.VMEM((batch_count, batch_rows, columns), jnp.float32),
            state, state, state, pltpu.VMEM((batch_count, batch_rows, 1), jnp.float32),
        ],
    )
    got_rows = lax.all_to_all(send_rows, ("rep", "blk"), split_axis=0, concat_axis=0, tiled=True)
    return call(
        place_kernel, "place", [], [got_rows],
        jax.ShapeDtypeStruct((users_here, width), jnp.float32), 1 << 20,
        [pltpu.SMEM((device_count, 1, LANES), jnp.float32), pltpu.SemaphoreType.DMA],
    )


def solution(mesh):
    placed = (
        P("blk", None),
        P(("rep", "blk"), None),
        P(("rep", "blk"), None),
        P(("rep", "blk")),
        P(("rep", "blk")),
    )
    return jax.shard_map(
        on_device, mesh=mesh, in_specs=placed, out_specs=P(("rep", "blk"), None), check_vma=False
    )
```

```python
import functools
import math
import jax
import jax.numpy as jnp
from jax import lax
from jax.experimental import pallas as pl
from jax.experimental.pallas import tpu as pltpu
from jax.sharding import PartitionSpec as P

ITERS = 8
WIDE_ITERS = 2
LANES = 128
SPARE_VMEM = 6 * 1024 * 1024

conf_scale = 6.0
ridge_term = 0.5


def dot32(left, right, dims=((1,), (0,))):
    return lax.dot_general(left, right, (dims, ((), ())), preferred_element_type=jnp.float32)


def halves(value):
    high = value.astype(jnp.bfloat16)
    low = (value - high.astype(jnp.float32)).astype(jnp.bfloat16)
    return high, low


def local_slots(core, per_panel):
    for side in range(2):
        parity = core if side == 0 else 1 - core
        for pick in range(per_panel):
            yield side, parity * per_panel + pick


def position(step):
    blk = lax.axis_index("blk")
    return lax.rem(blk, 2), lax.div(blk, 2) ^ step


def select_kernel(reps, steps, batch_count, per_panel, *refs):
    ids_refs, refs = refs[:reps], refs[reps:]
    panel_refs, refs = refs[:2 * len(steps)], refs[2 * len(steps):]
    gram_refs = [ref for ref in refs if ref.dtype == jnp.float32]
    out_refs = refs[len(gram_refs):]
    slots = 2 * per_panel
    blocks, size, _ = panel_refs[0].shape
    named = batch_count * slots
    for ids_ref, out_ref in zip(ids_refs, out_refs):
        for i, step in enumerate(steps):
            core, chip = position(step)
            for batch in range(batch_count):
                for side, local in local_slots(core, per_panel):
                    block = ids_ref[batch, chip * slots + local]
                    out_ref[i * named + batch * slots + local] = panel_refs[2 * i + side][lax.rem(block, blocks)]
        for gram_ref in gram_refs:
            gram = jnp.concatenate(halves(gram_ref[...]), axis=0)
            out_ref[len(steps) * named:] = gram.reshape(-1, size, gram.shape[1])


def join_kernel(reps, steps, batch_count, per_panel, *refs):
    part_refs, (rows_ref, cols_ref, *gram_refs) = refs[:reps], refs[reps:]
    rep = lax.axis_index("rep")
    size = part_refs[0].shape[1]
    slots = 2 * per_panel
    named = batch_count * slots
    for part, ref in enumerate(part_refs):
        for i in range(steps):
            for batch in range(batch_count):
                for local in range(slots):
                    offset = (i * slots + local) * reps * size + (rep ^ part) * size
                    rows_ref[batch, pl.ds(pl.multiple_of(offset, size), size), :] = ref[
                        i * named + batch * slots + local
                    ]
        extra = ref.shape[0] - steps * named
        half = extra // 2
        for i, gram_ref in enumerate(gram_refs):
            start = steps * named + i * half
            offset = pl.multiple_of((rep ^ part) * size * half, size * half)
            gram_ref[pl.ds(offset, size * half), :] = ref[start:start + half].reshape(size * half, ref.shape[2])
    for batch in range(batch_count):
        cols_ref[batch] = rows_ref[batch].T


def pick_kernel(batch_count, per_panel, ids_ref, own_ref, other_ref, rows_ref, cols_ref):
    core, chip = position(0)
    slots = 2 * per_panel
    blocks, block_size, _ = own_ref.shape
    for batch in range(batch_count):
        for side, local in local_slots(core, per_panel):
            block = ids_ref[batch, chip * slots + local]
            held = other_ref if side else own_ref
            offset = pl.multiple_of(local * block_size, block_size)
            rows_ref[batch, pl.ds(offset, block_size), :] = held[lax.rem(block, blocks)]
        cols_ref[batch] = rows_ref[batch].T


def solve_kernel(chips, steps, block_size, batch_count, *refs):
    live_ref, place_ref, ratings_ref, slots_ref, gram_high, gram_low = refs[:6]
    refs = refs[6:]
    tables = (len(refs) - 6) // 2
    rows_refs, cols_refs, refs = refs[:tables], refs[tables:2 * tables], refs[2 * tables:]
    send_ref, weight, x_s, r_s, p_s, n_s = refs
    users = ratings_ref.shape[0] // batch_count
    span = ratings_ref.shape[1] // chips
    batches = range(batch_count)
    chunks = []
    for table, ref in enumerate(rows_refs):
        chunks += [(table, first) for first in range(0, ref.shape[1], span)]

    totals = [None] * batch_count
    for k, (table, first) in enumerate(chunks):
        _, chip = position(steps[k])
        start = pl.multiple_of(chip * span, span)
        index = start + lax.broadcasted_iota(jnp.int32, (users, span), 1)
        for batch in batches:
            rated = ratings_ref[batch * users:(batch + 1) * users, pl.ds(start, span)].astype(jnp.float32)
            is_live = (index < live_ref[batch] * block_size).astype(jnp.float32)
            scaled = conf_scale * rated * is_live
            weight[batch, :, k * span:(k + 1) * span] = scaled
            both = jnp.concatenate(halves(is_live + scaled), axis=0)
            term = dot32(both, rows_refs[table][batch, first:first + span])
            totals[batch] = term if totals[batch] is None else totals[batch] + term
    for batch in batches:
        target_proj = totals[batch][:users] + totals[batch][users:]
        x_s[batch] = jnp.zeros_like(target_proj)
        r_s[batch] = target_proj
        p_s[batch] = target_proj
        n_s[batch] = jnp.sum(target_proj * target_proj, axis=1, keepdims=True)

    def step(wide):
        def body(_, carry):
            highs, boths, totals = [], [], [None] * batch_count
            for batch in batches:
                high, low = halves(p_s[batch])
                highs.append(high)
                boths.append(jnp.concatenate([high, low], axis=0))
            for k, (table, first) in enumerate(chunks):
                for batch in batches:
                    moving = boths[batch] if wide else highs[batch]
                    projected = dot32(moving, cols_refs[table][batch, :, first:first + span])
                    if wide:
                        projected = projected[:users] + projected[users:]
                    projected = projected * weight[batch, :, k * span:(k + 1) * span]
                    if wide:
                        back = jnp.concatenate(halves(projected), axis=0)
                    else:
                        back = projected.astype(jnp.bfloat16)
                    term = dot32(back, rows_refs[table][batch, first:first + span])
                    totals[batch] = term if totals[batch] is None else totals[batch] + term
            for batch in batches:
                total = totals[batch]
                if wide:
                    total = total[:users] + total[users:]
                direction = p_s[batch]
                gram_part = dot32(boths[batch], gram_high[...])
                image = (
                    gram_part[:users] + gram_part[users:] + dot32(highs[batch], gram_low[...])
                    + total + ridge_term * direction
                )
                norm_now = n_s[batch]
                step_size = norm_now / jnp.sum(direction * image, axis=1, keepdims=True)
                x_s[batch] = x_s[batch] + step_size * direction
                residual = r_s[batch] - step_size * image
                r_s[batch] = residual
                norm_next = jnp.sum(residual * residual, axis=1, keepdims=True)
                p_s[batch] = residual + norm_next / norm_now * direction
                n_s[batch] = norm_next
            return carry

        return body

    lax.fori_loop(0, WIDE_ITERS, step(True), 0)
    lax.fori_loop(WIDE_ITERS, ITERS, step(False), 0)
    width = x_s.shape[2]
    quota = batch_count * users // send_ref.shape[0]
    send_ref[:, :, quota * width:] = slots_ref[...]
    for batch in batches:
        for user in range(users):
            place = place_ref[batch * users + user]
            lanes = pl.ds(pl.multiple_of(lax.rem(place, quota) * width, width), width)
            send_ref[lax.div(place, quota), :, lanes] = x_s[batch, user:user + 1, :]


def place_kernel(got_ref, out_ref, slots, sem):
    width = out_ref.shape[1]
    quota = out_ref.shape[0] // got_ref.shape[0]
    copy = pltpu.make_async_copy(got_ref.at[:, :, pl.ds(quota * width, LANES)], slots, sem)
    copy.start()
    copy.wait()
    for source in range(got_ref.shape[0]):
        for row in range(quota):
            slot = slots[source, 0, row].astype(jnp.int32)
            out_ref[pl.ds(slot, 1), :] = got_ref[source, :, row * width:(row + 1) * width]


def smem():
    return pl.BlockSpec(memory_space=pltpu.SMEM)


def vmem():
    return pl.BlockSpec(memory_space=pltpu.VMEM)


def call(body, name, small, large, out_shape, flops, scratch=()):
    operands = (*small, *large)
    moved = sum(array.size * array.dtype.itemsize for array in (*operands, *jax.tree.leaves(out_shape)))
    kept = sum(math.prod(array.shape) * 4 for array in scratch if hasattr(array, "shape"))
    return pl.pallas_call(
        body,
        out_shape=out_shape,
        in_specs=[smem()] * len(small) + [vmem()] * len(large),
        out_specs=jax.tree.map(lambda _: vmem(), out_shape),
        scratch_shapes=list(scratch),
        compiler_params=pltpu.CompilerParams(vmem_limit_bytes=moved + kept + SPARE_VMEM),
        cost_estimate=pl.CostEstimate(flops=flops, bytes_accessed=moved, transcendentals=0),
        name=name,
    )(*operands)


def on_device(item_factors, ratings, block_ids, live_counts, owner_rows):
    item_local, width = item_factors.shape
    users_here, columns = ratings.shape
    batch_count, slot_count = block_ids.shape
    batch_rows = users_here // batch_count
    block_size = columns // slot_count
    panel_count = lax.axis_size("blk")
    rep_count = lax.axis_size("rep")
    device_count = rep_count * panel_count
    quota = users_here // device_count
    chips = panel_count // 2
    per_panel = slot_count // panel_count
    blocks = item_local // block_size
    part_rows = block_size // rep_count
    span = 2 * per_panel * block_size
    rep = lax.axis_index("rep")

    def over_blk(array, target):
        return lax.ppermute(array, "blk", [(b, target(b)) for b in range(panel_count)])

    def over_rep(array, part):
        return lax.ppermute(array, "rep", [(r, r ^ part) for r in range(rep_count)])

    def other_core(array):
        return over_blk(array, lambda b: b ^ 1)

    whole = item_factors.reshape(blocks, block_size, width)
    piece = lax.dynamic_slice(whole, (0, rep * part_rows, 0), (blocks, part_rows, width))

    after = lax.optimization_barrier
    other_whole = other_core(whole)
    pieces = {0: piece}
    for k in range(1, min(chips, 4), 2):
        pieces[k] = over_blk(piece, lambda b: b ^ 2 * k)
    if chips > 3:
        pieces[3], pieces[1] = after((pieces[3], pieces[1]))
    ids = [block_ids] + [over_rep(block_ids, part) for part in range(1, rep_count)]

    before = (jnp.arange(users_here)[:, None] < jnp.arange(users_here)[None, :]).astype(jnp.bfloat16)
    target_dev = owner_rows // users_here
    goes = target_dev[None, :] == jnp.arange(device_count)[:, None]
    goes_rank = dot32(goes.astype(jnp.bfloat16), before).astype(jnp.int32)
    sent = goes[:, None, :] & (goes_rank[:, None, :] == jnp.arange(quota)[None, :, None])
    slots = jnp.sum(jnp.where(sent, (owner_rows % users_here)[None, None, :], 0), axis=2)
    slots = jnp.pad(slots.astype(jnp.float32), ((0, 0), (0, LANES - quota)))[:, None, :]
    place = target_dev * quota + jnp.sum(jnp.where(goes, goes_rank, 0), axis=0)

    gram_rows = width // rep_count
    gram = sum(
        dot32(lax.dynamic_slice(panel, (0, rep * gram_rows), (item_local, gram_rows)), panel, ((0,), (0,)))
        for panel in (item_factors, other_whole.reshape(item_local, width))
    )
    gram = gram + over_blk(gram, lambda b: b ^ 2)

    def table_shape(count):
        rows = count * span
        return (
            jax.ShapeDtypeStruct((batch_count, rows, width), jnp.bfloat16),
            jax.ShapeDtypeStruct((batch_count, width, rows), jnp.bfloat16),
        )

    tables = [call(
        functools.partial(pick_kernel, batch_count, per_panel), "pick",
        [block_ids], [whole, other_whole], table_shape(1), 1 << 20,
    )]

    steps = [k for k in (1, 3, 2) if k < chips] + list(range(4, chips))
    chosen = None
    for k in steps:
        if k not in pieces:
            source, hop = (3, 1) if k == 2 else (k - 4, 4)
            pieces[k] = over_blk(pieces[source], lambda b: b ^ 2 * hop)
        piece = pieces[k]
        if k == 2:
            piece, chosen = after((piece, chosen))
        if k == steps[-1]:
            piece, tables[0], gram = after((piece, tables[0], gram))
        pair = [piece, other_core(piece)]
        if chosen is not None:
            parts = [chosen[0]] + [over_rep(chosen[part], part) for part in range(1, rep_count)]
            if k != steps[-1]:
                pair, parts = after((pair, parts))
            tables.append(call(
                functools.partial(join_kernel, rep_count, 1, batch_count, per_panel), "join",
                [], parts, table_shape(1), 1 << 20,
            ))
        last = k == steps[-1]
        bit = 4
        while last and bit < panel_count:
            gram = gram + over_blk(gram, lambda b: b ^ bit)
            bit *= 2
        count = batch_count * 2 * per_panel + last * (2 * gram_rows // part_rows)
        picked = jax.ShapeDtypeStruct((count, part_rows, width), jnp.bfloat16)
        chosen = call(
            functools.partial(select_kernel, rep_count, [k], batch_count, per_panel), "select",
            ids, pair + [gram] * last, (picked,) * rep_count, 1 << 20,
        )
    parts = [chosen[0]] + [over_rep(chosen[part], part) for part in range(1, rep_count)]
    grams = (jax.ShapeDtypeStruct((width, width), jnp.bfloat16),) * 2
    *table, gram_high, gram_low = call(
        functools.partial(join_kernel, rep_count, 1, batch_count, per_panel), "join",
        [], parts, table_shape(1) + grams, 1 << 20,
    )
    tables.append(table)
    rows_list, cols_list = [table[0] for table in tables], [table[1] for table in tables]

    state = pltpu.VMEM((batch_count, batch_rows, width), jnp.float32)
    lanes = quota * width + LANES
    send_rows = call(
        functools.partial(solve_kernel, chips, [0] + steps, block_size, batch_count), "solve",
        [live_counts, place], [ratings, slots, gram_high, gram_low, *rows_list, *cols_list],
        jax.ShapeDtypeStruct((device_count, 1, lanes), jnp.float32),
        12 * 4 * users_here * columns * width,
        [
            pltpu.VMEM((batch_count, batch_rows, columns), jnp.float32),
            state, state, state, pltpu.VMEM((batch_count, batch_rows, 1), jnp.float32),
        ],
    )
    got_rows = lax.all_to_all(send_rows, ("rep", "blk"), split_axis=0, concat_axis=0, tiled=True)
    return call(
        place_kernel, "place", [], [got_rows],
        jax.ShapeDtypeStruct((users_here, width), jnp.float32), 1 << 20,
        [pltpu.SMEM((device_count, 1, LANES), jnp.float32), pltpu.SemaphoreType.DMA],
    )


def solution(mesh):
    placed = (
        P("blk", None),
        P(("rep", "blk"), None),
        P(("rep", "blk"), None),
        P(("rep", "blk")),
        P(("rep", "blk")),
    )
    return jax.shard_map(
        on_device, mesh=mesh, in_specs=placed, out_specs=P(("rep", "blk"), None), check_vma=False
    )
```

```python
import functools
import math
import jax
import jax.numpy as jnp
from jax import lax
from jax.experimental import pallas as pl
from jax.experimental.pallas import tpu as pltpu
from jax.sharding import PartitionSpec as P

ITERS = 8
WIDE_ITERS = 2
LANES = 128
SPARE_VMEM = 6 * 1024 * 1024

conf_scale = 6.0
ridge_term = 0.5


def dot32(left, right, dims=((1,), (0,))):
    return lax.dot_general(left, right, (dims, ((), ())), preferred_element_type=jnp.float32)


def halves(value):
    high = value.astype(jnp.bfloat16)
    low = (value - high.astype(jnp.float32)).astype(jnp.bfloat16)
    return high, low


def local_slots(core, per_panel):
    for side in range(2):
        parity = core if side == 0 else 1 - core
        for pick in range(per_panel):
            yield side, parity * per_panel + pick


def position(step):
    blk = lax.axis_index("blk")
    return lax.rem(blk, 2), lax.div(blk, 2) ^ step


def select_kernel(reps, steps, batch_count, per_panel, *refs):
    ids_refs, refs = refs[:reps], refs[reps:]
    panel_refs, refs = refs[:2 * len(steps)], refs[2 * len(steps):]
    gram_refs = [ref for ref in refs if ref.dtype == jnp.float32]
    out_refs = refs[len(gram_refs):]
    slots = 2 * per_panel
    blocks, size, _ = panel_refs[0].shape
    named = batch_count * slots
    for ids_ref, out_ref in zip(ids_refs, out_refs):
        for i, step in enumerate(steps):
            core, chip = position(step)
            for batch in range(batch_count):
                for side, local in local_slots(core, per_panel):
                    block = ids_ref[batch, chip * slots + local]
                    out_ref[i * named + batch * slots + local] = panel_refs[2 * i + side][lax.rem(block, blocks)]
        for gram_ref in gram_refs:
            gram = jnp.concatenate(halves(gram_ref[...]), axis=0)
            out_ref[len(steps) * named:] = gram.reshape(-1, size, gram.shape[1])


def join_kernel(reps, steps, batch_count, per_panel, *refs):
    part_refs, (rows_ref, cols_ref, *gram_refs) = refs[:reps], refs[reps:]
    rep = lax.axis_index("rep")
    size = part_refs[0].shape[1]
    slots = 2 * per_panel
    named = batch_count * slots
    for part, ref in enumerate(part_refs):
        for i in range(steps):
            for batch in range(batch_count):
                for local in range(slots):
                    offset = (i * slots + local) * reps * size + (rep ^ part) * size
                    rows_ref[batch, pl.ds(pl.multiple_of(offset, size), size), :] = ref[
                        i * named + batch * slots + local
                    ]
        extra = ref.shape[0] - steps * named
        half = extra // 2
        for i, gram_ref in enumerate(gram_refs):
            start = steps * named + i * half
            offset = pl.multiple_of((rep ^ part) * size * half, size * half)
            gram_ref[pl.ds(offset, size * half), :] = ref[start:start + half].reshape(size * half, ref.shape[2])
    for batch in range(batch_count):
        cols_ref[batch] = rows_ref[batch].T


def pick_kernel(batch_count, per_panel, ids_ref, own_ref, other_ref, rows_ref, cols_ref):
    core, chip = position(0)
    slots = 2 * per_panel
    blocks, block_size, _ = own_ref.shape
    for batch in range(batch_count):
        for side, local in local_slots(core, per_panel):
            block = ids_ref[batch, chip * slots + local]
            held = other_ref if side else own_ref
            offset = pl.multiple_of(local * block_size, block_size)
            rows_ref[batch, pl.ds(offset, block_size), :] = held[lax.rem(block, blocks)]
        cols_ref[batch] = rows_ref[batch].T


def solve_kernel(chips, steps, block_size, batch_count, *refs):
    live_ref, place_ref, ratings_ref, slots_ref, gram_high, gram_low = refs[:6]
    refs = refs[6:]
    tables = (len(refs) - 6) // 2
    rows_refs, cols_refs, refs = refs[:tables], refs[tables:2 * tables], refs[2 * tables:]
    send_ref, weight, x_s, r_s, p_s, n_s = refs
    users = ratings_ref.shape[0] // batch_count
    span = ratings_ref.shape[1] // chips
    batches = range(batch_count)
    chunks = []
    for table, ref in enumerate(rows_refs):
        chunks += [(table, first) for first in range(0, ref.shape[1], span)]

    totals = [None] * batch_count
    for k, (table, first) in enumerate(chunks):
        _, chip = position(steps[k])
        start = pl.multiple_of(chip * span, span)
        index = start + lax.broadcasted_iota(jnp.int32, (users, span), 1)
        for batch in batches:
            rated = ratings_ref[batch * users:(batch + 1) * users, pl.ds(start, span)].astype(jnp.float32)
            is_live = (index < live_ref[batch] * block_size).astype(jnp.float32)
            scaled = conf_scale * rated * is_live
            weight[batch, :, k * span:(k + 1) * span] = scaled
            both = jnp.concatenate(halves(is_live + scaled), axis=0)
            term = dot32(both, rows_refs[table][batch, first:first + span])
            totals[batch] = term if totals[batch] is None else totals[batch] + term
    for batch in batches:
        target_proj = totals[batch][:users] + totals[batch][users:]
        x_s[batch] = jnp.zeros_like(target_proj)
        r_s[batch] = target_proj
        p_s[batch] = target_proj
        n_s[batch] = jnp.sum(target_proj * target_proj, axis=1, keepdims=True)

    def step(wide):
        def body(_, carry):
            highs, boths, totals = [], [], [None] * batch_count
            for batch in batches:
                high, low = halves(p_s[batch])
                highs.append(high)
                boths.append(jnp.concatenate([high, low], axis=0))
            for k, (table, first) in enumerate(chunks):
                for batch in batches:
                    moving = boths[batch] if wide else highs[batch]
                    projected = dot32(moving, cols_refs[table][batch, :, first:first + span])
                    if wide:
                        projected = projected[:users] + projected[users:]
                    projected = projected * weight[batch, :, k * span:(k + 1) * span]
                    if wide:
                        back = jnp.concatenate(halves(projected), axis=0)
                    else:
                        back = projected.astype(jnp.bfloat16)
                    term = dot32(back, rows_refs[table][batch, first:first + span])
                    totals[batch] = term if totals[batch] is None else totals[batch] + term
            for batch in batches:
                total = totals[batch]
                if wide:
                    total = total[:users] + total[users:]
                direction = p_s[batch]
                gram_part = dot32(boths[batch], gram_high[...])
                image = (
                    gram_part[:users] + gram_part[users:] + dot32(highs[batch], gram_low[...])
                    + total + ridge_term * direction
                )
                norm_now = n_s[batch]
                step_size = norm_now / jnp.sum(direction * image, axis=1, keepdims=True)
                x_s[batch] = x_s[batch] + step_size * direction
                residual = r_s[batch] - step_size * image
                r_s[batch] = residual
                norm_next = jnp.sum(residual * residual, axis=1, keepdims=True)
                p_s[batch] = residual + norm_next / norm_now * direction
                n_s[batch] = norm_next
            return carry

        return body

    lax.fori_loop(0, WIDE_ITERS, step(True), 0)
    lax.fori_loop(WIDE_ITERS, ITERS, step(False), 0)
    width = x_s.shape[2]
    quota = batch_count * users // send_ref.shape[0]
    send_ref[:, :, quota * width:] = slots_ref[...]
    for batch in batches:
        for user in range(users):
            place = place_ref[batch * users + user]
            lanes = pl.ds(pl.multiple_of(lax.rem(place, quota) * width, width), width)
            send_ref[lax.div(place, quota), :, lanes] = x_s[batch, user:user + 1, :]


def place_kernel(got_ref, out_ref, slots, sem):
    width = out_ref.shape[1]
    quota = out_ref.shape[0] // got_ref.shape[0]
    copy = pltpu.make_async_copy(got_ref.at[:, :, pl.ds(quota * width, LANES)], slots, sem)
    copy.start()
    copy.wait()
    for source in range(got_ref.shape[0]):
        for row in range(quota):
            slot = slots[source, 0, row].astype(jnp.int32)
            out_ref[pl.ds(slot, 1), :] = got_ref[source, :, row * width:(row + 1) * width]


def smem():
    return pl.BlockSpec(memory_space=pltpu.SMEM)


def vmem():
    return pl.BlockSpec(memory_space=pltpu.VMEM)


def call(body, name, small, large, out_shape, flops, scratch=()):
    operands = (*small, *large)
    moved = sum(array.size * array.dtype.itemsize for array in (*operands, *jax.tree.leaves(out_shape)))
    kept = sum(math.prod(array.shape) * 4 for array in scratch if hasattr(array, "shape"))
    return pl.pallas_call(
        body,
        out_shape=out_shape,
        in_specs=[smem()] * len(small) + [vmem()] * len(large),
        out_specs=jax.tree.map(lambda _: vmem(), out_shape),
        scratch_shapes=list(scratch),
        compiler_params=pltpu.CompilerParams(vmem_limit_bytes=moved + kept + SPARE_VMEM),
        cost_estimate=pl.CostEstimate(flops=flops, bytes_accessed=moved, transcendentals=0),
        name=name,
    )(*operands)


def on_device(item_factors, ratings, block_ids, live_counts, owner_rows):
    item_local, width = item_factors.shape
    users_here, columns = ratings.shape
    batch_count, slot_count = block_ids.shape
    batch_rows = users_here // batch_count
    block_size = columns // slot_count
    panel_count = lax.axis_size("blk")
    rep_count = lax.axis_size("rep")
    device_count = rep_count * panel_count
    quota = users_here // device_count
    chips = panel_count // 2
    per_panel = slot_count // panel_count
    blocks = item_local // block_size
    part_rows = block_size // rep_count
    span = 2 * per_panel * block_size
    rep = lax.axis_index("rep")

    def over_blk(array, target):
        return lax.ppermute(array, "blk", [(b, target(b)) for b in range(panel_count)])

    def over_rep(array, part):
        return lax.ppermute(array, "rep", [(r, r ^ part) for r in range(rep_count)])

    def other_core(array):
        return over_blk(array, lambda b: b ^ 1)

    whole = item_factors.reshape(blocks, block_size, width)
    piece = lax.dynamic_slice(whole, (0, rep * part_rows, 0), (blocks, part_rows, width))

    after = lax.optimization_barrier
    other_whole = other_core(whole)
    pieces = {k: over_blk(piece, lambda b: b ^ 2 * k) for k in range(1, min(chips, 4), 2)}
    ids = [block_ids] + [over_rep(block_ids, part) for part in range(1, rep_count)]

    before = (jnp.arange(users_here)[:, None] < jnp.arange(users_here)[None, :]).astype(jnp.bfloat16)
    target_dev = owner_rows // users_here
    goes = target_dev[None, :] == jnp.arange(device_count)[:, None]
    goes_rank = dot32(goes.astype(jnp.bfloat16), before).astype(jnp.int32)
    sent = goes[:, None, :] & (goes_rank[:, None, :] == jnp.arange(quota)[None, :, None])
    slots = jnp.sum(jnp.where(sent, (owner_rows % users_here)[None, None, :], 0), axis=2)
    slots = jnp.pad(slots.astype(jnp.float32), ((0, 0), (0, LANES - quota)))[:, None, :]
    place = target_dev * quota + jnp.sum(jnp.where(goes, goes_rank, 0), axis=0)

    gram_rows = width // rep_count
    gram = sum(
        dot32(lax.dynamic_slice(panel, (0, rep * gram_rows), (item_local, gram_rows)), panel, ((0,), (0,)))
        for panel in (item_factors, other_whole.reshape(item_local, width))
    )
    gram = gram + over_blk(gram, lambda b: b ^ 2)
    pieces, gram, ids = after((pieces, gram, ids))
    bit = 4
    while bit < panel_count:
        gram = gram + over_blk(gram, lambda b: b ^ bit)
        bit *= 2
    pieces[0] = piece

    def table_shape(count):
        rows = count * span
        return (
            jax.ShapeDtypeStruct((batch_count, rows, width), jnp.bfloat16),
            jax.ShapeDtypeStruct((batch_count, width, rows), jnp.bfloat16),
        )

    def send_and_join(chosen, count, with_gram=False):
        parts = [chosen[0]] + [over_rep(chosen[part], part) for part in range(1, rep_count)]
        grams = (jax.ShapeDtypeStruct((width, width), jnp.bfloat16),) * 2 * with_gram
        return call(
            functools.partial(join_kernel, rep_count, count, batch_count, per_panel), "join",
            [], parts, table_shape(count) + grams, 1 << 20,
        )

    tables = [call(
        functools.partial(pick_kernel, batch_count, per_panel), "pick",
        [block_ids], [whole, other_whole], table_shape(1), 1 << 20,
    )]

    steps = [k for k in (1, 3, 2) if k < chips] + list(range(4, chips))
    stages = [steps[i:i + 2] for i in range(0, chips - 1, 2)]
    named = batch_count * 2 * per_panel
    chosen = None
    for stage in stages:
        last = stage is stages[-1]
        pairs = []
        for k in stage:
            if k not in pieces:
                source, hop = (3, 1) if k == 2 else (k - 4, 4)
                moving, chosen, gram = after((pieces[source], chosen, gram))
                pieces[k] = over_blk(moving, lambda b: b ^ 2 * hop)
            piece = pieces[k]
            if last:
                piece, tables[0] = after((piece, tables[0]))
            pairs += [piece, other_core(piece)]
        if chosen is not None:
            tables.append(send_and_join(chosen, held))
        count = len(stage) * named + last * (2 * gram_rows // part_rows)
        chosen = call(
            functools.partial(select_kernel, rep_count, stage, batch_count, per_panel), "select",
            ids, pairs + [gram] * last,
            (jax.ShapeDtypeStruct((count, part_rows, width), jnp.bfloat16),) * rep_count, 1 << 20,
        )
        held = len(stage)
    *table, gram_high, gram_low = send_and_join(chosen, held, True)
    tables.append(table)
    rows_list, cols_list = [table[0] for table in tables], [table[1] for table in tables]

    state = pltpu.VMEM((batch_count, batch_rows, width), jnp.float32)
    lanes = quota * width + LANES
    send_rows = call(
        functools.partial(solve_kernel, chips, [0] + steps, block_size, batch_count), "solve",
        [live_counts, place], [ratings, slots, gram_high, gram_low, *rows_list, *cols_list],
        jax.ShapeDtypeStruct((device_count, 1, lanes), jnp.float32),
        12 * 4 * users_here * columns * width,
        [
            pltpu.VMEM((batch_count, batch_rows, columns), jnp.float32),
            state, state, state, pltpu.VMEM((batch_count, batch_rows, 1), jnp.float32),
        ],
    )
    got_rows = lax.all_to_all(send_rows, ("rep", "blk"), split_axis=0, concat_axis=0, tiled=True)
    return call(
        place_kernel, "place", [], [got_rows],
        jax.ShapeDtypeStruct((users_here, width), jnp.float32), 1 << 20,
        [pltpu.SMEM((device_count, 1, LANES), jnp.float32), pltpu.SemaphoreType.DMA],
    )


def solution(mesh):
    placed = (
        P("blk", None),
        P(("rep", "blk"), None),
        P(("rep", "blk"), None),
        P(("rep", "blk")),
        P(("rep", "blk")),
    )
    return jax.shard_map(
        on_device, mesh=mesh, in_specs=placed, out_specs=P(("rep", "blk"), None), check_vma=False
    )
```

```python
import functools
import math
import jax
import jax.numpy as jnp
from jax import lax
from jax.experimental import pallas as pl
from jax.experimental.pallas import tpu as pltpu
from jax.sharding import PartitionSpec as P

ITERS = 8
WIDE_ITERS = 1
TILE = 256
LANES = 128
SPARE_VMEM = 6 * 1024 * 1024

conf_scale = 6.0
ridge_term = 0.5


def dot32(left, right, dims=((1,), (0,))):
    return lax.dot_general(left, right, (dims, ((), ())), preferred_element_type=jnp.float32)


def halves(value):
    high = value.astype(jnp.bfloat16)
    low = (value - high.astype(jnp.float32)).astype(jnp.bfloat16)
    return high, low


def local_slots(core, per_panel):
    for side in range(2):
        parity = core if side == 0 else 1 - core
        for pick in range(per_panel):
            yield side, parity * per_panel + pick


def position(chips, back):
    blk = lax.axis_index("blk")
    return lax.rem(blk, 2), lax.rem(lax.div(blk, 2) + chips - back, chips)


def select_kernel(chips, reps, steps, batch_count, per_panel, *refs):
    ids_refs, refs = refs[:reps], refs[reps:]
    panel_refs, refs = refs[:2 * len(steps)], refs[2 * len(steps):]
    gram_refs = [ref for ref in refs if ref.dtype == jnp.float32]
    out_refs = refs[len(gram_refs):]
    slots = 2 * per_panel
    blocks, size, _ = panel_refs[0].shape
    named = batch_count * slots
    for ids_ref, out_ref in zip(ids_refs, out_refs):
        for i, back in enumerate(steps):
            core, chip = position(chips, back)
            for batch in range(batch_count):
                for side, local in local_slots(core, per_panel):
                    block = ids_ref[batch, chip * slots + local]
                    out_ref[i * named + batch * slots + local] = panel_refs[2 * i + side][lax.rem(block, blocks)]
        for gram_ref in gram_refs:
            gram = jnp.concatenate(halves(gram_ref[...]), axis=0)
            out_ref[len(steps) * named:] = gram.reshape(-1, size, gram.shape[1])


def join_kernel(reps, steps, batch_count, per_panel, *refs):
    part_refs, (rows_ref, cols_ref, *gram_refs) = refs[:reps], refs[reps:]
    rep = lax.axis_index("rep")
    size = part_refs[0].shape[1]
    slots = 2 * per_panel
    named = batch_count * slots
    for part, ref in enumerate(part_refs):
        for i in range(len(steps)):
            for batch in range(batch_count):
                for local in range(slots):
                    offset = (i * slots + local) * reps * size + (rep ^ part) * size
                    rows_ref[batch, pl.ds(pl.multiple_of(offset, size), size), :] = ref[
                        i * named + batch * slots + local
                    ]
        extra = ref.shape[0] - len(steps) * named
        half = extra // 2
        for i, gram_ref in enumerate(gram_refs):
            start = len(steps) * named + i * half
            offset = pl.multiple_of((rep ^ part) * size * half, size * half)
            gram_ref[pl.ds(offset, size * half), :] = ref[start:start + half].reshape(size * half, ref.shape[2])
    for batch in range(batch_count):
        cols_ref[batch] = rows_ref[batch].T


def pick_kernel(chips, batch_count, per_panel, ids_ref, own_ref, other_ref, rows_ref, cols_ref):
    core, chip = position(chips, 0)
    slots = 2 * per_panel
    blocks, block_size, _ = own_ref.shape
    for batch in range(batch_count):
        for side, local in local_slots(core, per_panel):
            block = ids_ref[batch, chip * slots + local]
            held = other_ref if side else own_ref
            offset = pl.multiple_of(local * block_size, block_size)
            rows_ref[batch, pl.ds(offset, block_size), :] = held[lax.rem(block, blocks)]
        cols_ref[batch] = rows_ref[batch].T


def solve_kernel(chips, steps, block_size, batch_count, *refs):
    live_ref, place_ref, ratings_ref, slots_ref, gram_high, gram_low = refs[:6]
    refs = refs[6:]
    tables = (len(refs) - 7) // 2
    rows_refs, cols_refs, refs = refs[:tables], refs[tables:2 * tables], refs[2 * tables:]
    send_ref, weight, back, x_s, r_s, p_s, n_s = refs
    users = ratings_ref.shape[0] // batch_count
    span = ratings_ref.shape[1] // chips
    batches = range(batch_count)
    tiles, starts = [], []
    for table, ref in enumerate(rows_refs):
        start = sum(other.shape[1] for other in rows_refs[:table])
        starts.append(start)
        tiles += [(table, first, start + first) for first in range(0, ref.shape[1], TILE)]

    def back_dot(batch, rows):
        total = None
        for table, start in enumerate(starts):
            size = rows_refs[table].shape[1]
            term = dot32(back[batch, :rows, start:start + size], rows_refs[table][batch])
            total = term if total is None else total + term
        return total

    def put_halves(batch, column, value):
        high, low = halves(value)
        back[batch, :users, column:column + TILE] = high
        back[batch, users:, column:column + TILE] = low

    for _, _, column in tiles:
        _, chip = position(chips, steps[column // span])
        start = pl.multiple_of(chip * span + column % span, TILE)
        index = start + lax.broadcasted_iota(jnp.int32, (users, TILE), 1)
        for batch in batches:
            rated = ratings_ref[batch * users:(batch + 1) * users, pl.ds(start, TILE)].astype(jnp.float32)
            live = index < live_ref[batch] * block_size
            scaled = jnp.where(live, conf_scale * rated, 0.0)
            weight[batch, :, column:column + TILE] = scaled
            put_halves(batch, column, jnp.where(live, 1.0 + scaled, 0.0))
    for batch in batches:
        total = back_dot(batch, 2 * users)
        target_proj = total[:users] + total[users:]
        x_s[batch] = jnp.zeros_like(target_proj)
        r_s[batch] = target_proj
        p_s[batch] = target_proj
        n_s[batch] = jnp.sum(target_proj * target_proj, axis=1, keepdims=True)

    def step(wide):
        def body(_, carry):
            highs, boths = [], []
            for batch in batches:
                high, low = halves(p_s[batch])
                highs.append(high)
                boths.append(jnp.concatenate([high, low], axis=0))
            for table, first, column in tiles:
                for batch in batches:
                    moving = boths[batch] if wide else highs[batch]
                    projected = dot32(moving, cols_refs[table][batch, :, first:first + TILE])
                    if wide:
                        projected = projected[:users] + projected[users:]
                    projected = projected * weight[batch, :, column:column + TILE]
                    if wide:
                        put_halves(batch, column, projected)
                    else:
                        back[batch, :users, column:column + TILE] = projected.astype(jnp.bfloat16)
            for batch in batches:
                total = back_dot(batch, 2 * users if wide else users)
                if wide:
                    total = total[:users] + total[users:]
                direction = p_s[batch]
                gram_part = dot32(boths[batch], gram_high[...])
                image = (
                    gram_part[:users] + gram_part[users:] + dot32(highs[batch], gram_low[...])
                    + total + ridge_term * direction
                )
                norm_now = n_s[batch]
                step_size = norm_now / jnp.sum(direction * image, axis=1, keepdims=True)
                x_s[batch] = x_s[batch] + step_size * direction
                residual = r_s[batch] - step_size * image
                r_s[batch] = residual
                norm_next = jnp.sum(residual * residual, axis=1, keepdims=True)
                p_s[batch] = residual + norm_next / norm_now * direction
                n_s[batch] = norm_next
            return carry

        return body

    lax.fori_loop(0, WIDE_ITERS, step(True), 0)
    lax.fori_loop(WIDE_ITERS, ITERS, step(False), 0)
    width = x_s.shape[2]
    quota = batch_count * users // send_ref.shape[0]
    send_ref[:, :, quota * width:] = slots_ref[...]
    for batch in batches:
        for user in range(users):
            place = place_ref[batch * users + user]
            lanes = pl.ds(pl.multiple_of(lax.rem(place, quota) * width, width), width)
            send_ref[lax.div(place, quota), :, lanes] = x_s[batch, user:user + 1, :]


def place_kernel(got_ref, out_ref, slots, sem):
    width = out_ref.shape[1]
    quota = out_ref.shape[0] // got_ref.shape[0]
    copy = pltpu.make_async_copy(got_ref.at[:, :, pl.ds(quota * width, LANES)], slots, sem)
    copy.start()
    copy.wait()
    for source in range(got_ref.shape[0]):
        for row in range(quota):
            slot = slots[source, 0, row].astype(jnp.int32)
            out_ref[pl.ds(slot, 1), :] = got_ref[source, :, row * width:(row + 1) * width]


def smem():
    return pl.BlockSpec(memory_space=pltpu.SMEM)


def vmem():
    return pl.BlockSpec(memory_space=pltpu.VMEM)


def call(body, name, small, large, out_shape, flops, scratch=()):
    operands = (*small, *large)
    moved = sum(array.size * array.dtype.itemsize for array in (*operands, *jax.tree.leaves(out_shape)))
    kept = sum(math.prod(array.shape) * 4 for array in scratch if hasattr(array, "shape"))
    return pl.pallas_call(
        body,
        out_shape=out_shape,
        in_specs=[smem()] * len(small) + [vmem()] * len(large),
        out_specs=jax.tree.map(lambda _: vmem(), out_shape),
        scratch_shapes=list(scratch),
        compiler_params=pltpu.CompilerParams(vmem_limit_bytes=moved + kept + SPARE_VMEM),
        cost_estimate=pl.CostEstimate(flops=flops, bytes_accessed=moved, transcendentals=0),
        name=name,
    )(*operands)


def on_device(item_factors, ratings, block_ids, live_counts, owner_rows):
    item_local, width = item_factors.shape
    users_here, columns = ratings.shape
    batch_count, slot_count = block_ids.shape
    batch_rows = users_here // batch_count
    block_size = columns // slot_count
    panel_count = lax.axis_size("blk")
    rep_count = lax.axis_size("rep")
    device_count = rep_count * panel_count
    quota = users_here // device_count
    chips = panel_count // 2
    per_panel = slot_count // panel_count
    blocks = item_local // block_size
    part_rows = block_size // rep_count
    span = 2 * per_panel * block_size
    rep = lax.axis_index("rep")

    def over_blk(array, target):
        return lax.ppermute(array, "blk", [(b, target(b)) for b in range(panel_count)])

    def over_rep(array, part):
        return lax.ppermute(array, "rep", [(r, r ^ part) for r in range(rep_count)])

    def other_core(array):
        return over_blk(array, lambda b: b ^ 1)

    whole = item_factors.reshape(blocks, block_size, width)
    piece = lax.dynamic_slice(whole, (0, rep * part_rows, 0), (blocks, part_rows, width))

    after = lax.optimization_barrier
    other_whole = other_core(whole)
    pieces = {0: piece}
    turn = chips // 2
    for k in range(1, turn + 1):
        pieces[k] = over_blk(pieces[k - 1], lambda b: (b + 2) % panel_count)
        if k < chips - k:
            pieces[chips - k] = over_blk(pieces[(chips - k + 1) % chips], lambda b: (b - 2) % panel_count)
    ids = [block_ids] + [over_rep(block_ids, part) for part in range(1, rep_count)]

    before = (jnp.arange(users_here)[:, None] < jnp.arange(users_here)[None, :]).astype(jnp.bfloat16)
    target_dev = owner_rows // users_here
    goes = target_dev[None, :] == jnp.arange(device_count)[:, None]
    goes_rank = dot32(goes.astype(jnp.bfloat16), before).astype(jnp.int32)
    sent = goes[:, None, :] & (goes_rank[:, None, :] == jnp.arange(quota)[None, :, None])
    slots = jnp.sum(jnp.where(sent, (owner_rows % users_here)[None, None, :], 0), axis=2)
    slots = jnp.pad(slots.astype(jnp.float32), ((0, 0), (0, LANES - quota)))[:, None, :]
    place = target_dev * quota + jnp.sum(jnp.where(goes, goes_rank, 0), axis=0)

    gram_rows = width // rep_count
    gram = sum(
        dot32(lax.dynamic_slice(panel, (0, rep * gram_rows), (item_local, gram_rows)), panel, ((0,), (0,)))
        for panel in (item_factors, other_whole.reshape(item_local, width))
    )
    gram = gram + over_blk(gram, lambda b: b ^ 2)

    def table_shape(steps):
        rows = len(steps) * span
        return (
            jax.ShapeDtypeStruct((batch_count, rows, width), jnp.bfloat16),
            jax.ShapeDtypeStruct((batch_count, width, rows), jnp.bfloat16),
        )

    tables = [call(
        functools.partial(pick_kernel, chips, batch_count, per_panel), "pick",
        [block_ids], [whole, other_whole], table_shape([0]), 1 << 20,
    )]

    near_first = sorted(range(1, chips), key=lambda k: min(k, chips - k))
    stages = [near_first[i:i + 2] for i in range(0, chips - 1, 2)]
    chosen = None
    for steps in stages:
        pairs = []
        for k in steps:
            piece = pieces[k]
            if chosen is not None:
                piece, chosen, tables[0], gram = after((piece, chosen, tables[0], gram))
            pairs += [piece, other_core(piece)]
        if chosen is not None:
            parts = [chosen[0]] + [over_rep(chosen[part], part) for part in range(1, rep_count)]
            tables.append(call(
                functools.partial(join_kernel, rep_count, held, batch_count, per_panel), "join",
                [], parts, table_shape(held), 1 << 20,
            ))
        last = steps is stages[-1]
        bit = 4
        while last and bit < panel_count:
            gram = gram + over_blk(gram, lambda b: b ^ bit)
            bit *= 2
        count = len(steps) * batch_count * 2 * per_panel + last * (2 * gram_rows // part_rows)
        picked = jax.ShapeDtypeStruct((count, part_rows, width), jnp.bfloat16)
        chosen = call(
            functools.partial(select_kernel, chips, rep_count, steps, batch_count, per_panel), "select",
            ids, pairs + [gram] * last, (picked,) * rep_count, 1 << 20,
        )
        held = steps
    parts = [chosen[0]] + [over_rep(chosen[part], part) for part in range(1, rep_count)]
    grams = (jax.ShapeDtypeStruct((width, width), jnp.bfloat16),) * 2
    *table, gram_high, gram_low = call(
        functools.partial(join_kernel, rep_count, held, batch_count, per_panel), "join",
        [], parts, table_shape(held) + grams, 1 << 20,
    )
    tables.append(table)
    rows_list, cols_list = [table[0] for table in tables], [table[1] for table in tables]

    state = pltpu.VMEM((batch_count, batch_rows, width), jnp.float32)
    lanes = quota * width + LANES
    send_rows = call(
        functools.partial(solve_kernel, chips, [0] + near_first, block_size, batch_count), "solve",
        [live_counts, place], [ratings, slots, gram_high, gram_low, *rows_list, *cols_list],
        jax.ShapeDtypeStruct((device_count, 1, lanes), jnp.float32),
        12 * 4 * users_here * columns * width,
        [
            pltpu.VMEM((batch_count, batch_rows, columns), jnp.float32),
            pltpu.VMEM((batch_count, 2 * batch_rows, columns), jnp.bfloat16),
            state, state, state, pltpu.VMEM((batch_count, batch_rows, 1), jnp.float32),
        ],
    )
    got_rows = lax.all_to_all(send_rows, ("rep", "blk"), split_axis=0, concat_axis=0, tiled=True)
    return call(
        place_kernel, "place", [], [got_rows],
        jax.ShapeDtypeStruct((users_here, width), jnp.float32), 1 << 20,
        [pltpu.SMEM((device_count, 1, LANES), jnp.float32), pltpu.SemaphoreType.DMA],
    )


def solution(mesh):
    placed = (
        P("blk", None),
        P(("rep", "blk"), None),
        P(("rep", "blk"), None),
        P(("rep", "blk")),
        P(("rep", "blk")),
    )
    return jax.shard_map(
        on_device, mesh=mesh, in_specs=placed, out_specs=P(("rep", "blk"), None), check_vma=False
    )
```

```python
import functools
import math
import jax
import jax.numpy as jnp
from jax import lax
from jax.experimental import pallas as pl
from jax.experimental.pallas import tpu as pltpu
from jax.sharding import PartitionSpec as P

ITERS = 8
WIDE_ITERS = 1
TILE = 256
LANES = 128
SPARE_VMEM = 6 * 1024 * 1024

conf_scale = 6.0
ridge_term = 0.5


def dot32(left, right, dims=((1,), (0,))):
    return lax.dot_general(left, right, (dims, ((), ())), preferred_element_type=jnp.float32)


def halves(value):
    high = value.astype(jnp.bfloat16)
    low = (value - high.astype(jnp.float32)).astype(jnp.bfloat16)
    return high, low


def local_slots(core, per_panel):
    for side in range(2):
        parity = core if side == 0 else 1 - core
        for pick in range(per_panel):
            yield side, parity * per_panel + pick


def position(chips, back):
    blk = lax.axis_index("blk")
    return lax.rem(blk, 2), lax.rem(lax.div(blk, 2) + chips - back, chips)


def select_kernel(chips, reps, steps, batch_count, per_panel, *refs):
    ids_refs, refs = refs[:reps], refs[reps:]
    panel_refs, refs = refs[:2 * len(steps)], refs[2 * len(steps):]
    gram_refs = [ref for ref in refs if ref.dtype == jnp.float32]
    out_refs = refs[len(gram_refs):]
    slots = 2 * per_panel
    blocks, size, _ = panel_refs[0].shape
    named = batch_count * slots
    for ids_ref, out_ref in zip(ids_refs, out_refs):
        for i, back in enumerate(steps):
            core, chip = position(chips, back)
            for batch in range(batch_count):
                for side, local in local_slots(core, per_panel):
                    block = ids_ref[batch, chip * slots + local]
                    out_ref[i * named + batch * slots + local] = panel_refs[2 * i + side][lax.rem(block, blocks)]
        for gram_ref in gram_refs:
            gram = jnp.concatenate(halves(gram_ref[...]), axis=0)
            out_ref[len(steps) * named:] = gram.reshape(-1, size, gram.shape[1])


def join_kernel(reps, steps, batch_count, per_panel, *refs):
    part_refs, (rows_ref, cols_ref, *gram_refs) = refs[:reps], refs[reps:]
    rep = lax.axis_index("rep")
    size = part_refs[0].shape[1]
    slots = 2 * per_panel
    named = batch_count * slots
    for part, ref in enumerate(part_refs):
        for i in range(len(steps)):
            for batch in range(batch_count):
                for local in range(slots):
                    offset = (i * slots + local) * reps * size + (rep ^ part) * size
                    rows_ref[batch, pl.ds(pl.multiple_of(offset, size), size), :] = ref[
                        i * named + batch * slots + local
                    ]
        extra = ref.shape[0] - len(steps) * named
        half = extra // 2
        for i, gram_ref in enumerate(gram_refs):
            start = len(steps) * named + i * half
            offset = pl.multiple_of((rep ^ part) * size * half, size * half)
            gram_ref[pl.ds(offset, size * half), :] = ref[start:start + half].reshape(size * half, ref.shape[2])
    for batch in range(batch_count):
        cols_ref[batch] = rows_ref[batch].T


def pick_kernel(chips, batch_count, per_panel, ids_ref, own_ref, other_ref, rows_ref, cols_ref):
    core, chip = position(chips, 0)
    slots = 2 * per_panel
    blocks, block_size, _ = own_ref.shape
    for batch in range(batch_count):
        for side, local in local_slots(core, per_panel):
            block = ids_ref[batch, chip * slots + local]
            held = other_ref if side else own_ref
            offset = pl.multiple_of(local * block_size, block_size)
            rows_ref[batch, pl.ds(offset, block_size), :] = held[lax.rem(block, blocks)]
        cols_ref[batch] = rows_ref[batch].T


def solve_kernel(chips, steps, block_size, batch_count, *refs):
    live_ref, place_ref, ratings_ref, slots_ref, gram_high, gram_low = refs[:6]
    refs = refs[6:]
    tables = (len(refs) - 7) // 2
    rows_refs, cols_refs, refs = refs[:tables], refs[tables:2 * tables], refs[2 * tables:]
    send_ref, weight, back, x_s, r_s, p_s, n_s = refs
    users = ratings_ref.shape[0] // batch_count
    span = ratings_ref.shape[1] // chips
    batches = range(batch_count)
    tiles, starts = [], []
    for table, ref in enumerate(rows_refs):
        start = sum(other.shape[1] for other in rows_refs[:table])
        starts.append(start)
        tiles += [(table, first, start + first) for first in range(0, ref.shape[1], TILE)]

    def back_dot(batch, rows):
        total = None
        for table, start in enumerate(starts):
            size = rows_refs[table].shape[1]
            term = dot32(back[batch, :rows, start:start + size], rows_refs[table][batch])
            total = term if total is None else total + term
        return total

    def put_halves(batch, column, value):
        high, low = halves(value)
        back[batch, :users, column:column + TILE] = high
        back[batch, users:, column:column + TILE] = low

    for _, _, column in tiles:
        _, chip = position(chips, steps[column // span])
        start = pl.multiple_of(chip * span + column % span, TILE)
        index = start + lax.broadcasted_iota(jnp.int32, (users, TILE), 1)
        for batch in batches:
            rated = ratings_ref[batch * users:(batch + 1) * users, pl.ds(start, TILE)].astype(jnp.float32)
            live = index < live_ref[batch] * block_size
            scaled = jnp.where(live, conf_scale * rated, 0.0)
            weight[batch, :, column:column + TILE] = scaled
            put_halves(batch, column, jnp.where(live, 1.0 + scaled, 0.0))
    for batch in batches:
        total = back_dot(batch, 2 * users)
        target_proj = total[:users] + total[users:]
        x_s[batch] = jnp.zeros_like(target_proj)
        r_s[batch] = target_proj
        p_s[batch] = target_proj
        n_s[batch] = jnp.sum(target_proj * target_proj, axis=1, keepdims=True)

    def advance(batch, wide):
        direction = p_s[batch]
        high, low = halves(direction)
        both = jnp.concatenate([high, low], axis=0)
        for table, first, column in tiles:
            projected = dot32(both if wide else high, cols_refs[table][batch, :, first:first + TILE])
            if wide:
                projected = projected[:users] + projected[users:]
            projected = projected * weight[batch, :, column:column + TILE]
            if wide:
                put_halves(batch, column, projected)
            else:
                back[batch, :users, column:column + TILE] = projected.astype(jnp.bfloat16)
        gram_part = dot32(both, gram_high[...])
        image = gram_part[:users] + gram_part[users:] + dot32(high, gram_low[...]) + ridge_term * direction
        total = back_dot(batch, 2 * users if wide else users)
        if wide:
            total = total[:users] + total[users:]
        image = image + total
        norm_now = n_s[batch]
        step_size = norm_now / jnp.sum(direction * image, axis=1, keepdims=True)
        x_s[batch] = x_s[batch] + step_size * direction
        residual = r_s[batch] - step_size * image
        r_s[batch] = residual
        norm_next = jnp.sum(residual * residual, axis=1, keepdims=True)
        p_s[batch] = residual + norm_next / norm_now * direction
        n_s[batch] = norm_next

    for iteration in range(ITERS):
        for batch in batches:
            advance(batch, iteration < WIDE_ITERS)
    width = x_s.shape[2]
    quota = batch_count * users // send_ref.shape[0]
    send_ref[:, :, quota * width:] = slots_ref[...]
    for batch in batches:
        for user in range(users):
            place = place_ref[batch * users + user]
            lanes = pl.ds(pl.multiple_of(lax.rem(place, quota) * width, width), width)
            send_ref[lax.div(place, quota), :, lanes] = x_s[batch, user:user + 1, :]


def place_kernel(got_ref, out_ref, slots, sem):
    width = out_ref.shape[1]
    quota = out_ref.shape[0] // got_ref.shape[0]
    copy = pltpu.make_async_copy(got_ref.at[:, :, pl.ds(quota * width, LANES)], slots, sem)
    copy.start()
    copy.wait()
    for source in range(got_ref.shape[0]):
        for row in range(quota):
            slot = slots[source, 0, row].astype(jnp.int32)
            out_ref[pl.ds(slot, 1), :] = got_ref[source, :, row * width:(row + 1) * width]


def smem():
    return pl.BlockSpec(memory_space=pltpu.SMEM)


def vmem():
    return pl.BlockSpec(memory_space=pltpu.VMEM)


def call(body, name, small, large, out_shape, flops, scratch=()):
    operands = (*small, *large)
    moved = sum(array.size * array.dtype.itemsize for array in (*operands, *jax.tree.leaves(out_shape)))
    kept = sum(math.prod(array.shape) * 4 for array in scratch if hasattr(array, "shape"))
    return pl.pallas_call(
        body,
        out_shape=out_shape,
        in_specs=[smem()] * len(small) + [vmem()] * len(large),
        out_specs=jax.tree.map(lambda _: vmem(), out_shape),
        scratch_shapes=list(scratch),
        compiler_params=pltpu.CompilerParams(vmem_limit_bytes=moved + kept + SPARE_VMEM),
        cost_estimate=pl.CostEstimate(flops=flops, bytes_accessed=moved, transcendentals=0),
        name=name,
    )(*operands)


def on_device(item_factors, ratings, block_ids, live_counts, owner_rows):
    item_local, width = item_factors.shape
    users_here, columns = ratings.shape
    batch_count, slot_count = block_ids.shape
    batch_rows = users_here // batch_count
    block_size = columns // slot_count
    panel_count = lax.axis_size("blk")
    rep_count = lax.axis_size("rep")
    device_count = rep_count * panel_count
    quota = users_here // device_count
    chips = panel_count // 2
    per_panel = slot_count // panel_count
    blocks = item_local // block_size
    part_rows = block_size // rep_count
    span = 2 * per_panel * block_size
    rep = lax.axis_index("rep")

    def over_blk(array, target):
        return lax.ppermute(array, "blk", [(b, target(b)) for b in range(panel_count)])

    def over_rep(array, part):
        return lax.ppermute(array, "rep", [(r, r ^ part) for r in range(rep_count)])

    def other_core(array):
        return over_blk(array, lambda b: b ^ 1)

    whole = item_factors.reshape(blocks, block_size, width)
    piece = lax.dynamic_slice(whole, (0, rep * part_rows, 0), (blocks, part_rows, width))

    after = lax.optimization_barrier
    other_whole = other_core(whole)
    pieces = {0: piece}
    turn = chips // 2
    for k in range(1, turn + 1):
        pieces[k] = over_blk(pieces[k - 1], lambda b: (b + 2) % panel_count)
        if k < chips - k:
            pieces[chips - k] = over_blk(pieces[(chips - k + 1) % chips], lambda b: (b - 2) % panel_count)
    ids = [block_ids] + [over_rep(block_ids, part) for part in range(1, rep_count)]

    before = (jnp.arange(users_here)[:, None] < jnp.arange(users_here)[None, :]).astype(jnp.bfloat16)
    target_dev = owner_rows // users_here
    goes = target_dev[None, :] == jnp.arange(device_count)[:, None]
    goes_rank = dot32(goes.astype(jnp.bfloat16), before).astype(jnp.int32)
    sent = goes[:, None, :] & (goes_rank[:, None, :] == jnp.arange(quota)[None, :, None])
    slots = jnp.sum(jnp.where(sent, (owner_rows % users_here)[None, None, :], 0), axis=2)
    slots = jnp.pad(slots.astype(jnp.float32), ((0, 0), (0, LANES - quota)))[:, None, :]
    place = target_dev * quota + jnp.sum(jnp.where(goes, goes_rank, 0), axis=0)

    gram_rows = width // rep_count
    gram = sum(
        dot32(lax.dynamic_slice(panel, (0, rep * gram_rows), (item_local, gram_rows)), panel, ((0,), (0,)))
        for panel in (item_factors, other_whole.reshape(item_local, width))
    )
    gram = gram + over_blk(gram, lambda b: b ^ 2)

    def table_shape(steps):
        rows = len(steps) * span
        return (
            jax.ShapeDtypeStruct((batch_count, rows, width), jnp.bfloat16),
            jax.ShapeDtypeStruct((batch_count, width, rows), jnp.bfloat16),
        )

    tables = [call(
        functools.partial(pick_kernel, chips, batch_count, per_panel), "pick",
        [block_ids], [whole, other_whole], table_shape([0]), 1 << 20,
    )]

    near_first = sorted(range(1, chips), key=lambda k: min(k, chips - k))
    stages = [near_first[i:i + 2] for i in range(0, chips - 1, 2)]
    chosen = None
    for steps in stages:
        pairs = []
        for k in steps:
            piece = pieces[k]
            if chosen is not None:
                piece, chosen, tables[0], gram = after((piece, chosen, tables[0], gram))
            pairs += [piece, other_core(piece)]
        if chosen is not None:
            parts = [chosen[0]] + [over_rep(chosen[part], part) for part in range(1, rep_count)]
            tables.append(call(
                functools.partial(join_kernel, rep_count, held, batch_count, per_panel), "join",
                [], parts, table_shape(held), 1 << 20,
            ))
        last = steps is stages[-1]
        bit = 4
        while last and bit < panel_count:
            gram = gram + over_blk(gram, lambda b: b ^ bit)
            bit *= 2
        count = len(steps) * batch_count * 2 * per_panel + last * (2 * gram_rows // part_rows)
        picked = jax.ShapeDtypeStruct((count, part_rows, width), jnp.bfloat16)
        chosen = call(
            functools.partial(select_kernel, chips, rep_count, steps, batch_count, per_panel), "select",
            ids, pairs + [gram] * last, (picked,) * rep_count, 1 << 20,
        )
        held = steps
    parts = [chosen[0]] + [over_rep(chosen[part], part) for part in range(1, rep_count)]
    grams = (jax.ShapeDtypeStruct((width, width), jnp.bfloat16),) * 2
    *table, gram_high, gram_low = call(
        functools.partial(join_kernel, rep_count, held, batch_count, per_panel), "join",
        [], parts, table_shape(held) + grams, 1 << 20,
    )
    tables.append(table)
    rows_list, cols_list = [table[0] for table in tables], [table[1] for table in tables]

    state = pltpu.VMEM((batch_count, batch_rows, width), jnp.float32)
    lanes = quota * width + LANES
    send_rows = call(
        functools.partial(solve_kernel, chips, [0] + near_first, block_size, batch_count), "solve",
        [live_counts, place], [ratings, slots, gram_high, gram_low, *rows_list, *cols_list],
        jax.ShapeDtypeStruct((device_count, 1, lanes), jnp.float32),
        12 * 4 * users_here * columns * width,
        [
            pltpu.VMEM((batch_count, batch_rows, columns), jnp.float32),
            pltpu.VMEM((batch_count, 2 * batch_rows, columns), jnp.bfloat16),
            state, state, state, pltpu.VMEM((batch_count, batch_rows, 1), jnp.float32),
        ],
    )
    got_rows = lax.all_to_all(send_rows, ("rep", "blk"), split_axis=0, concat_axis=0, tiled=True)
    return call(
        place_kernel, "place", [], [got_rows],
        jax.ShapeDtypeStruct((users_here, width), jnp.float32), 1 << 20,
        [pltpu.SMEM((device_count, 1, LANES), jnp.float32), pltpu.SemaphoreType.DMA],
    )


def solution(mesh):
    placed = (
        P("blk", None),
        P(("rep", "blk"), None),
        P(("rep", "blk"), None),
        P(("rep", "blk")),
        P(("rep", "blk")),
    )
    return jax.shard_map(
        on_device, mesh=mesh, in_specs=placed, out_specs=P(("rep", "blk"), None), check_vma=False
    )
```

```python
import functools
import math
import jax
import jax.numpy as jnp
from jax import lax
from jax.experimental import pallas as pl
from jax.experimental.pallas import tpu as pltpu
from jax.sharding import PartitionSpec as P

ITERS = 8
WIDE_ITERS = 1
TILE = 256
LANES = 128
SPARE_VMEM = 6 * 1024 * 1024

conf_scale = 6.0
ridge_term = 0.5


def dot32(left, right, dims=((1,), (0,))):
    return lax.dot_general(left, right, (dims, ((), ())), preferred_element_type=jnp.float32)


def halves(value):
    high = value.astype(jnp.bfloat16)
    low = (value - high.astype(jnp.float32)).astype(jnp.bfloat16)
    return high, low


def local_slots(core, per_panel):
    for side in range(2):
        parity = core if side == 0 else 1 - core
        for pick in range(per_panel):
            yield side, parity * per_panel + pick


def position(chips, back):
    blk = lax.axis_index("blk")
    return lax.rem(blk, 2), lax.rem(lax.div(blk, 2) + chips - back, chips)


def select_kernel(chips, reps, steps, batch_count, per_panel, *refs):
    ids_refs, refs = refs[:reps], refs[reps:]
    panel_refs, refs = refs[:2 * len(steps)], refs[2 * len(steps):]
    gram_refs = [ref for ref in refs if ref.dtype == jnp.float32]
    out_refs = refs[len(gram_refs):]
    slots = 2 * per_panel
    blocks, size, _ = panel_refs[0].shape
    named = batch_count * slots
    for ids_ref, out_ref in zip(ids_refs, out_refs):
        for i, back in enumerate(steps):
            core, chip = position(chips, back)
            for batch in range(batch_count):
                for side, local in local_slots(core, per_panel):
                    block = ids_ref[batch, chip * slots + local]
                    out_ref[i * named + batch * slots + local] = panel_refs[2 * i + side][lax.rem(block, blocks)]
        for gram_ref in gram_refs:
            gram = jnp.concatenate(halves(gram_ref[...]), axis=0)
            out_ref[len(steps) * named:] = gram.reshape(-1, size, gram.shape[1])


def join_kernel(reps, steps, batch_count, per_panel, *refs):
    part_refs, (rows_ref, cols_ref, *gram_refs) = refs[:reps], refs[reps:]
    rep = lax.axis_index("rep")
    size = part_refs[0].shape[1]
    slots = 2 * per_panel
    named = batch_count * slots
    for part, ref in enumerate(part_refs):
        for i in range(len(steps)):
            for batch in range(batch_count):
                for local in range(slots):
                    offset = (i * slots + local) * reps * size + (rep ^ part) * size
                    rows_ref[batch, pl.ds(pl.multiple_of(offset, size), size), :] = ref[
                        i * named + batch * slots + local
                    ]
        extra = ref.shape[0] - len(steps) * named
        half = extra // 2
        for i, gram_ref in enumerate(gram_refs):
            start = len(steps) * named + i * half
            offset = pl.multiple_of((rep ^ part) * size * half, size * half)
            gram_ref[pl.ds(offset, size * half), :] = ref[start:start + half].reshape(size * half, ref.shape[2])
    for batch in range(batch_count):
        cols_ref[batch] = rows_ref[batch].T


def pick_kernel(chips, batch_count, per_panel, ids_ref, own_ref, other_ref, rows_ref, cols_ref):
    core, chip = position(chips, 0)
    slots = 2 * per_panel
    blocks, block_size, _ = own_ref.shape
    for batch in range(batch_count):
        for side, local in local_slots(core, per_panel):
            block = ids_ref[batch, chip * slots + local]
            held = other_ref if side else own_ref
            offset = pl.multiple_of(local * block_size, block_size)
            rows_ref[batch, pl.ds(offset, block_size), :] = held[lax.rem(block, blocks)]
        cols_ref[batch] = rows_ref[batch].T


def weigh_kernel(chips, steps, block_size, batch_count, *refs):
    live_ref, ratings_ref = refs[:2]
    rows_refs, (weight, last, partial, early) = refs[2:-4], refs[-4:]
    users = ratings_ref.shape[0] // batch_count
    columns = ratings_ref.shape[1]
    span = columns // chips
    first_last = columns - last.shape[2]
    for column in range(0, columns, TILE):
        _, chip = position(chips, steps[column // span])
        start = pl.multiple_of(chip * span + column % span, TILE)
        index = start + lax.broadcasted_iota(jnp.int32, (users, TILE), 1)
        for batch in range(batch_count):
            rated = ratings_ref[batch * users:(batch + 1) * users, pl.ds(start, TILE)].astype(jnp.float32)
            live = index < live_ref[batch] * block_size
            scaled = jnp.where(live, conf_scale * rated, 0.0)
            weight[batch, :, column:column + TILE] = scaled
            high, low = halves(jnp.where(live, 1.0 + scaled, 0.0))
            target, at = (early, column) if column < first_last else (last, column - first_last)
            target[batch, :users, at:at + TILE] = high
            target[batch, users:, at:at + TILE] = low
    for batch in range(batch_count):
        total, start = None, 0
        for ref in rows_refs:
            term = dot32(early[batch, :, start:start + ref.shape[1]], ref[batch])
            total = term if total is None else total + term
            start += ref.shape[1]
        partial[batch] = total[:users] + total[users:]


def solve_kernel(users, batch_count, *refs):
    place_ref, slots_ref, gram_high, gram_low, weight, last, partial = refs[:7]
    refs = refs[7:]
    tables = (len(refs) - 6) // 2
    rows_refs, cols_refs, refs = refs[:tables], refs[tables:2 * tables], refs[2 * tables:]
    send_ref, back, x_s, r_s, p_s, n_s = refs
    batches = range(batch_count)
    tiles, starts = [], []
    for table, ref in enumerate(rows_refs):
        start = sum(other.shape[1] for other in rows_refs[:table])
        starts.append(start)
        tiles += [(table, first, start + first) for first in range(0, ref.shape[1], TILE)]

    def back_dot(batch, rows):
        total = None
        for table, start in enumerate(starts):
            size = rows_refs[table].shape[1]
            term = dot32(back[batch, :rows, start:start + size], rows_refs[table][batch])
            total = term if total is None else total + term
        return total

    def put_halves(batch, column, value):
        high, low = halves(value)
        back[batch, :users, column:column + TILE] = high
        back[batch, users:, column:column + TILE] = low

    for batch in batches:
        total = dot32(last[batch], rows_refs[-1][batch])
        target_proj = partial[batch] + total[:users] + total[users:]
        x_s[batch] = jnp.zeros_like(target_proj)
        r_s[batch] = target_proj
        p_s[batch] = target_proj
        n_s[batch] = jnp.sum(target_proj * target_proj, axis=1, keepdims=True)

    def advance(batch, wide):
        direction = p_s[batch]
        high, low = halves(direction)
        both = jnp.concatenate([high, low], axis=0)
        for table, first, column in tiles:
            projected = dot32(both if wide else high, cols_refs[table][batch, :, first:first + TILE])
            if wide:
                projected = projected[:users] + projected[users:]
            projected = projected * weight[batch, :, column:column + TILE]
            if wide:
                put_halves(batch, column, projected)
            else:
                back[batch, :users, column:column + TILE] = projected.astype(jnp.bfloat16)
        gram_part = dot32(both, gram_high[...])
        image = gram_part[:users] + gram_part[users:] + dot32(high, gram_low[...]) + ridge_term * direction
        total = back_dot(batch, 2 * users if wide else users)
        if wide:
            total = total[:users] + total[users:]
        image = image + total
        norm_now = n_s[batch]
        step_size = norm_now / jnp.sum(direction * image, axis=1, keepdims=True)
        x_s[batch] = x_s[batch] + step_size * direction
        residual = r_s[batch] - step_size * image
        r_s[batch] = residual
        norm_next = jnp.sum(residual * residual, axis=1, keepdims=True)
        p_s[batch] = residual + norm_next / norm_now * direction
        n_s[batch] = norm_next

    for iteration in range(ITERS):
        for batch in batches:
            advance(batch, iteration < WIDE_ITERS)
    width = x_s.shape[2]
    quota = batch_count * users // send_ref.shape[0]
    send_ref[:, :, quota * width:] = slots_ref[...]
    for batch in batches:
        for user in range(users):
            place = place_ref[batch * users + user]
            lanes = pl.ds(pl.multiple_of(lax.rem(place, quota) * width, width), width)
            send_ref[lax.div(place, quota), :, lanes] = x_s[batch, user:user + 1, :]


def place_kernel(got_ref, out_ref, slots, sem):
    width = out_ref.shape[1]
    quota = out_ref.shape[0] // got_ref.shape[0]
    copy = pltpu.make_async_copy(got_ref.at[:, :, pl.ds(quota * width, LANES)], slots, sem)
    copy.start()
    copy.wait()
    for source in range(got_ref.shape[0]):
        for row in range(quota):
            slot = slots[source, 0, row].astype(jnp.int32)
            out_ref[pl.ds(slot, 1), :] = got_ref[source, :, row * width:(row + 1) * width]


def smem():
    return pl.BlockSpec(memory_space=pltpu.SMEM)


def vmem():
    return pl.BlockSpec(memory_space=pltpu.VMEM)


def call(body, name, small, large, out_shape, flops, scratch=()):
    operands = (*small, *large)
    moved = sum(array.size * array.dtype.itemsize for array in (*operands, *jax.tree.leaves(out_shape)))
    kept = sum(math.prod(array.shape) * 4 for array in scratch if hasattr(array, "shape"))
    return pl.pallas_call(
        body,
        out_shape=out_shape,
        in_specs=[smem()] * len(small) + [vmem()] * len(large),
        out_specs=jax.tree.map(lambda _: vmem(), out_shape),
        scratch_shapes=list(scratch),
        compiler_params=pltpu.CompilerParams(vmem_limit_bytes=moved + kept + SPARE_VMEM),
        cost_estimate=pl.CostEstimate(flops=flops, bytes_accessed=moved, transcendentals=0),
        name=name,
    )(*operands)


def on_device(item_factors, ratings, block_ids, live_counts, owner_rows):
    item_local, width = item_factors.shape
    users_here, columns = ratings.shape
    batch_count, slot_count = block_ids.shape
    batch_rows = users_here // batch_count
    block_size = columns // slot_count
    panel_count = lax.axis_size("blk")
    rep_count = lax.axis_size("rep")
    device_count = rep_count * panel_count
    quota = users_here // device_count
    chips = panel_count // 2
    per_panel = slot_count // panel_count
    blocks = item_local // block_size
    part_rows = block_size // rep_count
    span = 2 * per_panel * block_size
    rep = lax.axis_index("rep")

    def over_blk(array, target):
        return lax.ppermute(array, "blk", [(b, target(b)) for b in range(panel_count)])

    def over_rep(array, part):
        return lax.ppermute(array, "rep", [(r, r ^ part) for r in range(rep_count)])

    def other_core(array):
        return over_blk(array, lambda b: b ^ 1)

    whole = item_factors.reshape(blocks, block_size, width)
    piece = lax.dynamic_slice(whole, (0, rep * part_rows, 0), (blocks, part_rows, width))

    after = lax.optimization_barrier
    other_whole = other_core(whole)
    pieces = {0: piece}
    for hop in (1, chips - 1):
        pieces[hop] = over_blk(piece, lambda b: (b + 2 * hop) % panel_count)
    other_whole, wanted = after((other_whole, block_ids))
    ids = [wanted] + [over_rep(wanted, part) for part in range(1, rep_count)]

    gram_rows = width // rep_count
    gram = sum(
        dot32(lax.dynamic_slice(panel, (0, rep * gram_rows), (item_local, gram_rows)), panel, ((0,), (0,)))
        for panel in (item_factors, other_whole.reshape(item_local, width))
    )
    pieces[chips - 1], _ = after((pieces[chips - 1], ids))
    pieces[1], ids, gram = after((pieces[1], ids, gram))
    for k in range(2, chips - 1):
        pieces[k] = over_blk(pieces[k - 1], lambda b: (b + 2) % panel_count)

    before = (jnp.arange(users_here)[:, None] < jnp.arange(users_here)[None, :]).astype(jnp.bfloat16)
    target_dev = owner_rows // users_here
    goes = target_dev[None, :] == jnp.arange(device_count)[:, None]
    goes_rank = dot32(goes.astype(jnp.bfloat16), before).astype(jnp.int32)
    sent = goes[:, None, :] & (goes_rank[:, None, :] == jnp.arange(quota)[None, :, None])
    slots = jnp.sum(jnp.where(sent, (owner_rows % users_here)[None, None, :], 0), axis=2)
    slots = jnp.pad(slots.astype(jnp.float32), ((0, 0), (0, LANES - quota)))[:, None, :]
    place = target_dev * quota + jnp.sum(jnp.where(goes, goes_rank, 0), axis=0)

    def table_shape(steps):
        rows = len(steps) * span
        return (
            jax.ShapeDtypeStruct((batch_count, rows, width), jnp.bfloat16),
            jax.ShapeDtypeStruct((batch_count, width, rows), jnp.bfloat16),
        )

    near_first = sorted(range(1, chips), key=lambda k: min(k, chips - k))
    stages = [near_first[i:i + 2] for i in range(0, chips - 1, 2)]
    chosen, tables = None, []
    for steps in stages:
        pairs = []
        if chosen is not None:
            parts = [chosen[0]] + [over_rep(chosen[part], part) for part in range(1, rep_count)]
        if steps is stages[1]:
            chosen, home, gram = after((chosen, other_whole, gram))
            gram = gram + over_blk(gram, lambda b: b ^ 2)
            tables = [call(
                functools.partial(pick_kernel, chips, batch_count, per_panel), "pick",
                [block_ids], [whole, home], table_shape([0]), 1 << 20,
            )]
        for k in steps:
            piece = pieces[k]
            if chosen is not None:
                piece, parts[1:3], tables[0] = after((piece, parts[1:3], tables[0]))
            pairs += [piece, other_core(piece)]
        if chosen is not None:
            tables.append(call(
                functools.partial(join_kernel, rep_count, held, batch_count, per_panel), "join",
                [], parts, table_shape(held), 1 << 20,
            ))
        last = steps is stages[-1]
        bit = 4
        while last and bit < panel_count:
            gram = gram + over_blk(gram, lambda b: b ^ bit)
            bit *= 2
        count = len(steps) * batch_count * 2 * per_panel + last * (2 * gram_rows // part_rows)
        picked = jax.ShapeDtypeStruct((count, part_rows, width), jnp.bfloat16)
        chosen = call(
            functools.partial(select_kernel, chips, rep_count, steps, batch_count, per_panel), "select",
            ids, pairs + [gram] * last, (picked,) * rep_count, 1 << 20,
        )
        held = steps
    parts = [chosen[0]] + [over_rep(chosen[part], part) for part in range(1, rep_count)]
    grams = (jax.ShapeDtypeStruct((width, width), jnp.bfloat16),) * 2
    *table, gram_high, gram_low = call(
        functools.partial(join_kernel, rep_count, held, batch_count, per_panel), "join",
        [], parts, table_shape(held) + grams, 1 << 20,
    )
    tables.append(table)
    rows_list, cols_list = [table[0] for table in tables], [table[1] for table in tables]

    lanes = quota * width + LANES
    last_columns = rows_list[-1].shape[1]
    per_batch = functools.partial(jax.ShapeDtypeStruct, dtype=jnp.float32)
    weight, last_targets, partial = call(
        functools.partial(weigh_kernel, chips, [0] + near_first, block_size, batch_count), "weigh",
        [live_counts], [ratings, *rows_list[:-1]],
        (
            per_batch((batch_count, batch_rows, columns)),
            jax.ShapeDtypeStruct((batch_count, 2 * batch_rows, last_columns), jnp.bfloat16),
            per_batch((batch_count, batch_rows, width)),
        ),
        4 * users_here * columns * width,
        [pltpu.VMEM((batch_count, 2 * batch_rows, columns - last_columns), jnp.bfloat16)],
    )
    state = pltpu.VMEM((batch_count, batch_rows, width), jnp.float32)
    send_rows = call(
        functools.partial(solve_kernel, batch_rows, batch_count), "solve",
        [place], [slots, gram_high, gram_low, weight, last_targets, partial, *rows_list, *cols_list],
        jax.ShapeDtypeStruct((device_count, 1, lanes), jnp.float32),
        8 * 4 * users_here * columns * width,
        [
            pltpu.VMEM((batch_count, 2 * batch_rows, columns), jnp.bfloat16),
            state, state, state, pltpu.VMEM((batch_count, batch_rows, 1), jnp.float32),
        ],
    )
    got_rows = lax.all_to_all(send_rows, ("rep", "blk"), split_axis=0, concat_axis=0, tiled=True)
    return call(
        place_kernel, "place", [], [got_rows],
        jax.ShapeDtypeStruct((users_here, width), jnp.float32), 1 << 20,
        [pltpu.SMEM((device_count, 1, LANES), jnp.float32), pltpu.SemaphoreType.DMA],
    )


def solution(mesh):
    placed = (
        P("blk", None),
        P(("rep", "blk"), None),
        P(("rep", "blk"), None),
        P(("rep", "blk")),
        P(("rep", "blk")),
    )
    return jax.shard_map(
        on_device, mesh=mesh, in_specs=placed, out_specs=P(("rep", "blk"), None), check_vma=False
    )
```

```python
import functools
import math
import jax
import jax.numpy as jnp
from jax import lax
from jax.experimental import pallas as pl
from jax.experimental.pallas import tpu as pltpu
from jax.sharding import PartitionSpec as P

ITERS = 8
WIDE_ITERS = 1
TILE = 256
LANES = 128
SPARE_VMEM = 6 * 1024 * 1024

conf_scale = 6.0
ridge_term = 0.5


def dot32(left, right, dims=((1,), (0,))):
    return lax.dot_general(left, right, (dims, ((), ())), preferred_element_type=jnp.float32)


def halves(value):
    high = value.astype(jnp.bfloat16)
    low = (value - high.astype(jnp.float32)).astype(jnp.bfloat16)
    return high, low


def local_slots(core, per_panel):
    for side in range(2):
        parity = core if side == 0 else 1 - core
        for pick in range(per_panel):
            yield side, parity * per_panel + pick


def position(chips, back):
    blk = lax.axis_index("blk")
    return lax.rem(blk, 2), lax.rem(lax.div(blk, 2) + chips - back, chips)


def select_kernel(chips, reps, steps, batch_count, per_panel, *refs):
    ids_refs, refs = refs[:reps], refs[reps:]
    panel_refs, refs = refs[:2 * len(steps)], refs[2 * len(steps):]
    gram_refs = [ref for ref in refs if ref.dtype == jnp.float32]
    out_refs = refs[len(gram_refs):]
    slots = 2 * per_panel
    blocks, size, _ = panel_refs[0].shape
    named = batch_count * slots
    for ids_ref, out_ref in zip(ids_refs, out_refs):
        for i, back in enumerate(steps):
            core, chip = position(chips, back)
            for batch in range(batch_count):
                for side, local in local_slots(core, per_panel):
                    block = ids_ref[batch, chip * slots + local]
                    out_ref[i * named + batch * slots + local] = panel_refs[2 * i + side][lax.rem(block, blocks)]
        for gram_ref in gram_refs:
            gram = jnp.concatenate(halves(gram_ref[...]), axis=0)
            out_ref[len(steps) * named:] = gram.reshape(-1, size, gram.shape[1])


def join_kernel(reps, steps, batch_count, per_panel, *refs):
    part_refs, (rows_ref, cols_ref, *gram_refs) = refs[:reps], refs[reps:]
    rep = lax.axis_index("rep")
    size = part_refs[0].shape[1]
    slots = 2 * per_panel
    named = batch_count * slots
    for part, ref in enumerate(part_refs):
        for i in range(len(steps)):
            for batch in range(batch_count):
                for local in range(slots):
                    offset = (i * slots + local) * reps * size + (rep ^ part) * size
                    rows_ref[batch, pl.ds(pl.multiple_of(offset, size), size), :] = ref[
                        i * named + batch * slots + local
                    ]
        extra = ref.shape[0] - len(steps) * named
        half = extra // 2
        for i, gram_ref in enumerate(gram_refs):
            start = len(steps) * named + i * half
            offset = pl.multiple_of((rep ^ part) * size * half, size * half)
            gram_ref[pl.ds(offset, size * half), :] = ref[start:start + half].reshape(size * half, ref.shape[2])
    for batch in range(batch_count):
        cols_ref[batch] = rows_ref[batch].T


def pick_kernel(chips, batch_count, per_panel, ids_ref, own_ref, other_ref, rows_ref, cols_ref):
    core, chip = position(chips, 0)
    slots = 2 * per_panel
    blocks, block_size, _ = own_ref.shape
    for batch in range(batch_count):
        for side, local in local_slots(core, per_panel):
            block = ids_ref[batch, chip * slots + local]
            held = other_ref if side else own_ref
            offset = pl.multiple_of(local * block_size, block_size)
            rows_ref[batch, pl.ds(offset, block_size), :] = held[lax.rem(block, blocks)]
        cols_ref[batch] = rows_ref[batch].T


def weigh_kernel(chips, steps, block_size, batch_count, *refs):
    live_ref, ratings_ref = refs[:2]
    rows_refs, (weight, last, partial, early) = refs[2:-4], refs[-4:]
    users = ratings_ref.shape[0] // batch_count
    columns = ratings_ref.shape[1]
    span = columns // chips
    first_last = columns - last.shape[2]
    for column in range(0, columns, TILE):
        _, chip = position(chips, steps[column // span])
        start = pl.multiple_of(chip * span + column % span, TILE)
        index = start + lax.broadcasted_iota(jnp.int32, (users, TILE), 1)
        for batch in range(batch_count):
            rated = ratings_ref[batch * users:(batch + 1) * users, pl.ds(start, TILE)].astype(jnp.float32)
            live = index < live_ref[batch] * block_size
            scaled = jnp.where(live, conf_scale * rated, 0.0)
            weight[batch, :, column:column + TILE] = scaled
            high, low = halves(jnp.where(live, 1.0 + scaled, 0.0))
            target, at = (early, column) if column < first_last else (last, column - first_last)
            target[batch, :users, at:at + TILE] = high
            target[batch, users:, at:at + TILE] = low
    for batch in range(batch_count):
        total, start = None, 0
        for ref in rows_refs:
            term = dot32(early[batch, :, start:start + ref.shape[1]], ref[batch])
            total = term if total is None else total + term
            start += ref.shape[1]
        partial[batch] = total[:users] + total[users:]


def solve_kernel(users, batch_count, *refs):
    place_ref, slots_ref, gram_high, gram_low, weight, last, partial = refs[:7]
    refs = refs[7:]
    tables = (len(refs) - 6) // 2
    rows_refs, cols_refs, refs = refs[:tables], refs[tables:2 * tables], refs[2 * tables:]
    send_ref, back, x_s, r_s, p_s, n_s = refs
    batches = range(batch_count)
    tiles, starts = [], []
    for table, ref in enumerate(rows_refs):
        start = sum(other.shape[1] for other in rows_refs[:table])
        starts.append(start)
        tiles += [(table, first, start + first) for first in range(0, ref.shape[1], TILE)]

    def back_dot(batch, rows):
        total = None
        for table, start in enumerate(starts):
            size = rows_refs[table].shape[1]
            term = dot32(back[batch, :rows, start:start + size], rows_refs[table][batch])
            total = term if total is None else total + term
        return total

    def put_halves(batch, column, value):
        high, low = halves(value)
        back[batch, :users, column:column + TILE] = high
        back[batch, users:, column:column + TILE] = low

    for batch in batches:
        total = dot32(last[batch], rows_refs[-1][batch])
        target_proj = partial[batch] + total[:users] + total[users:]
        x_s[batch] = jnp.zeros_like(target_proj)
        r_s[batch] = target_proj
        p_s[batch] = target_proj
        n_s[batch] = jnp.sum(target_proj * target_proj, axis=1, keepdims=True)

    def advance(batch, wide, final):
        direction = p_s[batch]
        high, low = halves(direction)
        both = jnp.concatenate([high, low], axis=0)
        for table, first, column in tiles:
            projected = dot32(both if wide else high, cols_refs[table][batch, :, first:first + TILE])
            if wide:
                projected = projected[:users] + projected[users:]
            projected = projected * weight[batch, :, column:column + TILE]
            if wide:
                put_halves(batch, column, projected)
            else:
                back[batch, :users, column:column + TILE] = projected.astype(jnp.bfloat16)
        gram_part = dot32(both, gram_high[...])
        image = gram_part[:users] + gram_part[users:] + dot32(high, gram_low[...]) + ridge_term * direction
        total = back_dot(batch, 2 * users if wide else users)
        if wide:
            total = total[:users] + total[users:]
        image = image + total
        norm_now = n_s[batch]
        step_size = norm_now / jnp.sum(direction * image, axis=1, keepdims=True)
        x_s[batch] = x_s[batch] + step_size * direction
        if final:
            return
        residual = r_s[batch] - step_size * image
        r_s[batch] = residual
        norm_next = jnp.sum(residual * residual, axis=1, keepdims=True)
        p_s[batch] = residual + norm_next / norm_now * direction
        n_s[batch] = norm_next

    for iteration in range(ITERS):
        for batch in batches:
            advance(batch, iteration < WIDE_ITERS, iteration == ITERS - 1)
    width = x_s.shape[2]
    quota = batch_count * users // send_ref.shape[0]
    send_ref[:, :, quota * width:] = slots_ref[...]
    for batch in batches:
        for user in range(users):
            place = place_ref[batch * users + user]
            lanes = pl.ds(pl.multiple_of(lax.rem(place, quota) * width, width), width)
            send_ref[lax.div(place, quota), :, lanes] = x_s[batch, user:user + 1, :]


def place_kernel(got_ref, out_ref, slots, sem):
    width = out_ref.shape[1]
    quota = out_ref.shape[0] // got_ref.shape[0]
    copy = pltpu.make_async_copy(got_ref.at[:, :, pl.ds(quota * width, LANES)], slots, sem)
    copy.start()
    copy.wait()
    for source in range(got_ref.shape[0]):
        for row in range(quota):
            slot = slots[source, 0, row].astype(jnp.int32)
            out_ref[pl.ds(slot, 1), :] = got_ref[source, :, row * width:(row + 1) * width]


def smem():
    return pl.BlockSpec(memory_space=pltpu.SMEM)


def vmem():
    return pl.BlockSpec(memory_space=pltpu.VMEM)


def call(body, name, small, large, out_shape, flops, scratch=()):
    operands = (*small, *large)
    moved = sum(array.size * array.dtype.itemsize for array in (*operands, *jax.tree.leaves(out_shape)))
    kept = sum(math.prod(array.shape) * 4 for array in scratch if hasattr(array, "shape"))
    return pl.pallas_call(
        body,
        out_shape=out_shape,
        in_specs=[smem()] * len(small) + [vmem()] * len(large),
        out_specs=jax.tree.map(lambda _: vmem(), out_shape),
        scratch_shapes=list(scratch),
        compiler_params=pltpu.CompilerParams(vmem_limit_bytes=moved + kept + SPARE_VMEM),
        cost_estimate=pl.CostEstimate(flops=flops, bytes_accessed=moved, transcendentals=0),
        name=name,
    )(*operands)


def on_device(item_factors, ratings, block_ids, live_counts, owner_rows):
    item_local, width = item_factors.shape
    users_here, columns = ratings.shape
    batch_count, slot_count = block_ids.shape
    batch_rows = users_here // batch_count
    block_size = columns // slot_count
    panel_count = lax.axis_size("blk")
    rep_count = lax.axis_size("rep")
    device_count = rep_count * panel_count
    quota = users_here // device_count
    chips = panel_count // 2
    per_panel = slot_count // panel_count
    blocks = item_local // block_size
    part_rows = block_size // rep_count
    span = 2 * per_panel * block_size
    rep = lax.axis_index("rep")

    def over_blk(array, target):
        return lax.ppermute(array, "blk", [(b, target(b)) for b in range(panel_count)])

    def over_rep(array, part):
        return lax.ppermute(array, "rep", [(r, r ^ part) for r in range(rep_count)])

    def other_core(array):
        return over_blk(array, lambda b: b ^ 1)

    whole = item_factors.reshape(blocks, block_size, width)
    piece = lax.dynamic_slice(whole, (0, rep * part_rows, 0), (blocks, part_rows, width))

    after = lax.optimization_barrier
    other_whole = other_core(whole)
    pieces = {0: piece}
    for hop in (1, chips - 1):
        pieces[hop] = over_blk(piece, lambda b: (b + 2 * hop) % panel_count)
    other_whole, wanted = after((other_whole, block_ids))
    ids = [wanted] + [over_rep(wanted, part) for part in range(1, rep_count)]

    gram_rows = width // rep_count
    gram = sum(
        dot32(lax.dynamic_slice(panel, (0, rep * gram_rows), (item_local, gram_rows)), panel, ((0,), (0,)))
        for panel in (item_factors, other_whole.reshape(item_local, width))
    )
    pieces[chips - 1], _ = after((pieces[chips - 1], ids))
    pieces[1], ids, gram = after((pieces[1], ids, gram))
    gram_next = over_blk(gram, lambda b: b ^ 2)
    for k in range(2, chips - 1):
        pieces[k] = over_blk(pieces[k - 1], lambda b: (b + 2) % panel_count)

    before = (jnp.arange(users_here)[:, None] < jnp.arange(users_here)[None, :]).astype(jnp.bfloat16)
    target_dev = owner_rows // users_here
    goes = target_dev[None, :] == jnp.arange(device_count)[:, None]
    goes_rank = dot32(goes.astype(jnp.bfloat16), before).astype(jnp.int32)
    sent = goes[:, None, :] & (goes_rank[:, None, :] == jnp.arange(quota)[None, :, None])
    slots = jnp.sum(jnp.where(sent, (owner_rows % users_here)[None, None, :], 0), axis=2)
    slots = jnp.pad(slots.astype(jnp.float32), ((0, 0), (0, LANES - quota)))[:, None, :]
    place = target_dev * quota + jnp.sum(jnp.where(goes, goes_rank, 0), axis=0)

    def table_shape(steps):
        rows = len(steps) * span
        return (
            jax.ShapeDtypeStruct((batch_count, rows, width), jnp.bfloat16),
            jax.ShapeDtypeStruct((batch_count, width, rows), jnp.bfloat16),
        )

    near_first = sorted(range(1, chips), key=lambda k: min(k, chips - k))
    stages = [near_first[i:i + 2] for i in range(0, chips - 1, 2)]
    chosen, tables = None, []
    for steps in stages:
        pairs = []
        if chosen is not None:
            parts = [chosen[0]] + [over_rep(chosen[part], part) for part in range(1, rep_count)]
        if steps is stages[1]:
            chosen, home, gram_next = after((chosen, other_whole, gram_next))
            gram = gram + gram_next
            bit = 4
            while bit < panel_count:
                gram = gram + over_blk(gram, lambda b: b ^ bit)
                bit *= 2
            tables = [call(
                functools.partial(pick_kernel, chips, batch_count, per_panel), "pick",
                [block_ids], [whole, home], table_shape([0]), 1 << 20,
            )]
        for k in steps:
            piece = pieces[k]
            if chosen is not None:
                piece, parts[1:3], tables[0], gram = after((piece, parts[1:3], tables[0], gram))
            pairs += [piece, other_core(piece)]
        if chosen is not None:
            tables.append(call(
                functools.partial(join_kernel, rep_count, held, batch_count, per_panel), "join",
                [], parts, table_shape(held), 1 << 20,
            ))
        last = steps is stages[-1]
        count = len(steps) * batch_count * 2 * per_panel + last * (2 * gram_rows // part_rows)
        picked = jax.ShapeDtypeStruct((count, part_rows, width), jnp.bfloat16)
        chosen = call(
            functools.partial(select_kernel, chips, rep_count, steps, batch_count, per_panel), "select",
            ids, pairs + [gram] * last, (picked,) * rep_count, 1 << 20,
        )
        held = steps
    parts = [chosen[0]] + [over_rep(chosen[part], part) for part in range(1, rep_count)]
    grams = (jax.ShapeDtypeStruct((width, width), jnp.bfloat16),) * 2
    *table, gram_high, gram_low = call(
        functools.partial(join_kernel, rep_count, held, batch_count, per_panel), "join",
        [], parts, table_shape(held) + grams, 1 << 20,
    )
    tables.append(table)
    rows_list, cols_list = [table[0] for table in tables], [table[1] for table in tables]

    lanes = quota * width + LANES
    last_columns = rows_list[-1].shape[1]
    per_batch = functools.partial(jax.ShapeDtypeStruct, dtype=jnp.float32)
    weight, last_targets, partial = call(
        functools.partial(weigh_kernel, chips, [0] + near_first, block_size, batch_count), "weigh",
        [live_counts], [ratings, *rows_list[:-1]],
        (
            per_batch((batch_count, batch_rows, columns)),
            jax.ShapeDtypeStruct((batch_count, 2 * batch_rows, last_columns), jnp.bfloat16),
            per_batch((batch_count, batch_rows, width)),
        ),
        4 * users_here * columns * width,
        [pltpu.VMEM((batch_count, 2 * batch_rows, columns - last_columns), jnp.bfloat16)],
    )
    state = pltpu.VMEM((batch_count, batch_rows, width), jnp.float32)
    send_rows = call(
        functools.partial(solve_kernel, batch_rows, batch_count), "solve",
        [place], [slots, gram_high, gram_low, weight, last_targets, partial, *rows_list, *cols_list],
        jax.ShapeDtypeStruct((device_count, 1, lanes), jnp.float32),
        8 * 4 * users_here * columns * width,
        [
            pltpu.VMEM((batch_count, 2 * batch_rows, columns), jnp.bfloat16),
            state, state, state, pltpu.VMEM((batch_count, batch_rows, 1), jnp.float32),
        ],
    )
    got_rows = lax.all_to_all(send_rows, ("rep", "blk"), split_axis=0, concat_axis=0, tiled=True)
    return call(
        place_kernel, "place", [], [got_rows],
        jax.ShapeDtypeStruct((users_here, width), jnp.float32), 1 << 20,
        [pltpu.SMEM((device_count, 1, LANES), jnp.float32), pltpu.SemaphoreType.DMA],
    )


def solution(mesh):
    placed = (
        P("blk", None),
        P(("rep", "blk"), None),
        P(("rep", "blk"), None),
        P(("rep", "blk")),
        P(("rep", "blk")),
    )
    return jax.shard_map(
        on_device, mesh=mesh, in_specs=placed, out_specs=P(("rep", "blk"), None), check_vma=False
    )
```

```python
import functools
import math
import jax
import jax.numpy as jnp
from jax import lax
from jax.experimental import pallas as pl
from jax.experimental.pallas import tpu as pltpu
from jax.sharding import PartitionSpec as P

ITERS = 8
WIDE_ITERS = 1
TILE = 256
LANES = 128
SPARE_VMEM = 6 * 1024 * 1024

conf_scale = 6.0
ridge_term = 0.5


def dot32(left, right, dims=((1,), (0,))):
    return lax.dot_general(left, right, (dims, ((), ())), preferred_element_type=jnp.float32)


def halves(value):
    high = value.astype(jnp.bfloat16)
    low = (value - high.astype(jnp.float32)).astype(jnp.bfloat16)
    return high, low


def local_slots(core, per_panel):
    for side in range(2):
        parity = core if side == 0 else 1 - core
        for pick in range(per_panel):
            yield side, parity * per_panel + pick


def position(chips, back):
    blk = lax.axis_index("blk")
    return lax.rem(blk, 2), lax.rem(lax.div(blk, 2) + chips - back, chips)


def head_kernel(panel_ref, piece_ref, gram_ref):
    rep = lax.axis_index("rep")
    blocks, block_size, width = panel_ref.shape
    size = piece_ref.shape[1]
    part = pl.ds(pl.multiple_of(rep * size, size), size)
    piece_ref[:blocks] = panel_ref[:, part, :]
    flat = panel_ref[...].reshape(blocks * block_size, width)
    rows = width * size // block_size
    product = dot32(flat, flat, ((0,), (0,)))
    gram = product[:rows]
    for other in range(1, block_size // size):
        gram = jnp.where(rep == other, product[other * rows:(other + 1) * rows], gram)
    gram = jnp.concatenate(halves(gram), axis=0).reshape(gram_ref.shape)
    piece_ref[blocks:] = gram
    gram_ref[...] = gram


def select_kernel(chips, reps, blocks, steps, batch_count, per_panel, first, last, *refs):
    ids_refs, refs = refs[:reps], refs[reps:]
    panel_refs, refs = refs[:2 * len(steps)], refs[2 * len(steps):]
    gram_refs, refs = refs[:1 + first], refs[1 + first:]
    out_refs, sum_refs = refs[:reps], refs[reps:]
    slots = 2 * per_panel
    size, width = panel_refs[0].shape[1:]
    named = batch_count * slots
    for ids_ref, out_ref in zip(ids_refs, out_refs):
        for i, step in enumerate(steps):
            core, chip = position(chips, step)
            for batch in range(batch_count):
                for side, local in local_slots(core, per_panel):
                    block = ids_ref[batch, chip * slots + local]
                    out_ref[i * named + batch * slots + local] = panel_refs[2 * i + side][lax.rem(block, blocks)]

    def summed(ref, start):
        both = ref[start:].astype(jnp.float32).reshape(-1, width)
        return both[:both.shape[0] // 2] + both[both.shape[0] // 2:]

    gram = sum(summed(ref, 0) for ref in gram_refs) if first else gram_refs[0][...]
    gram = gram + sum(summed(ref, blocks) for ref in panel_refs)
    for sum_ref in sum_refs:
        sum_ref[...] = gram
    if last:
        gram = jnp.concatenate(halves(gram), axis=0).reshape(-1, size, width)
        for out_ref in out_refs:
            out_ref[len(steps) * named:] = gram


def join_kernel(reps, steps, batch_count, per_panel, *refs):
    part_refs, (rows_ref, cols_ref, *gram_refs) = refs[:reps], refs[reps:]
    rep = lax.axis_index("rep")
    size = part_refs[0].shape[1]
    slots = 2 * per_panel
    named = batch_count * slots
    for part, ref in enumerate(part_refs):
        for i in range(len(steps)):
            for batch in range(batch_count):
                for local in range(slots):
                    offset = (i * slots + local) * reps * size + (rep ^ part) * size
                    rows_ref[batch, pl.ds(pl.multiple_of(offset, size), size), :] = ref[
                        i * named + batch * slots + local
                    ]
        extra = ref.shape[0] - len(steps) * named
        half = extra // 2
        for i, gram_ref in enumerate(gram_refs):
            start = len(steps) * named + i * half
            offset = pl.multiple_of((rep ^ part) * size * half, size * half)
            gram_ref[pl.ds(offset, size * half), :] = ref[start:start + half].reshape(size * half, ref.shape[2])
    for batch in range(batch_count):
        cols_ref[batch] = rows_ref[batch].T


def pick_kernel(chips, batch_count, per_panel, ids_ref, own_ref, other_ref, rows_ref, cols_ref):
    core, chip = position(chips, 0)
    slots = 2 * per_panel
    blocks, block_size, _ = own_ref.shape
    for batch in range(batch_count):
        for side, local in local_slots(core, per_panel):
            block = ids_ref[batch, chip * slots + local]
            held = other_ref if side else own_ref
            offset = pl.multiple_of(local * block_size, block_size)
            rows_ref[batch, pl.ds(offset, block_size), :] = held[lax.rem(block, blocks)]
        cols_ref[batch] = rows_ref[batch].T


def weigh_kernel(chips, steps, block_size, batch_count, *refs):
    live_ref, ratings_ref = refs[:2]
    rows_refs, (weight, last, partial, early) = refs[2:-4], refs[-4:]
    users = ratings_ref.shape[0] // batch_count
    columns = ratings_ref.shape[1]
    span = columns // chips
    first_last = columns - last.shape[2]
    for column in range(0, columns, TILE):
        _, chip = position(chips, steps[column // span])
        start = pl.multiple_of(chip * span + column % span, TILE)
        index = start + lax.broadcasted_iota(jnp.int32, (users, TILE), 1)
        for batch in range(batch_count):
            rated = ratings_ref[batch * users:(batch + 1) * users, pl.ds(start, TILE)].astype(jnp.float32)
            live = index < live_ref[batch] * block_size
            scaled = jnp.where(live, conf_scale * rated, 0.0)
            weight[batch, :, column:column + TILE] = scaled
            high, low = halves(jnp.where(live, 1.0 + scaled, 0.0))
            target, at = (early, column) if column < first_last else (last, column - first_last)
            target[batch, :users, at:at + TILE] = high
            target[batch, users:, at:at + TILE] = low
    for batch in range(batch_count):
        total, start = None, 0
        for ref in rows_refs:
            term = dot32(early[batch, :, start:start + ref.shape[1]], ref[batch])
            total = term if total is None else total + term
            start += ref.shape[1]
        partial[batch] = total[:users] + total[users:]


def solve_kernel(users, batch_count, *refs):
    place_ref, slots_ref, gram_high, gram_low, weight, last, partial = refs[:7]
    refs = refs[7:]
    tables = (len(refs) - 6) // 2
    rows_refs, cols_refs, refs = refs[:tables], refs[tables:2 * tables], refs[2 * tables:]
    send_ref, back, x_s, r_s, p_s, n_s = refs
    batches = range(batch_count)
    tiles, starts = [], []
    for table, ref in enumerate(rows_refs):
        start = sum(other.shape[1] for other in rows_refs[:table])
        starts.append(start)
        tiles += [(table, first, start + first) for first in range(0, ref.shape[1], TILE)]

    def back_dot(batch, rows):
        total = None
        for table, start in enumerate(starts):
            size = rows_refs[table].shape[1]
            term = dot32(back[batch, :rows, start:start + size], rows_refs[table][batch])
            total = term if total is None else total + term
        return total

    def put_halves(batch, column, value):
        high, low = halves(value)
        back[batch, :users, column:column + TILE] = high
        back[batch, users:, column:column + TILE] = low

    for batch in batches:
        total = dot32(last[batch], rows_refs[-1][batch])
        target_proj = partial[batch] + total[:users] + total[users:]
        x_s[batch] = jnp.zeros_like(target_proj)
        r_s[batch] = target_proj
        p_s[batch] = target_proj
        n_s[batch] = jnp.sum(target_proj * target_proj, axis=1, keepdims=True)

    def advance(batch, wide, final):
        direction = p_s[batch]
        high, low = halves(direction)
        both = jnp.concatenate([high, low], axis=0)
        for table, first, column in tiles:
            projected = dot32(both if wide else high, cols_refs[table][batch, :, first:first + TILE])
            if wide:
                projected = projected[:users] + projected[users:]
            projected = projected * weight[batch, :, column:column + TILE]
            if wide:
                put_halves(batch, column, projected)
            else:
                back[batch, :users, column:column + TILE] = projected.astype(jnp.bfloat16)
        gram_part = dot32(both, gram_high[...])
        image = gram_part[:users] + gram_part[users:] + dot32(high, gram_low[...]) + ridge_term * direction
        total = back_dot(batch, 2 * users if wide else users)
        if wide:
            total = total[:users] + total[users:]
        image = image + total
        norm_now = n_s[batch]
        step_size = norm_now / jnp.sum(direction * image, axis=1, keepdims=True)
        x_s[batch] = x_s[batch] + step_size * direction
        if final:
            return
        residual = r_s[batch] - step_size * image
        r_s[batch] = residual
        norm_next = jnp.sum(residual * residual, axis=1, keepdims=True)
        p_s[batch] = residual + norm_next / norm_now * direction
        n_s[batch] = norm_next

    for iteration in range(ITERS):
        for batch in batches:
            advance(batch, iteration < WIDE_ITERS, iteration == ITERS - 1)
    width = x_s.shape[2]
    quota = batch_count * users // send_ref.shape[0]
    send_ref[:, :, quota * width:] = slots_ref[...]
    for batch in batches:
        for user in range(users):
            place = place_ref[batch * users + user]
            lanes = pl.ds(pl.multiple_of(lax.rem(place, quota) * width, width), width)
            send_ref[lax.div(place, quota), :, lanes] = x_s[batch, user:user + 1, :]


def place_kernel(got_ref, out_ref, slots, sem):
    width = out_ref.shape[1]
    quota = out_ref.shape[0] // got_ref.shape[0]
    copy = pltpu.make_async_copy(got_ref.at[:, :, pl.ds(quota * width, LANES)], slots, sem)
    copy.start()
    copy.wait()
    for source in range(got_ref.shape[0]):
        for row in range(quota):
            slot = slots[source, 0, row].astype(jnp.int32)
            out_ref[pl.ds(slot, 1), :] = got_ref[source, :, row * width:(row + 1) * width]


def smem():
    return pl.BlockSpec(memory_space=pltpu.SMEM)


def vmem():
    return pl.BlockSpec(memory_space=pltpu.VMEM)


def call(body, name, small, large, out_shape, flops, scratch=()):
    operands = (*small, *large)
    moved = sum(array.size * array.dtype.itemsize for array in (*operands, *jax.tree.leaves(out_shape)))
    kept = sum(math.prod(array.shape) * 4 for array in scratch if hasattr(array, "shape"))
    return pl.pallas_call(
        body,
        out_shape=out_shape,
        in_specs=[smem()] * len(small) + [vmem()] * len(large),
        out_specs=jax.tree.map(lambda _: vmem(), out_shape),
        scratch_shapes=list(scratch),
        compiler_params=pltpu.CompilerParams(vmem_limit_bytes=moved + kept + SPARE_VMEM),
        cost_estimate=pl.CostEstimate(flops=flops, bytes_accessed=moved, transcendentals=0),
        name=name,
    )(*operands)


def on_device(item_factors, ratings, block_ids, live_counts, owner_rows):
    item_local, width = item_factors.shape
    users_here, columns = ratings.shape
    batch_count, slot_count = block_ids.shape
    batch_rows = users_here // batch_count
    block_size = columns // slot_count
    panel_count = lax.axis_size("blk")
    rep_count = lax.axis_size("rep")
    device_count = rep_count * panel_count
    quota = users_here // device_count
    chips = panel_count // 2
    per_panel = slot_count // panel_count
    blocks = item_local // block_size
    part_rows = block_size // rep_count
    span = 2 * per_panel * block_size

    def over_blk(array, target):
        return lax.ppermute(array, "blk", [(b, target(b)) for b in range(panel_count)])

    def over_rep(array, part):
        return lax.ppermute(array, "rep", [(r, r ^ part) for r in range(rep_count)])

    def other_core(array):
        return over_blk(array, lambda b: b ^ 1)

    whole = item_factors.reshape(blocks, block_size, width)
    gram_rows = width // rep_count
    gram_blocks = 2 * gram_rows // part_rows
    bf16 = functools.partial(jax.ShapeDtypeStruct, dtype=jnp.bfloat16)
    piece, gram = call(
        head_kernel, "head", [], [whole],
        (bf16((blocks + gram_blocks, part_rows, width)), bf16((gram_blocks, part_rows, width))),
        2 * item_local * width * width,
    )

    after = lax.optimization_barrier
    other_whole = other_core(whole)
    pieces = {0: piece}
    for hop in (1, chips - 1):
        pieces[hop] = over_blk(piece, lambda b: (b + 2 * hop) % panel_count)
    other_gram = other_core(gram)
    other_whole, other_gram, wanted = after((other_whole, other_gram, block_ids))
    ids = [wanted] + [over_rep(wanted, part) for part in range(1, rep_count)]

    pieces[chips - 1], _ = after((pieces[chips - 1], ids))
    pieces[1], ids = after((pieces[1], ids))
    for k in range(2, chips - 1):
        pieces[k] = over_blk(pieces[k - 1], lambda b: (b + 2) % panel_count)

    before = (jnp.arange(users_here)[:, None] < jnp.arange(users_here)[None, :]).astype(jnp.bfloat16)
    target_dev = owner_rows // users_here
    goes = target_dev[None, :] == jnp.arange(device_count)[:, None]
    goes_rank = dot32(goes.astype(jnp.bfloat16), before).astype(jnp.int32)
    sent = goes[:, None, :] & (goes_rank[:, None, :] == jnp.arange(quota)[None, :, None])
    slots = jnp.sum(jnp.where(sent, (owner_rows % users_here)[None, None, :], 0), axis=2)
    slots = jnp.pad(slots.astype(jnp.float32), ((0, 0), (0, LANES - quota)))[:, None, :]
    place = target_dev * quota + jnp.sum(jnp.where(goes, goes_rank, 0), axis=0)

    def table_shape(steps):
        rows = len(steps) * span
        return (
            jax.ShapeDtypeStruct((batch_count, rows, width), jnp.bfloat16),
            jax.ShapeDtypeStruct((batch_count, width, rows), jnp.bfloat16),
        )

    near_first = sorted(range(1, chips), key=lambda k: min(k, chips - k))
    stages = [near_first[i:i + 2] for i in range(0, chips - 1, 2)]
    chosen, tables = None, []
    for steps in stages:
        pairs = []
        if chosen is not None:
            parts = [chosen[0]] + [over_rep(chosen[part], part) for part in range(1, rep_count)]
        if steps is stages[1]:
            chosen, home = after((chosen, other_whole))
            tables = [call(
                functools.partial(pick_kernel, chips, batch_count, per_panel), "pick",
                [block_ids], [whole, home], table_shape([0]), 1 << 20,
            )]
        for k in steps:
            piece = pieces[k]
            if chosen is not None:
                piece, parts[1:3], tables[0] = after((piece, parts[1:3], tables[0]))
            pairs += [piece, other_core(piece)]
        if chosen is not None:
            tables.append(call(
                functools.partial(join_kernel, rep_count, held, batch_count, per_panel), "join",
                [], parts, table_shape(held), 1 << 20,
            ))
        first, last = steps is stages[0], steps is stages[-1]
        count = len(steps) * batch_count * 2 * per_panel + last * gram_blocks
        sums = () if last else (jax.ShapeDtypeStruct((gram_rows, width), jnp.float32),)
        chosen = call(
            functools.partial(
                select_kernel, chips, rep_count, blocks, steps, batch_count, per_panel, first, last
            ), "select",
            ids, pairs + ([gram, other_gram] if first else [gram]),
            (bf16((count, part_rows, width)),) * rep_count + sums, 1 << 20,
        )
        *chosen, gram = chosen if sums else (*chosen, None)
        held = steps
    parts = [chosen[0]] + [over_rep(chosen[part], part) for part in range(1, rep_count)]
    grams = (jax.ShapeDtypeStruct((width, width), jnp.bfloat16),) * 2
    *table, gram_high, gram_low = call(
        functools.partial(join_kernel, rep_count, held, batch_count, per_panel), "join",
        [], parts, table_shape(held) + grams, 1 << 20,
    )
    tables.append(table)
    rows_list, cols_list = [table[0] for table in tables], [table[1] for table in tables]

    lanes = quota * width + LANES
    last_columns = rows_list[-1].shape[1]
    per_batch = functools.partial(jax.ShapeDtypeStruct, dtype=jnp.float32)
    weight, last_targets, partial = call(
        functools.partial(weigh_kernel, chips, [0] + near_first, block_size, batch_count), "weigh",
        [live_counts], [ratings, *rows_list[:-1]],
        (
            per_batch((batch_count, batch_rows, columns)),
            jax.ShapeDtypeStruct((batch_count, 2 * batch_rows, last_columns), jnp.bfloat16),
            per_batch((batch_count, batch_rows, width)),
        ),
        4 * users_here * columns * width,
        [pltpu.VMEM((batch_count, 2 * batch_rows, columns - last_columns), jnp.bfloat16)],
    )
    state = pltpu.VMEM((batch_count, batch_rows, width), jnp.float32)
    send_rows = call(
        functools.partial(solve_kernel, batch_rows, batch_count), "solve",
        [place], [slots, gram_high, gram_low, weight, last_targets, partial, *rows_list, *cols_list],
        jax.ShapeDtypeStruct((device_count, 1, lanes), jnp.float32),
        8 * 4 * users_here * columns * width,
        [
            pltpu.VMEM((batch_count, 2 * batch_rows, columns), jnp.bfloat16),
            state, state, state, pltpu.VMEM((batch_count, batch_rows, 1), jnp.float32),
        ],
    )
    got_rows = lax.all_to_all(send_rows, ("rep", "blk"), split_axis=0, concat_axis=0, tiled=True)
    return call(
        place_kernel, "place", [], [got_rows],
        jax.ShapeDtypeStruct((users_here, width), jnp.float32), 1 << 20,
        [pltpu.SMEM((device_count, 1, LANES), jnp.float32), pltpu.SemaphoreType.DMA],
    )


def solution(mesh):
    placed = (
        P("blk", None),
        P(("rep", "blk"), None),
        P(("rep", "blk"), None),
        P(("rep", "blk")),
        P(("rep", "blk")),
    )
    return jax.shard_map(
        on_device, mesh=mesh, in_specs=placed, out_specs=P(("rep", "blk"), None), check_vma=False
    )
```

```python
import functools
import math
import jax
import jax.numpy as jnp
from jax import lax
from jax.experimental import pallas as pl
from jax.experimental.pallas import tpu as pltpu
from jax.sharding import PartitionSpec as P

ITERS = 8
WIDE_ITERS = 1
TILE = 256
LANES = 128
SPARE_VMEM = 6 * 1024 * 1024

conf_scale = 6.0
ridge_term = 0.5


def dot32(left, right, dims=((1,), (0,))):
    return lax.dot_general(left, right, (dims, ((), ())), preferred_element_type=jnp.float32)


def halves(value):
    high = value.astype(jnp.bfloat16)
    low = (value - high.astype(jnp.float32)).astype(jnp.bfloat16)
    return high, low


def local_slots(core, per_panel):
    for side in range(2):
        parity = core if side == 0 else 1 - core
        for pick in range(per_panel):
            yield side, parity * per_panel + pick


def position(chips, back):
    blk = lax.axis_index("blk")
    return lax.rem(blk, 2), lax.rem(lax.div(blk, 2) + chips - back, chips)


def select_kernel(chips, reps, steps, batch_count, per_panel, *refs):
    ids_refs, refs = refs[:reps], refs[reps:]
    panel_refs, refs = refs[:2 * len(steps)], refs[2 * len(steps):]
    gram_refs = [ref for ref in refs if ref.dtype == jnp.float32]
    out_refs = refs[len(gram_refs):]
    slots = 2 * per_panel
    blocks, size, _ = panel_refs[0].shape
    named = batch_count * slots
    for ids_ref, out_ref in zip(ids_refs, out_refs):
        for i, back in enumerate(steps):
            core, chip = position(chips, back)
            for batch in range(batch_count):
                for side, local in local_slots(core, per_panel):
                    block = ids_ref[batch, chip * slots + local]
                    out_ref[i * named + batch * slots + local] = panel_refs[2 * i + side][lax.rem(block, blocks)]
        for gram_ref in gram_refs:
            gram = jnp.concatenate(halves(gram_ref[...]), axis=0)
            out_ref[len(steps) * named:] = gram.reshape(-1, size, gram.shape[1])


def join_kernel(reps, steps, batch_count, per_panel, *refs):
    part_refs, (rows_ref, cols_ref, *gram_refs) = refs[:reps], refs[reps:]
    rep = lax.axis_index("rep")
    size = part_refs[0].shape[1]
    slots = 2 * per_panel
    named = batch_count * slots
    for part, ref in enumerate(part_refs):
        for i in range(len(steps)):
            for batch in range(batch_count):
                for local in range(slots):
                    offset = (i * slots + local) * reps * size + (rep ^ part) * size
                    rows_ref[batch, pl.ds(pl.multiple_of(offset, size), size), :] = ref[
                        i * named + batch * slots + local
                    ]
        extra = ref.shape[0] - len(steps) * named
        half = extra // 2
        for i, gram_ref in enumerate(gram_refs):
            start = len(steps) * named + i * half
            offset = pl.multiple_of((rep ^ part) * size * half, size * half)
            gram_ref[pl.ds(offset, size * half), :] = ref[start:start + half].reshape(size * half, ref.shape[2])
    for batch in range(batch_count):
        cols_ref[batch] = rows_ref[batch].T


def pick_kernel(chips, batch_count, per_panel, ids_ref, own_ref, other_ref, rows_ref, cols_ref):
    core, chip = position(chips, 0)
    slots = 2 * per_panel
    blocks, block_size, _ = own_ref.shape
    for batch in range(batch_count):
        for side, local in local_slots(core, per_panel):
            block = ids_ref[batch, chip * slots + local]
            held = other_ref if side else own_ref
            offset = pl.multiple_of(local * block_size, block_size)
            rows_ref[batch, pl.ds(offset, block_size), :] = held[lax.rem(block, blocks)]
        cols_ref[batch] = rows_ref[batch].T


def weigh_kernel(chips, steps, block_size, batch_count, *refs):
    live_ref, ratings_ref = refs[:2]
    rows_refs, (weight, last, partial, early) = refs[2:-4], refs[-4:]
    users = ratings_ref.shape[0] // batch_count
    columns = ratings_ref.shape[1]
    span = columns // chips
    first_last = columns - last.shape[2]
    for column in range(0, columns, TILE):
        _, chip = position(chips, steps[column // span])
        start = pl.multiple_of(chip * span + column % span, TILE)
        index = start + lax.broadcasted_iota(jnp.int32, (users, TILE), 1)
        for batch in range(batch_count):
            rated = ratings_ref[batch * users:(batch + 1) * users, pl.ds(start, TILE)].astype(jnp.float32)
            live = index < live_ref[batch] * block_size
            scaled = jnp.where(live, conf_scale * rated, 0.0)
            weight[batch, :, column:column + TILE] = scaled
            high, low = halves(jnp.where(live, 1.0 + scaled, 0.0))
            target, at = (early, column) if column < first_last else (last, column - first_last)
            target[batch, :users, at:at + TILE] = high
            target[batch, users:, at:at + TILE] = low
    for batch in range(batch_count):
        total, start = None, 0
        for ref in rows_refs:
            term = dot32(early[batch, :, start:start + ref.shape[1]], ref[batch])
            total = term if total is None else total + term
            start += ref.shape[1]
        partial[batch] = total[:users] + total[users:]


def solve_kernel(users, batch_count, *refs):
    place_ref, slots_ref, gram_high, gram_low, weight, last, partial = refs[:7]
    refs = refs[7:]
    tables = (len(refs) - 6) // 2
    rows_refs, cols_refs, refs = refs[:tables], refs[tables:2 * tables], refs[2 * tables:]
    send_ref, back, x_s, r_s, p_s, n_s = refs
    batches = range(batch_count)
    tiles, starts = [], []
    for table, ref in enumerate(rows_refs):
        start = sum(other.shape[1] for other in rows_refs[:table])
        starts.append(start)
        tiles += [(table, first, start + first) for first in range(0, ref.shape[1], TILE)]

    def back_dot(batch, rows):
        total = None
        for table, start in enumerate(starts):
            size = rows_refs[table].shape[1]
            term = dot32(back[batch, :rows, start:start + size], rows_refs[table][batch])
            total = term if total is None else total + term
        return total

    def put_halves(batch, column, value):
        high, low = halves(value)
        back[batch, :users, column:column + TILE] = high
        back[batch, users:, column:column + TILE] = low

    for batch in batches:
        total = dot32(last[batch], rows_refs[-1][batch])
        target_proj = partial[batch] + total[:users] + total[users:]
        x_s[batch] = jnp.zeros_like(target_proj)
        r_s[batch] = target_proj
        p_s[batch] = target_proj
        n_s[batch] = jnp.sum(target_proj * target_proj, axis=1, keepdims=True)

    def advance(batch, wide, final):
        direction = p_s[batch]
        high, low = halves(direction)
        both = jnp.concatenate([high, low], axis=0)
        for table, first, column in tiles:
            projected = dot32(both if wide else high, cols_refs[table][batch, :, first:first + TILE])
            if wide:
                projected = projected[:users] + projected[users:]
            projected = projected * weight[batch, :, column:column + TILE]
            if wide:
                put_halves(batch, column, projected)
            else:
                back[batch, :users, column:column + TILE] = projected.astype(jnp.bfloat16)
        gram_part = dot32(both, gram_high[...])
        image = gram_part[:users] + gram_part[users:] + dot32(high, gram_low[...]) + ridge_term * direction
        total = back_dot(batch, 2 * users if wide else users)
        if wide:
            total = total[:users] + total[users:]
        image = image + total
        norm_now = n_s[batch]
        step_size = norm_now / jnp.sum(direction * image, axis=1, keepdims=True)
        x_s[batch] = x_s[batch] + step_size * direction
        if final:
            return
        residual = r_s[batch] - step_size * image
        r_s[batch] = residual
        norm_next = jnp.sum(residual * residual, axis=1, keepdims=True)
        p_s[batch] = residual + norm_next / norm_now * direction
        n_s[batch] = norm_next

    for iteration in range(ITERS):
        for batch in batches:
            advance(batch, iteration < WIDE_ITERS, iteration == ITERS - 1)
    width = x_s.shape[2]
    quota = batch_count * users // send_ref.shape[0]
    send_ref[:, :, quota * width:] = slots_ref[...]
    for batch in batches:
        for user in range(users):
            row = batch * users + user
            lanes = pl.ds(pl.multiple_of(place_ref[1, row], width), width)
            send_ref[place_ref[0, row], :, lanes] = x_s[batch, user:user + 1, :]


def place_kernel(got_ref, out_ref, rows, slots, sems):
    width = out_ref.shape[1]
    quota = out_ref.shape[0] // got_ref.shape[0]
    copies = [
        pltpu.make_async_copy(got_ref.at[:, :, pl.ds(quota * width, LANES)], slots, sems.at[0]),
        pltpu.make_async_copy(got_ref.at[:, :, pl.ds(0, quota * width)], rows, sems.at[1]),
    ]
    for copy in copies:
        copy.start()
    for copy in copies:
        copy.wait()
    for source in range(got_ref.shape[0]):
        for row in range(quota):
            slot = slots[source, 0, row].astype(jnp.int32)
            out_ref[pl.ds(slot, 1), :] = rows[source, :, row * width:(row + 1) * width]


def smem():
    return pl.BlockSpec(memory_space=pltpu.SMEM)


def vmem():
    return pl.BlockSpec(memory_space=pltpu.VMEM)


def call(body, name, small, large, out_shape, flops, scratch=(), space=pltpu.VMEM):
    operands = (*small, *large)
    moved = sum(array.size * array.dtype.itemsize for array in (*operands, *jax.tree.leaves(out_shape)))
    kept = sum(math.prod(array.shape) * 4 for array in scratch)
    return pl.pallas_call(
        body,
        out_shape=out_shape,
        in_specs=[smem()] * len(small) + [pl.BlockSpec(memory_space=space)] * len(large),
        out_specs=jax.tree.map(lambda _: vmem(), out_shape),
        scratch_shapes=list(scratch),
        compiler_params=pltpu.CompilerParams(vmem_limit_bytes=moved + kept + SPARE_VMEM),
        cost_estimate=pl.CostEstimate(flops=flops, bytes_accessed=moved, transcendentals=0),
        name=name,
    )(*operands)


def on_device(item_factors, ratings, block_ids, live_counts, owner_rows):
    item_local, width = item_factors.shape
    users_here, columns = ratings.shape
    batch_count, slot_count = block_ids.shape
    batch_rows = users_here // batch_count
    block_size = columns // slot_count
    panel_count = lax.axis_size("blk")
    rep_count = lax.axis_size("rep")
    device_count = rep_count * panel_count
    quota = users_here // device_count
    chips = panel_count // 2
    per_panel = slot_count // panel_count
    blocks = item_local // block_size
    part_rows = block_size // rep_count
    span = 2 * per_panel * block_size
    rep = lax.axis_index("rep")

    def over_blk(array, target):
        return lax.ppermute(array, "blk", [(b, target(b)) for b in range(panel_count)])

    def over_rep(array, part):
        return lax.ppermute(array, "rep", [(r, r ^ part) for r in range(rep_count)])

    def other_core(array):
        return over_blk(array, lambda b: b ^ 1)

    whole = item_factors.reshape(blocks, block_size, width)
    piece = lax.dynamic_slice(whole, (0, rep * part_rows, 0), (blocks, part_rows, width))

    after = lax.optimization_barrier
    other_whole = other_core(whole)
    pieces = {0: piece}
    for hop in (1, chips - 1):
        pieces[hop] = over_blk(piece, lambda b: (b + 2 * hop) % panel_count)
    other_whole, wanted = after((other_whole, block_ids))
    ids = [wanted] + [over_rep(wanted, part) for part in range(1, rep_count)]

    gram_rows = width // rep_count
    gram = sum(
        dot32(lax.dynamic_slice(panel, (0, rep * gram_rows), (item_local, gram_rows)), panel, ((0,), (0,)))
        for panel in (item_factors, other_whole.reshape(item_local, width))
    )
    pieces[chips - 1], _ = after((pieces[chips - 1], ids))
    pieces[1], ids, gram = after((pieces[1], ids, gram))
    for k in range(2, chips - 1):
        pieces[k] = over_blk(pieces[k - 1], lambda b: (b + 2) % panel_count)

    before = (jnp.arange(users_here)[:, None] < jnp.arange(users_here)[None, :]).astype(jnp.bfloat16)
    target_dev = owner_rows // users_here
    goes = target_dev[None, :] == jnp.arange(device_count)[:, None]
    goes_rank = dot32(goes.astype(jnp.bfloat16), before).astype(jnp.int32)
    sent = goes[:, None, :] & (goes_rank[:, None, :] == jnp.arange(quota)[None, :, None])
    slots = jnp.sum(jnp.where(sent, (owner_rows % users_here)[None, None, :], 0), axis=2)
    slots = jnp.pad(slots.astype(jnp.float32), ((0, 0), (0, LANES - quota)))[:, None, :]
    place = jnp.stack([target_dev, width * jnp.sum(jnp.where(goes, goes_rank, 0), axis=0)])

    def table_shape(steps):
        rows = len(steps) * span
        return (
            jax.ShapeDtypeStruct((batch_count, rows, width), jnp.bfloat16),
            jax.ShapeDtypeStruct((batch_count, width, rows), jnp.bfloat16),
        )

    near_first = sorted(range(1, chips), key=lambda k: min(k, chips - k))
    stages = [near_first[i:i + 2] for i in range(0, chips - 1, 2)]
    chosen, tables = None, []
    for steps in stages:
        pairs = []
        if chosen is not None:
            parts = [chosen[0]] + [over_rep(chosen[part], part) for part in range(1, rep_count)]
        if steps is stages[1]:
            chosen, home, gram = after((chosen, other_whole, gram))
            gram = gram + over_blk(gram, lambda b: b ^ 2)
            tables = [call(
                functools.partial(pick_kernel, chips, batch_count, per_panel), "pick",
                [block_ids], [whole, home], table_shape([0]), 1 << 20,
            )]
        for k in steps:
            piece = pieces[k]
            if chosen is not None:
                piece, parts[1:3], tables[0] = after((piece, parts[1:3], tables[0]))
            pairs += [piece, other_core(piece)]
        if chosen is not None:
            tables.append(call(
                functools.partial(join_kernel, rep_count, held, batch_count, per_panel), "join",
                [], parts, table_shape(held), 1 << 20,
            ))
        last = steps is stages[-1]
        bit = 4
        while last and bit < panel_count:
            gram = gram + over_blk(gram, lambda b: b ^ bit)
            bit *= 2
        count = len(steps) * batch_count * 2 * per_panel + last * (2 * gram_rows // part_rows)
        picked = jax.ShapeDtypeStruct((count, part_rows, width), jnp.bfloat16)
        chosen = call(
            functools.partial(select_kernel, chips, rep_count, steps, batch_count, per_panel), "select",
            ids, pairs + [gram] * last, (picked,) * rep_count, 1 << 20,
        )
        held = steps
    parts = [chosen[0]] + [over_rep(chosen[part], part) for part in range(1, rep_count)]
    grams = (jax.ShapeDtypeStruct((width, width), jnp.bfloat16),) * 2
    *table, gram_high, gram_low = call(
        functools.partial(join_kernel, rep_count, held, batch_count, per_panel), "join",
        [], parts, table_shape(held) + grams, 1 << 20,
    )
    tables.append(table)
    rows_list, cols_list = [table[0] for table in tables], [table[1] for table in tables]

    lanes = quota * width + LANES
    last_columns = rows_list[-1].shape[1]
    per_batch = functools.partial(jax.ShapeDtypeStruct, dtype=jnp.float32)
    weight, last_targets, partial = call(
        functools.partial(weigh_kernel, chips, [0] + near_first, block_size, batch_count), "weigh",
        [live_counts], [ratings, *rows_list[:-1]],
        (
            per_batch((batch_count, batch_rows, columns)),
            jax.ShapeDtypeStruct((batch_count, 2 * batch_rows, last_columns), jnp.bfloat16),
            per_batch((batch_count, batch_rows, width)),
        ),
        4 * users_here * columns * width,
        [pltpu.VMEM((batch_count, 2 * batch_rows, columns - last_columns), jnp.bfloat16)],
    )
    state = pltpu.VMEM((batch_count, batch_rows, width), jnp.float32)
    send_rows = call(
        functools.partial(solve_kernel, batch_rows, batch_count), "solve",
        [place], [slots, gram_high, gram_low, weight, last_targets, partial, *rows_list, *cols_list],
        jax.ShapeDtypeStruct((device_count, 1, lanes), jnp.float32),
        8 * 4 * users_here * columns * width,
        [
            pltpu.VMEM((batch_count, 2 * batch_rows, columns), jnp.bfloat16),
            state, state, state, pltpu.VMEM((batch_count, batch_rows, 1), jnp.float32),
        ],
    )
    got_rows = lax.all_to_all(send_rows, ("rep", "blk"), split_axis=0, concat_axis=0, tiled=True)
    return call(
        place_kernel, "place", [], [got_rows],
        jax.ShapeDtypeStruct((users_here, width), jnp.float32), 1 << 20,
        [
            pltpu.VMEM((device_count, 1, quota * width), jnp.float32),
            pltpu.SMEM((device_count, 1, LANES), jnp.float32), pltpu.SemaphoreType.DMA((2,)),
        ],
        pl.ANY,
    )


def solution(mesh):
    placed = (
        P("blk", None),
        P(("rep", "blk"), None),
        P(("rep", "blk"), None),
        P(("rep", "blk")),
        P(("rep", "blk")),
    )
    return jax.shard_map(
        on_device, mesh=mesh, in_specs=placed, out_specs=P(("rep", "blk"), None), check_vma=False
    )
```

```python
import functools
import math
import jax
import jax.numpy as jnp
from jax import lax
from jax.experimental import pallas as pl
from jax.experimental.pallas import tpu as pltpu
from jax.sharding import PartitionSpec as P

ITERS = 8
WIDE_ITERS = 1
TILE = 256
LANES = 128
SPARE_VMEM = 6 * 1024 * 1024

conf_scale = 6.0
ridge_term = 0.5


def dot32(left, right, dims=((1,), (0,))):
    return lax.dot_general(left, right, (dims, ((), ())), preferred_element_type=jnp.float32)


def halves(value):
    high = value.astype(jnp.bfloat16)
    low = (value - high.astype(jnp.float32)).astype(jnp.bfloat16)
    return high, low


def local_slots(core, per_panel):
    for side in range(2):
        parity = core if side == 0 else 1 - core
        for pick in range(per_panel):
            yield side, parity * per_panel + pick


def position(chips, back):
    blk = lax.axis_index("blk")
    return lax.rem(blk, 2), lax.rem(lax.div(blk, 2) + chips - back, chips)


def select_kernel(chips, reps, steps, batch_count, per_panel, *refs):
    ids_refs, refs = refs[:reps], refs[reps:]
    panel_refs, refs = refs[:2 * len(steps)], refs[2 * len(steps):]
    gram_refs = [ref for ref in refs if ref.dtype == jnp.float32]
    out_refs = refs[len(gram_refs):]
    slots = 2 * per_panel
    blocks, size, _ = panel_refs[0].shape
    named = batch_count * slots
    for ids_ref, out_ref in zip(ids_refs, out_refs):
        for i, back in enumerate(steps):
            core, chip = position(chips, back)
            for batch in range(batch_count):
                for side, local in local_slots(core, per_panel):
                    block = ids_ref[batch, chip * slots + local]
                    out_ref[i * named + batch * slots + local] = panel_refs[2 * i + side][lax.rem(block, blocks)]
        for gram_ref in gram_refs:
            gram = jnp.concatenate(halves(gram_ref[...]), axis=0)
            out_ref[len(steps) * named:] = gram.reshape(-1, size, gram.shape[1])


def join_kernel(reps, steps, batch_count, per_panel, *refs):
    part_refs, (rows_ref, cols_ref, *gram_refs) = refs[:reps], refs[reps:]
    rep = lax.axis_index("rep")
    size = part_refs[0].shape[1]
    slots = 2 * per_panel
    named = batch_count * slots
    for part, ref in enumerate(part_refs):
        for i in range(len(steps)):
            for batch in range(batch_count):
                for local in range(slots):
                    offset = (i * slots + local) * reps * size + (rep ^ part) * size
                    rows_ref[batch, pl.ds(pl.multiple_of(offset, size), size), :] = ref[
                        i * named + batch * slots + local
                    ]
        extra = ref.shape[0] - len(steps) * named
        half = extra // 2
        for i, gram_ref in enumerate(gram_refs):
            start = len(steps) * named + i * half
            offset = pl.multiple_of((rep ^ part) * size * half, size * half)
            gram_ref[pl.ds(offset, size * half), :] = ref[start:start + half].reshape(size * half, ref.shape[2])
    for batch in range(batch_count):
        cols_ref[batch] = rows_ref[batch].T


def pick_kernel(chips, batch_count, per_panel, ids_ref, own_ref, other_ref, rows_ref, cols_ref):
    core, chip = position(chips, 0)
    slots = 2 * per_panel
    blocks, block_size, _ = own_ref.shape
    for batch in range(batch_count):
        for side, local in local_slots(core, per_panel):
            block = ids_ref[batch, chip * slots + local]
            held = other_ref if side else own_ref
            offset = pl.multiple_of(local * block_size, block_size)
            rows_ref[batch, pl.ds(offset, block_size), :] = held[lax.rem(block, blocks)]
        cols_ref[batch] = rows_ref[batch].T


def weigh_kernel(chips, steps, block_size, batch_count, *refs):
    live_ref, ratings_ref = refs[:2]
    rows_refs, (weight, last, partial, early) = refs[2:-4], refs[-4:]
    users = ratings_ref.shape[0] // batch_count
    columns = ratings_ref.shape[1]
    span = columns // chips
    first_last = columns - last.shape[2]
    for column in range(0, columns, TILE):
        _, chip = position(chips, steps[column // span])
        start = pl.multiple_of(chip * span + column % span, TILE)
        index = start + lax.broadcasted_iota(jnp.int32, (users, TILE), 1)
        for batch in range(batch_count):
            rated = ratings_ref[batch * users:(batch + 1) * users, pl.ds(start, TILE)].astype(jnp.float32)
            live = index < live_ref[batch] * block_size
            scaled = jnp.where(live, conf_scale * rated, 0.0)
            weight[batch, :, column:column + TILE] = scaled
            high, low = halves(jnp.where(live, 1.0 + scaled, 0.0))
            target, at = (early, column) if column < first_last else (last, column - first_last)
            target[batch, :users, at:at + TILE] = high
            target[batch, users:, at:at + TILE] = low
    for batch in range(batch_count):
        total, start = None, 0
        for ref in rows_refs:
            term = dot32(early[batch, :, start:start + ref.shape[1]], ref[batch])
            total = term if total is None else total + term
            start += ref.shape[1]
        partial[batch] = total[:users] + total[users:]


def solve_kernel(users, batch_count, *refs):
    place_ref, slots_ref, gram_high, gram_low, weight, last, partial = refs[:7]
    refs = refs[7:]
    tables = (len(refs) - 6) // 2
    rows_refs, cols_refs, refs = refs[:tables], refs[tables:2 * tables], refs[2 * tables:]
    send_ref, back, x_s, r_s, p_s, n_s = refs
    batches = range(batch_count)
    tiles, starts = [], []
    for table, ref in enumerate(rows_refs):
        start = sum(other.shape[1] for other in rows_refs[:table])
        starts.append(start)
        tiles += [(table, first, start + first) for first in range(0, ref.shape[1], TILE)]

    def back_dot(batch, rows):
        total = None
        for table, start in enumerate(starts):
            size = rows_refs[table].shape[1]
            term = dot32(back[batch, :rows, start:start + size], rows_refs[table][batch])
            total = term if total is None else total + term
        return total

    def put_halves(batch, column, value):
        high, low = halves(value)
        back[batch, :users, column:column + TILE] = high
        back[batch, users:, column:column + TILE] = low

    for batch in batches:
        total = dot32(last[batch], rows_refs[-1][batch])
        target_proj = partial[batch] + total[:users] + total[users:]
        x_s[batch] = jnp.zeros_like(target_proj)
        r_s[batch] = target_proj
        p_s[batch] = target_proj
        n_s[batch] = jnp.sum(target_proj * target_proj, axis=1, keepdims=True)

    def advance(batch, wide, final):
        direction = p_s[batch]
        high, low = halves(direction)
        both = jnp.concatenate([high, low], axis=0)
        for table, first, column in tiles:
            projected = dot32(both if wide else high, cols_refs[table][batch, :, first:first + TILE])
            if wide:
                projected = projected[:users] + projected[users:]
            projected = projected * weight[batch, :, column:column + TILE]
            if wide:
                put_halves(batch, column, projected)
            else:
                back[batch, :users, column:column + TILE] = projected.astype(jnp.bfloat16)
        gram_part = dot32(both, gram_high[...])
        image = gram_part[:users] + gram_part[users:] + dot32(high, gram_low[...]) + ridge_term * direction
        total = back_dot(batch, 2 * users if wide else users)
        if wide:
            total = total[:users] + total[users:]
        image = image + total
        norm_now = n_s[batch]
        step_size = norm_now / jnp.sum(direction * image, axis=1, keepdims=True)
        x_s[batch] = x_s[batch] + step_size * direction
        if final:
            return
        residual = r_s[batch] - step_size * image
        r_s[batch] = residual
        norm_next = jnp.sum(residual * residual, axis=1, keepdims=True)
        p_s[batch] = residual + norm_next / norm_now * direction
        n_s[batch] = norm_next

    for iteration in range(ITERS):
        for batch in batches:
            advance(batch, iteration < WIDE_ITERS, iteration == ITERS - 1)
    width = x_s.shape[2]
    quota = batch_count * users // send_ref.shape[0]
    send_ref[:, :, quota * width:] = slots_ref[...]
    for batch in batches:
        for user in range(users):
            row = batch * users + user
            lanes = pl.ds(pl.multiple_of(place_ref[1, row], width), width)
            send_ref[place_ref[0, row], :, lanes] = x_s[batch, user:user + 1, :]


def place_kernel(got_ref, out_ref, as_integers, slots, sem):
    width = out_ref.shape[1]
    quota = out_ref.shape[0] // got_ref.shape[0]
    as_integers[...] = got_ref[:, :, quota * width:].astype(jnp.int32)
    copy = pltpu.make_async_copy(as_integers, slots, sem)
    copy.start()
    copy.wait()
    for source in range(got_ref.shape[0]):
        for row in range(quota):
            out_ref[pl.ds(slots[source, 0, row], 1), :] = got_ref[source, :, row * width:(row + 1) * width]


def smem():
    return pl.BlockSpec(memory_space=pltpu.SMEM)


def vmem():
    return pl.BlockSpec(memory_space=pltpu.VMEM)


def call(body, name, small, large, out_shape, flops, scratch=()):
    operands = (*small, *large)
    moved = sum(array.size * array.dtype.itemsize for array in (*operands, *jax.tree.leaves(out_shape)))
    kept = sum(math.prod(array.shape) * 4 for array in scratch if hasattr(array, "shape"))
    return pl.pallas_call(
        body,
        out_shape=out_shape,
        in_specs=[smem()] * len(small) + [vmem()] * len(large),
        out_specs=jax.tree.map(lambda _: vmem(), out_shape),
        scratch_shapes=list(scratch),
        compiler_params=pltpu.CompilerParams(vmem_limit_bytes=moved + kept + SPARE_VMEM),
        cost_estimate=pl.CostEstimate(flops=flops, bytes_accessed=moved, transcendentals=0),
        name=name,
    )(*operands)


def on_device(item_factors, ratings, block_ids, live_counts, owner_rows):
    item_local, width = item_factors.shape
    users_here, columns = ratings.shape
    batch_count, slot_count = block_ids.shape
    batch_rows = users_here // batch_count
    block_size = columns // slot_count
    panel_count = lax.axis_size("blk")
    rep_count = lax.axis_size("rep")
    device_count = rep_count * panel_count
    quota = users_here // device_count
    chips = panel_count // 2
    per_panel = slot_count // panel_count
    blocks = item_local // block_size
    part_rows = block_size // rep_count
    span = 2 * per_panel * block_size
    rep = lax.axis_index("rep")

    def over_blk(array, target):
        return lax.ppermute(array, "blk", [(b, target(b)) for b in range(panel_count)])

    def over_rep(array, part):
        return lax.ppermute(array, "rep", [(r, r ^ part) for r in range(rep_count)])

    def other_core(array):
        return over_blk(array, lambda b: b ^ 1)

    whole = item_factors.reshape(blocks, block_size, width)
    piece = lax.dynamic_slice(whole, (0, rep * part_rows, 0), (blocks, part_rows, width))

    after = lax.optimization_barrier
    whole, piece = after((whole, piece))
    other_whole = other_core(whole)
    pieces = {0: piece}
    for hop in (1, chips - 1):
        pieces[hop] = over_blk(piece, lambda b: (b + 2 * hop) % panel_count)
    other_whole, wanted = after((other_whole, block_ids))
    ids = [wanted] + [over_rep(wanted, part) for part in range(1, rep_count)]

    gram_rows = width // rep_count
    gram = sum(
        dot32(lax.dynamic_slice(panel, (0, rep * gram_rows), (item_local, gram_rows)), panel, ((0,), (0,)))
        for panel in (item_factors, other_whole.reshape(item_local, width))
    )
    pieces[chips - 1], _ = after((pieces[chips - 1], ids))
    ids, gram = after((ids, gram))
    gram = gram + over_blk(gram, lambda b: b ^ 2)
    pieces[1], gram = after((pieces[1], gram))
    for k in range(2, chips - 1):
        pieces[k] = over_blk(pieces[k - 1], lambda b: (b + 2) % panel_count)

    before = (jnp.arange(users_here)[:, None] < jnp.arange(users_here)[None, :]).astype(jnp.bfloat16)
    target_dev = owner_rows // users_here
    goes = target_dev[None, :] == jnp.arange(device_count)[:, None]
    goes_rank = dot32(goes.astype(jnp.bfloat16), before).astype(jnp.int32)
    sent = goes[:, None, :] & (goes_rank[:, None, :] == jnp.arange(quota)[None, :, None])
    slots = jnp.sum(jnp.where(sent, (owner_rows % users_here)[None, None, :], 0), axis=2)
    slots = jnp.pad(slots.astype(jnp.float32), ((0, 0), (0, LANES - quota)))[:, None, :]
    place = jnp.stack([target_dev, width * jnp.sum(jnp.where(goes, goes_rank, 0), axis=0)])

    def table_shape(steps):
        rows = len(steps) * span
        return (
            jax.ShapeDtypeStruct((batch_count, rows, width), jnp.bfloat16),
            jax.ShapeDtypeStruct((batch_count, width, rows), jnp.bfloat16),
        )

    near_first = sorted(range(1, chips), key=lambda k: min(k, chips - k))
    stages = [near_first[i:i + 2] for i in range(0, chips - 1, 2)]
    chosen, tables = None, []
    for steps in stages:
        pairs = []
        if chosen is not None:
            parts = [chosen[0]] + [over_rep(chosen[part], part) for part in range(1, rep_count)]
        if steps is stages[1]:
            chosen, home, gram = after((chosen, other_whole, gram))
            bit = 4
            while bit < panel_count:
                gram = gram + over_blk(gram, lambda b: b ^ bit)
                bit *= 2
            tables = [call(
                functools.partial(pick_kernel, chips, batch_count, per_panel), "pick",
                [block_ids], [whole, home], table_shape([0]), 1 << 20,
            )]
        for k in steps:
            piece = pieces[k]
            if chosen is not None:
                piece, parts[1:3], tables[0], gram = after((piece, parts[1:3], tables[0], gram))
            pairs += [piece, other_core(piece)]
        if chosen is not None:
            tables.append(call(
                functools.partial(join_kernel, rep_count, held, batch_count, per_panel), "join",
                [], parts, table_shape(held), 1 << 20,
            ))
        last = steps is stages[-1]
        count = len(steps) * batch_count * 2 * per_panel + last * (2 * gram_rows // part_rows)
        picked = jax.ShapeDtypeStruct((count, part_rows, width), jnp.bfloat16)
        chosen = call(
            functools.partial(select_kernel, chips, rep_count, steps, batch_count, per_panel), "select",
            ids, pairs + [gram] * last, (picked,) * rep_count, 1 << 20,
        )
        held = steps
    parts = [chosen[0]] + [over_rep(chosen[part], part) for part in range(1, rep_count)]
    grams = (jax.ShapeDtypeStruct((width, width), jnp.bfloat16),) * 2
    *table, gram_high, gram_low = call(
        functools.partial(join_kernel, rep_count, held, batch_count, per_panel), "join",
        [], parts, table_shape(held) + grams, 1 << 20,
    )
    tables.append(table)
    rows_list, cols_list = [table[0] for table in tables], [table[1] for table in tables]

    lanes = quota * width + LANES
    last_columns = rows_list[-1].shape[1]
    per_batch = functools.partial(jax.ShapeDtypeStruct, dtype=jnp.float32)
    weight, last_targets, partial = call(
        functools.partial(weigh_kernel, chips, [0] + near_first, block_size, batch_count), "weigh",
        [live_counts], [ratings, *rows_list[:-1]],
        (
            per_batch((batch_count, batch_rows, columns)),
            jax.ShapeDtypeStruct((batch_count, 2 * batch_rows, last_columns), jnp.bfloat16),
            per_batch((batch_count, batch_rows, width)),
        ),
        4 * users_here * columns * width,
        [pltpu.VMEM((batch_count, 2 * batch_rows, columns - last_columns), jnp.bfloat16)],
    )
    state = pltpu.VMEM((batch_count, batch_rows, width), jnp.float32)
    send_rows = call(
        functools.partial(solve_kernel, batch_rows, batch_count), "solve",
        [place], [slots, gram_high, gram_low, weight, last_targets, partial, *rows_list, *cols_list],
        jax.ShapeDtypeStruct((device_count, 1, lanes), jnp.float32),
        8 * 4 * users_here * columns * width,
        [
            pltpu.VMEM((batch_count, 2 * batch_rows, columns), jnp.bfloat16),
            state, state, state, pltpu.VMEM((batch_count, batch_rows, 1), jnp.float32),
        ],
    )
    got_rows = lax.all_to_all(send_rows, ("rep", "blk"), split_axis=0, concat_axis=0, tiled=True)
    return call(
        place_kernel, "place", [], [got_rows],
        jax.ShapeDtypeStruct((users_here, width), jnp.float32), 1 << 20,
        [
            pltpu.VMEM((device_count, 1, LANES), jnp.int32),
            pltpu.SMEM((device_count, 1, LANES), jnp.int32), pltpu.SemaphoreType.DMA,
        ],
    )


def solution(mesh):
    placed = (
        P("blk", None),
        P(("rep", "blk"), None),
        P(("rep", "blk"), None),
        P(("rep", "blk")),
        P(("rep", "blk")),
    )
    return jax.shard_map(
        on_device, mesh=mesh, in_specs=placed, out_specs=P(("rep", "blk"), None), check_vma=False
    )
```

```python
import functools
import math
import jax
import jax.numpy as jnp
from jax import lax
from jax.experimental import pallas as pl
from jax.experimental.pallas import tpu as pltpu
from jax.sharding import PartitionSpec as P

ITERS = 8
WIDE_ITERS = 1
TILE = 256
LANES = 128
SPARE_VMEM = 6 * 1024 * 1024

conf_scale = 6.0
ridge_term = 0.5


def dot32(left, right, dims=((1,), (0,))):
    return lax.dot_general(left, right, (dims, ((), ())), preferred_element_type=jnp.float32)


def halves(value):
    high = value.astype(jnp.bfloat16)
    low = (value - high.astype(jnp.float32)).astype(jnp.bfloat16)
    return high, low


def local_slots(core, per_panel):
    for side in range(2):
        parity = core if side == 0 else 1 - core
        for pick in range(per_panel):
            yield side, parity * per_panel + pick


def position(chips, back):
    blk = lax.axis_index("blk")
    return lax.rem(blk, 2), lax.rem(lax.div(blk, 2) + chips - back, chips)


def select_kernel(chips, reps, steps, batch_count, per_panel, *refs):
    ids_refs, refs = refs[:reps], refs[reps:]
    panel_refs, refs = refs[:2 * len(steps)], refs[2 * len(steps):]
    gram_refs = [ref for ref in refs if ref.dtype == jnp.float32]
    out_refs = refs[len(gram_refs):]
    slots = 2 * per_panel
    blocks, size, _ = panel_refs[0].shape
    named = batch_count * slots
    for ids_ref, out_ref in zip(ids_refs, out_refs):
        for i, back in enumerate(steps):
            core, chip = position(chips, back)
            for batch in range(batch_count):
                for side, local in local_slots(core, per_panel):
                    block = ids_ref[batch, chip * slots + local]
                    out_ref[i * named + batch * slots + local] = panel_refs[2 * i + side][lax.rem(block, blocks)]
        for gram_ref in gram_refs:
            gram = jnp.concatenate(halves(gram_ref[...]), axis=0)
            out_ref[len(steps) * named:] = gram.reshape(-1, size, gram.shape[1])


def join_kernel(reps, steps, batch_count, per_panel, *refs):
    part_refs, (rows_ref, cols_ref, *gram_refs) = refs[:reps], refs[reps:]
    rep = lax.axis_index("rep")
    size = part_refs[0].shape[1]
    slots = 2 * per_panel
    named = batch_count * slots
    for part, ref in enumerate(part_refs):
        for i in range(len(steps)):
            for batch in range(batch_count):
                for local in range(slots):
                    offset = (i * slots + local) * reps * size + (rep ^ part) * size
                    rows_ref[batch, pl.ds(pl.multiple_of(offset, size), size), :] = ref[
                        i * named + batch * slots + local
                    ]
        extra = ref.shape[0] - len(steps) * named
        half = extra // 2
        for i, gram_ref in enumerate(gram_refs):
            start = len(steps) * named + i * half
            offset = pl.multiple_of((rep ^ part) * size * half, size * half)
            gram_ref[pl.ds(offset, size * half), :] = ref[start:start + half].reshape(size * half, ref.shape[2])
    for batch in range(batch_count):
        cols_ref[batch] = rows_ref[batch].T


def pick_kernel(chips, batch_count, per_panel, ids_ref, own_ref, other_ref, rows_ref, cols_ref):
    core, chip = position(chips, 0)
    slots = 2 * per_panel
    blocks, block_size, _ = own_ref.shape
    for batch in range(batch_count):
        for side, local in local_slots(core, per_panel):
            block = ids_ref[batch, chip * slots + local]
            held = other_ref if side else own_ref
            offset = pl.multiple_of(local * block_size, block_size)
            rows_ref[batch, pl.ds(offset, block_size), :] = held[lax.rem(block, blocks)]
        cols_ref[batch] = rows_ref[batch].T


def weigh_kernel(chips, steps, block_size, batch_count, *refs):
    live_ref, ratings_ref = refs[:2]
    rows_refs, (weight, last, partial, early) = refs[2:-4], refs[-4:]
    users = ratings_ref.shape[0] // batch_count
    columns = ratings_ref.shape[1]
    span = columns // chips
    first_last = columns - last.shape[2]
    for column in range(0, columns, TILE):
        _, chip = position(chips, steps[column // span])
        start = pl.multiple_of(chip * span + column % span, TILE)
        index = start + lax.broadcasted_iota(jnp.int32, (users, TILE), 1)
        for batch in range(batch_count):
            rated = ratings_ref[batch * users:(batch + 1) * users, pl.ds(start, TILE)].astype(jnp.float32)
            live = index < live_ref[batch] * block_size
            scaled = jnp.where(live, conf_scale * rated, 0.0)
            weight[batch, :, column:column + TILE] = scaled
            high, low = halves(jnp.where(live, 1.0 + scaled, 0.0))
            target, at = (early, column) if column < first_last else (last, column - first_last)
            target[batch, :users, at:at + TILE] = high
            target[batch, users:, at:at + TILE] = low
    for batch in range(batch_count):
        total, start = None, 0
        for ref in rows_refs:
            term = dot32(early[batch, :, start:start + ref.shape[1]], ref[batch])
            total = term if total is None else total + term
            start += ref.shape[1]
        partial[batch] = total[:users] + total[users:]


def solve_kernel(users, batch_count, *refs):
    place_ref, slots_ref, gram_high, gram_low, weight, last, partial = refs[:7]
    refs = refs[7:]
    tables = (len(refs) - 6) // 2
    rows_refs, cols_refs, refs = refs[:tables], refs[tables:2 * tables], refs[2 * tables:]
    send_ref, back, x_s, r_s, p_s, n_s = refs
    batches = range(batch_count)
    tiles, starts = [], []
    for table, ref in enumerate(rows_refs):
        start = sum(other.shape[1] for other in rows_refs[:table])
        starts.append(start)
        tiles += [(table, first, start + first) for first in range(0, ref.shape[1], TILE)]

    def back_dot(batch, rows):
        total = None
        for table, start in enumerate(starts):
            size = rows_refs[table].shape[1]
            term = dot32(back[batch, :rows, start:start + size], rows_refs[table][batch])
            total = term if total is None else total + term
        return total

    def put_halves(batch, column, value):
        high, low = halves(value)
        back[batch, :users, column:column + TILE] = high
        back[batch, users:, column:column + TILE] = low

    for batch in batches:
        total = dot32(last[batch], rows_refs[-1][batch])
        target_proj = partial[batch] + total[:users] + total[users:]
        x_s[batch] = jnp.zeros_like(target_proj)
        r_s[batch] = target_proj
        p_s[batch] = target_proj
        n_s[batch] = jnp.sum(target_proj * target_proj, axis=1, keepdims=True)

    def advance(batch, wide, final):
        direction = p_s[batch]
        high, low = halves(direction)
        both = jnp.concatenate([high, low], axis=0)
        for table, first, column in tiles:
            projected = dot32(both if wide else high, cols_refs[table][batch, :, first:first + TILE])
            if wide:
                projected = projected[:users] + projected[users:]
            projected = projected * weight[batch, :, column:column + TILE]
            if wide:
                put_halves(batch, column, projected)
            else:
                back[batch, :users, column:column + TILE] = projected.astype(jnp.bfloat16)
        gram_part = dot32(both, gram_high[...])
        image = gram_part[:users] + gram_part[users:] + dot32(high, gram_low[...]) + ridge_term * direction
        total = back_dot(batch, 2 * users if wide else users)
        if wide:
            total = total[:users] + total[users:]
        image = image + total
        norm_now = n_s[batch]
        step_size = norm_now / jnp.sum(direction * image, axis=1, keepdims=True)
        x_s[batch] = x_s[batch] + step_size * direction
        if final:
            return
        residual = r_s[batch] - step_size * image
        r_s[batch] = residual
        norm_next = jnp.sum(residual * residual, axis=1, keepdims=True)
        p_s[batch] = residual + norm_next / norm_now * direction
        n_s[batch] = norm_next

    width = x_s.shape[2]
    quota = batch_count * users // send_ref.shape[0]
    send_ref[:, :, quota * width:] = slots_ref[...]
    for iteration in range(ITERS):
        for batch in batches:
            advance(batch, iteration < WIDE_ITERS, iteration == ITERS - 1)
            for user in range(users if iteration == ITERS - 1 else 0):
                row = batch * users + user
                lanes = pl.ds(pl.multiple_of(place_ref[1, row], width), width)
                send_ref[place_ref[0, row], :, lanes] = x_s[batch, user:user + 1, :]


def place_kernel(got_ref, out_ref, as_integers, slots, sem):
    width = out_ref.shape[1]
    quota = out_ref.shape[0] // got_ref.shape[0]
    as_integers[...] = got_ref[:, :, quota * width:].astype(jnp.int32)
    copy = pltpu.make_async_copy(as_integers, slots, sem)
    copy.start()
    copy.wait()
    for source in range(got_ref.shape[0]):
        for row in range(quota):
            out_ref[pl.ds(slots[source, 0, row], 1), :] = got_ref[source, :, row * width:(row + 1) * width]


def smem():
    return pl.BlockSpec(memory_space=pltpu.SMEM)


def vmem():
    return pl.BlockSpec(memory_space=pltpu.VMEM)


def call(body, name, small, large, out_shape, flops, scratch=()):
    operands = (*small, *large)
    moved = sum(array.size * array.dtype.itemsize for array in (*operands, *jax.tree.leaves(out_shape)))
    kept = sum(math.prod(array.shape) * 4 for array in scratch if hasattr(array, "shape"))
    return pl.pallas_call(
        body,
        out_shape=out_shape,
        in_specs=[smem()] * len(small) + [vmem()] * len(large),
        out_specs=jax.tree.map(lambda _: vmem(), out_shape),
        scratch_shapes=list(scratch),
        compiler_params=pltpu.CompilerParams(vmem_limit_bytes=moved + kept + SPARE_VMEM),
        cost_estimate=pl.CostEstimate(flops=flops, bytes_accessed=moved, transcendentals=0),
        name=name,
    )(*operands)


def on_device(item_factors, ratings, block_ids, live_counts, owner_rows):
    item_local, width = item_factors.shape
    users_here, columns = ratings.shape
    batch_count, slot_count = block_ids.shape
    batch_rows = users_here // batch_count
    block_size = columns // slot_count
    panel_count = lax.axis_size("blk")
    rep_count = lax.axis_size("rep")
    device_count = rep_count * panel_count
    quota = users_here // device_count
    chips = panel_count // 2
    per_panel = slot_count // panel_count
    blocks = item_local // block_size
    part_rows = block_size // rep_count
    span = 2 * per_panel * block_size
    rep = lax.axis_index("rep")

    def over_blk(array, target):
        return lax.ppermute(array, "blk", [(b, target(b)) for b in range(panel_count)])

    def over_rep(array, part):
        return lax.ppermute(array, "rep", [(r, r ^ part) for r in range(rep_count)])

    def other_core(array):
        return over_blk(array, lambda b: b ^ 1)

    whole = item_factors.reshape(blocks, block_size, width)
    piece = lax.dynamic_slice(whole, (0, rep * part_rows, 0), (blocks, part_rows, width))

    after = lax.optimization_barrier
    whole, piece = after((whole, piece))
    other_whole = other_core(whole)
    pieces = {0: piece}
    for hop in (1, chips - 1):
        pieces[hop] = over_blk(piece, lambda b: (b + 2 * hop) % panel_count)
    other_whole, wanted = after((other_whole, block_ids))
    ids = [wanted] + [over_rep(wanted, part) for part in range(1, rep_count)]

    gram_rows = width // rep_count
    gram = sum(
        dot32(lax.dynamic_slice(panel, (0, rep * gram_rows), (item_local, gram_rows)), panel, ((0,), (0,)))
        for panel in (item_factors, other_whole.reshape(item_local, width))
    )
    pieces[chips - 1], _ = after((pieces[chips - 1], ids))
    ids, gram = after((ids, gram))
    gram = gram + over_blk(gram, lambda b: b ^ 2)
    pieces[1], gram = after((pieces[1], gram))
    for k in range(2, chips - 1):
        pieces[k] = over_blk(pieces[k - 1], lambda b: (b + 2) % panel_count)

    before = (jnp.arange(users_here)[:, None] < jnp.arange(users_here)[None, :]).astype(jnp.bfloat16)
    target_dev = owner_rows // users_here
    goes = target_dev[None, :] == jnp.arange(device_count)[:, None]
    goes_rank = dot32(goes.astype(jnp.bfloat16), before).astype(jnp.int32)
    sent = goes[:, None, :] & (goes_rank[:, None, :] == jnp.arange(quota)[None, :, None])
    slots = jnp.sum(jnp.where(sent, (owner_rows % users_here)[None, None, :], 0), axis=2)
    slots = jnp.pad(slots.astype(jnp.float32), ((0, 0), (0, LANES - quota)))[:, None, :]
    place = jnp.stack([target_dev, width * jnp.sum(jnp.where(goes, goes_rank, 0), axis=0)])

    def table_shape(steps):
        rows = len(steps) * span
        return (
            jax.ShapeDtypeStruct((batch_count, rows, width), jnp.bfloat16),
            jax.ShapeDtypeStruct((batch_count, width, rows), jnp.bfloat16),
        )

    near_first = sorted(range(1, chips), key=lambda k: min(k, chips - k))
    stages = [near_first[i:i + 2] for i in range(0, chips - 1, 2)]
    chosen, tables = None, []
    for steps in stages:
        pairs = []
        if steps is stages[1]:
            chosen, home, gram = after((chosen, other_whole, gram))
            bit = 4
            while bit < panel_count:
                gram = gram + over_blk(gram, lambda b: b ^ bit)
                bit *= 2
            chosen = list(chosen)
            chosen[-1], gram = after((chosen[-1], gram))
        if chosen is not None:
            parts = [chosen[0]] + [over_rep(chosen[part], part) for part in range(1, rep_count)]
        if steps is stages[1]:
            tables = [call(
                functools.partial(pick_kernel, chips, batch_count, per_panel), "pick",
                [block_ids], [whole, home], table_shape([0]), 1 << 20,
            )]
        for k in steps:
            piece = pieces[k]
            if chosen is not None:
                piece, parts[1:3], tables[0] = after((piece, parts[1:3], tables[0]))
            pairs += [piece, other_core(piece)]
        if chosen is not None:
            tables.append(call(
                functools.partial(join_kernel, rep_count, held, batch_count, per_panel), "join",
                [], parts, table_shape(held), 1 << 20,
            ))
        last = steps is stages[-1]
        count = len(steps) * batch_count * 2 * per_panel + last * (2 * gram_rows // part_rows)
        picked = jax.ShapeDtypeStruct((count, part_rows, width), jnp.bfloat16)
        chosen = call(
            functools.partial(select_kernel, chips, rep_count, steps, batch_count, per_panel), "select",
            ids, pairs + [gram] * last, (picked,) * rep_count, 1 << 20,
        )
        held = steps
    parts = [chosen[0]] + [over_rep(chosen[part], part) for part in range(1, rep_count)]
    grams = (jax.ShapeDtypeStruct((width, width), jnp.bfloat16),) * 2
    *table, gram_high, gram_low = call(
        functools.partial(join_kernel, rep_count, held, batch_count, per_panel), "join",
        [], parts, table_shape(held) + grams, 1 << 20,
    )
    tables.append(table)
    rows_list, cols_list = [table[0] for table in tables], [table[1] for table in tables]

    lanes = quota * width + LANES
    last_columns = rows_list[-1].shape[1]
    per_batch = functools.partial(jax.ShapeDtypeStruct, dtype=jnp.float32)
    weight, last_targets, partial = call(
        functools.partial(weigh_kernel, chips, [0] + near_first, block_size, batch_count), "weigh",
        [live_counts], [ratings, *rows_list[:-1]],
        (
            per_batch((batch_count, batch_rows, columns)),
            jax.ShapeDtypeStruct((batch_count, 2 * batch_rows, last_columns), jnp.bfloat16),
            per_batch((batch_count, batch_rows, width)),
        ),
        4 * users_here * columns * width,
        [pltpu.VMEM((batch_count, 2 * batch_rows, columns - last_columns), jnp.bfloat16)],
    )
    state = pltpu.VMEM((batch_count, batch_rows, width), jnp.float32)
    send_rows = call(
        functools.partial(solve_kernel, batch_rows, batch_count), "solve",
        [place], [slots, gram_high, gram_low, weight, last_targets, partial, *rows_list, *cols_list],
        jax.ShapeDtypeStruct((device_count, 1, lanes), jnp.float32),
        8 * 4 * users_here * columns * width,
        [
            pltpu.VMEM((batch_count, 2 * batch_rows, columns), jnp.bfloat16),
            state, state, state, pltpu.VMEM((batch_count, batch_rows, 1), jnp.float32),
        ],
    )
    got_rows = lax.all_to_all(send_rows, ("rep", "blk"), split_axis=0, concat_axis=0, tiled=True)
    return call(
        place_kernel, "place", [], [got_rows],
        jax.ShapeDtypeStruct((users_here, width), jnp.float32), 1 << 20,
        [
            pltpu.VMEM((device_count, 1, LANES), jnp.int32),
            pltpu.SMEM((device_count, 1, LANES), jnp.int32), pltpu.SemaphoreType.DMA,
        ],
    )


def solution(mesh):
    placed = (
        P("blk", None),
        P(("rep", "blk"), None),
        P(("rep", "blk"), None),
        P(("rep", "blk")),
        P(("rep", "blk")),
    )
    return jax.shard_map(
        on_device, mesh=mesh, in_specs=placed, out_specs=P(("rep", "blk"), None), check_vma=False
    )
```

```python
import functools
import math
import jax
import jax.numpy as jnp
from jax import lax
from jax.experimental import pallas as pl
from jax.experimental.pallas import tpu as pltpu
from jax.sharding import PartitionSpec as P

ITERS = 8
WIDE_ITERS = 1
TILE = 256
LANES = 128
SPARE_VMEM = 6 * 1024 * 1024

conf_scale = 6.0
ridge_term = 0.5


def dot32(left, right, dims=((1,), (0,))):
    return lax.dot_general(left, right, (dims, ((), ())), preferred_element_type=jnp.float32)


def halves(value):
    high = value.astype(jnp.bfloat16)
    low = (value - high.astype(jnp.float32)).astype(jnp.bfloat16)
    return high, low


def local_slots(core, per_panel):
    for side in range(2):
        parity = core if side == 0 else 1 - core
        for pick in range(per_panel):
            yield side, parity * per_panel + pick


def position(chips, back):
    blk = lax.axis_index("blk")
    return lax.rem(blk, 2), lax.rem(lax.div(blk, 2) + chips - back, chips)


def part_at(refs, reps, part, i, named):
    if part == reps - 1 and len(refs) > reps:
        return refs[part + i], 0
    return refs[part], i * named


def select_kernel(chips, reps, steps, batch_count, per_panel, *refs):
    ids_refs, refs = refs[:reps], refs[reps:]
    panel_refs, refs = refs[:2 * len(steps)], refs[2 * len(steps):]
    gram_refs = [ref for ref in refs if ref.dtype == jnp.float32]
    out_refs = refs[len(gram_refs):]
    slots = 2 * per_panel
    blocks, size, _ = panel_refs[0].shape
    named = batch_count * slots
    for part, ids_ref in enumerate(ids_refs):
        for i, back in enumerate(steps):
            core, chip = position(chips, back)
            out_ref, first = part_at(out_refs, reps, part, i, named)
            for batch in range(batch_count):
                for side, local in local_slots(core, per_panel):
                    block = ids_ref[batch, chip * slots + local]
                    out_ref[first + batch * slots + local] = panel_refs[2 * i + side][lax.rem(block, blocks)]
        for gram_ref in gram_refs:
            out_ref = out_refs[part]
            gram = jnp.concatenate(halves(gram_ref[...]), axis=0)
            out_ref[len(steps) * named:] = gram.reshape(-1, size, gram.shape[1])


def join_kernel(reps, inputs, steps, batch_count, per_panel, *refs):
    part_refs, (rows_ref, cols_ref, *gram_refs) = refs[:inputs], refs[inputs:]
    rep = lax.axis_index("rep")
    size = part_refs[0].shape[1]
    slots = 2 * per_panel
    named = batch_count * slots
    for part in range(reps):
        for i in range(len(steps)):
            ref, first = part_at(part_refs, reps, part, i, named)
            for batch in range(batch_count):
                for local in range(slots):
                    offset = (i * slots + local) * reps * size + (rep ^ part) * size
                    rows_ref[batch, pl.ds(pl.multiple_of(offset, size), size), :] = ref[
                        first + batch * slots + local
                    ]
        ref = part_refs[part]
        extra = ref.shape[0] - len(steps) * named
        half = extra // 2
        for i, gram_ref in enumerate(gram_refs):
            start = len(steps) * named + i * half
            offset = pl.multiple_of((rep ^ part) * size * half, size * half)
            gram_ref[pl.ds(offset, size * half), :] = ref[start:start + half].reshape(size * half, ref.shape[2])
    for batch in range(batch_count):
        cols_ref[batch] = rows_ref[batch].T


def pick_kernel(chips, batch_count, per_panel, ids_ref, own_ref, other_ref, rows_ref, cols_ref):
    core, chip = position(chips, 0)
    slots = 2 * per_panel
    blocks, block_size, _ = own_ref.shape
    for batch in range(batch_count):
        for side, local in local_slots(core, per_panel):
            block = ids_ref[batch, chip * slots + local]
            held = other_ref if side else own_ref
            offset = pl.multiple_of(local * block_size, block_size)
            rows_ref[batch, pl.ds(offset, block_size), :] = held[lax.rem(block, blocks)]
        cols_ref[batch] = rows_ref[batch].T


def weigh_kernel(chips, steps, block_size, batch_count, *refs):
    live_ref, ratings_ref = refs[:2]
    rows_refs, (weight, last, partial, early) = refs[2:-4], refs[-4:]
    users = ratings_ref.shape[0] // batch_count
    columns = ratings_ref.shape[1]
    span = columns // chips
    first_last = columns - last.shape[2]
    for column in range(0, columns, TILE):
        _, chip = position(chips, steps[column // span])
        start = pl.multiple_of(chip * span + column % span, TILE)
        index = start + lax.broadcasted_iota(jnp.int32, (users, TILE), 1)
        for batch in range(batch_count):
            rated = ratings_ref[batch * users:(batch + 1) * users, pl.ds(start, TILE)].astype(jnp.float32)
            live = index < live_ref[batch] * block_size
            scaled = jnp.where(live, conf_scale * rated, 0.0)
            weight[batch, :, column:column + TILE] = scaled
            high, low = halves(jnp.where(live, 1.0 + scaled, 0.0))
            target, at = (early, column) if column < first_last else (last, column - first_last)
            target[batch, :users, at:at + TILE] = high
            target[batch, users:, at:at + TILE] = low
    for batch in range(batch_count):
        total, start = None, 0
        for ref in rows_refs:
            term = dot32(early[batch, :, start:start + ref.shape[1]], ref[batch])
            total = term if total is None else total + term
            start += ref.shape[1]
        partial[batch] = total[:users] + total[users:]


def solve_kernel(users, batch_count, *refs):
    place_ref, slots_ref, gram_high, gram_low, weight, last, partial = refs[:7]
    refs = refs[7:]
    tables = (len(refs) - 6) // 2
    rows_refs, cols_refs, refs = refs[:tables], refs[tables:2 * tables], refs[2 * tables:]
    send_ref, back, x_s, r_s, p_s, n_s = refs
    batches = range(batch_count)
    tiles, starts = [], []
    for table, ref in enumerate(rows_refs):
        start = sum(other.shape[1] for other in rows_refs[:table])
        starts.append(start)
        tiles += [(table, first, start + first) for first in range(0, ref.shape[1], TILE)]

    def back_dot(batch, rows):
        total = None
        for table, start in enumerate(starts):
            size = rows_refs[table].shape[1]
            term = dot32(back[batch, :rows, start:start + size], rows_refs[table][batch])
            total = term if total is None else total + term
        return total

    def put_halves(batch, column, value):
        high, low = halves(value)
        back[batch, :users, column:column + TILE] = high
        back[batch, users:, column:column + TILE] = low

    for batch in batches:
        total = dot32(last[batch], rows_refs[-1][batch])
        target_proj = partial[batch] + total[:users] + total[users:]
        x_s[batch] = jnp.zeros_like(target_proj)
        r_s[batch] = target_proj
        p_s[batch] = target_proj
        n_s[batch] = jnp.sum(target_proj * target_proj, axis=1, keepdims=True)

    def advance(batch, wide, final):
        direction = p_s[batch]
        high, low = halves(direction)
        both = jnp.concatenate([high, low], axis=0)
        for table, first, column in tiles:
            projected = dot32(both if wide else high, cols_refs[table][batch, :, first:first + TILE])
            if wide:
                projected = projected[:users] + projected[users:]
            projected = projected * weight[batch, :, column:column + TILE]
            if wide:
                put_halves(batch, column, projected)
            else:
                back[batch, :users, column:column + TILE] = projected.astype(jnp.bfloat16)
        gram_part = dot32(both, gram_high[...])
        image = gram_part[:users] + gram_part[users:] + dot32(high, gram_low[...]) + ridge_term * direction
        total = back_dot(batch, 2 * users if wide else users)
        if wide:
            total = total[:users] + total[users:]
        image = image + total
        norm_now = n_s[batch]
        step_size = norm_now / jnp.sum(direction * image, axis=1, keepdims=True)
        x_s[batch] = x_s[batch] + step_size * direction
        if final:
            return
        residual = r_s[batch] - step_size * image
        r_s[batch] = residual
        norm_next = jnp.sum(residual * residual, axis=1, keepdims=True)
        p_s[batch] = residual + norm_next / norm_now * direction
        n_s[batch] = norm_next

    width = x_s.shape[2]
    quota = batch_count * users // send_ref.shape[0]
    send_ref[:, :, quota * width:] = slots_ref[...]
    for iteration in range(ITERS):
        for batch in batches:
            advance(batch, iteration < WIDE_ITERS, iteration == ITERS - 1)
            for user in range(users if iteration == ITERS - 1 else 0):
                row = batch * users + user
                lanes = pl.ds(pl.multiple_of(place_ref[1, row], width), width)
                send_ref[place_ref[0, row], :, lanes] = x_s[batch, user:user + 1, :]


def place_kernel(got_ref, out_ref, as_integers, slots, sem):
    width = out_ref.shape[1]
    quota = out_ref.shape[0] // got_ref.shape[0]
    as_integers[...] = got_ref[:, :, quota * width:].astype(jnp.int32)
    copy = pltpu.make_async_copy(as_integers, slots, sem)
    copy.start()
    copy.wait()
    for source in range(got_ref.shape[0]):
        for row in range(quota):
            out_ref[pl.ds(slots[source, 0, row], 1), :] = got_ref[source, :, row * width:(row + 1) * width]


def smem():
    return pl.BlockSpec(memory_space=pltpu.SMEM)


def vmem():
    return pl.BlockSpec(memory_space=pltpu.VMEM)


def call(body, name, small, large, out_shape, flops, scratch=()):
    operands = (*small, *large)
    moved = sum(array.size * array.dtype.itemsize for array in (*operands, *jax.tree.leaves(out_shape)))
    kept = sum(math.prod(array.shape) * 4 for array in scratch if hasattr(array, "shape"))
    return pl.pallas_call(
        body,
        out_shape=out_shape,
        in_specs=[smem()] * len(small) + [vmem()] * len(large),
        out_specs=jax.tree.map(lambda _: vmem(), out_shape),
        scratch_shapes=list(scratch),
        compiler_params=pltpu.CompilerParams(vmem_limit_bytes=moved + kept + SPARE_VMEM),
        cost_estimate=pl.CostEstimate(flops=flops, bytes_accessed=moved, transcendentals=0),
        name=name,
    )(*operands)


def on_device(item_factors, ratings, block_ids, live_counts, owner_rows):
    item_local, width = item_factors.shape
    users_here, columns = ratings.shape
    batch_count, slot_count = block_ids.shape
    batch_rows = users_here // batch_count
    block_size = columns // slot_count
    panel_count = lax.axis_size("blk")
    rep_count = lax.axis_size("rep")
    device_count = rep_count * panel_count
    quota = users_here // device_count
    chips = panel_count // 2
    per_panel = slot_count // panel_count
    blocks = item_local // block_size
    part_rows = block_size // rep_count
    span = 2 * per_panel * block_size
    rep = lax.axis_index("rep")

    def over_blk(array, target):
        return lax.ppermute(array, "blk", [(b, target(b)) for b in range(panel_count)])

    def over_rep(array, part):
        return lax.ppermute(array, "rep", [(r, r ^ part) for r in range(rep_count)])

    def other_core(array):
        return over_blk(array, lambda b: b ^ 1)

    whole = item_factors.reshape(blocks, block_size, width)
    piece = lax.dynamic_slice(whole, (0, rep * part_rows, 0), (blocks, part_rows, width))

    after = lax.optimization_barrier
    whole, piece = after((whole, piece))
    other_whole = other_core(whole)
    pieces = {0: piece}
    for hop in (1, chips - 1):
        pieces[hop] = over_blk(piece, lambda b: (b + 2 * hop) % panel_count)
    other_whole, wanted = after((other_whole, block_ids))
    ids = [wanted] + [over_rep(wanted, part) for part in range(1, rep_count)]

    gram_rows = width // rep_count
    gram = sum(
        dot32(lax.dynamic_slice(panel, (0, rep * gram_rows), (item_local, gram_rows)), panel, ((0,), (0,)))
        for panel in (item_factors, other_whole.reshape(item_local, width))
    )
    pieces[chips - 1], _ = after((pieces[chips - 1], ids))
    ids, gram = after((ids, gram))
    gram = gram + over_blk(gram, lambda b: b ^ 2)
    pieces[1], gram = after((pieces[1], gram))
    for k in range(2, chips - 1):
        pieces[k] = over_blk(pieces[k - 1], lambda b: (b + 2) % panel_count)

    before = (jnp.arange(users_here)[:, None] < jnp.arange(users_here)[None, :]).astype(jnp.bfloat16)
    target_dev = owner_rows // users_here
    goes = target_dev[None, :] == jnp.arange(device_count)[:, None]
    goes_rank = dot32(goes.astype(jnp.bfloat16), before).astype(jnp.int32)
    sent = goes[:, None, :] & (goes_rank[:, None, :] == jnp.arange(quota)[None, :, None])
    slots = jnp.sum(jnp.where(sent, (owner_rows % users_here)[None, None, :], 0), axis=2)
    slots = jnp.pad(slots.astype(jnp.float32), ((0, 0), (0, LANES - quota)))[:, None, :]
    place = jnp.stack([target_dev, width * jnp.sum(jnp.where(goes, goes_rank, 0), axis=0)])

    def table_shape(steps):
        rows = len(steps) * span
        return (
            jax.ShapeDtypeStruct((batch_count, rows, width), jnp.bfloat16),
            jax.ShapeDtypeStruct((batch_count, width, rows), jnp.bfloat16),
        )

    near_first = sorted(range(1, chips), key=lambda k: min(k, chips - k))
    stages = [near_first[i:i + 2] for i in range(0, chips - 1, 2)]
    chosen, tables = None, []
    for steps in stages:
        pairs = []
        if steps is stages[1]:
            chosen, home, gram = after((chosen, other_whole, gram))
            bit = 4
            while bit < panel_count:
                gram = gram + over_blk(gram, lambda b: b ^ bit)
                bit *= 2
        if chosen is not None:
            parts = [chosen[0]] + [
                over_rep(array, min(part, rep_count - 1)) for part, array in enumerate(chosen) if part
            ]
        if steps is stages[1]:
            tables = [call(
                functools.partial(pick_kernel, chips, batch_count, per_panel), "pick",
                [block_ids], [whole, home], table_shape([0]), 1 << 20,
            )]
        for k in steps:
            piece = pieces[k]
            if chosen is not None:
                near = [1, 2, rep_count - 1]
                piece, some, tables[0], gram = after((piece, [parts[part] for part in near], tables[0], gram))
                for part, array in zip(near, some):
                    parts[part] = array
            pairs += [piece, other_core(piece)]
        if chosen is not None:
            tables.append(call(
                functools.partial(join_kernel, rep_count, len(parts), held, batch_count, per_panel), "join",
                [], parts, table_shape(held), 1 << 20,
            ))
        last = steps is stages[-1]
        count = len(steps) * batch_count * 2 * per_panel + last * (2 * gram_rows // part_rows)
        counts = [count] * rep_count
        if steps is stages[0]:
            counts[-1:] = [batch_count * 2 * per_panel] * len(steps)
        picked = tuple(jax.ShapeDtypeStruct((n, part_rows, width), jnp.bfloat16) for n in counts)
        chosen = call(
            functools.partial(select_kernel, chips, rep_count, steps, batch_count, per_panel), "select",
            ids, pairs + [gram] * last, picked, 1 << 20,
        )
        held = steps
    parts = [chosen[0]] + [over_rep(chosen[part], part) for part in range(1, rep_count)]
    grams = (jax.ShapeDtypeStruct((width, width), jnp.bfloat16),) * 2
    *table, gram_high, gram_low = call(
        functools.partial(join_kernel, rep_count, len(parts), held, batch_count, per_panel), "join",
        [], parts, table_shape(held) + grams, 1 << 20,
    )
    tables.append(table)
    rows_list, cols_list = [table[0] for table in tables], [table[1] for table in tables]

    lanes = quota * width + LANES
    last_columns = rows_list[-1].shape[1]
    per_batch = functools.partial(jax.ShapeDtypeStruct, dtype=jnp.float32)
    weight, last_targets, partial = call(
        functools.partial(weigh_kernel, chips, [0] + near_first, block_size, batch_count), "weigh",
        [live_counts], [ratings, *rows_list[:-1]],
        (
            per_batch((batch_count, batch_rows, columns)),
            jax.ShapeDtypeStruct((batch_count, 2 * batch_rows, last_columns), jnp.bfloat16),
            per_batch((batch_count, batch_rows, width)),
        ),
        4 * users_here * columns * width,
        [pltpu.VMEM((batch_count, 2 * batch_rows, columns - last_columns), jnp.bfloat16)],
    )
    state = pltpu.VMEM((batch_count, batch_rows, width), jnp.float32)
    send_rows = call(
        functools.partial(solve_kernel, batch_rows, batch_count), "solve",
        [place], [slots, gram_high, gram_low, weight, last_targets, partial, *rows_list, *cols_list],
        jax.ShapeDtypeStruct((device_count, 1, lanes), jnp.float32),
        8 * 4 * users_here * columns * width,
        [
            pltpu.VMEM((batch_count, 2 * batch_rows, columns), jnp.bfloat16),
            state, state, state, pltpu.VMEM((batch_count, batch_rows, 1), jnp.float32),
        ],
    )
    got_rows = lax.all_to_all(send_rows, ("rep", "blk"), split_axis=0, concat_axis=0, tiled=True)
    return call(
        place_kernel, "place", [], [got_rows],
        jax.ShapeDtypeStruct((users_here, width), jnp.float32), 1 << 20,
        [
            pltpu.VMEM((device_count, 1, LANES), jnp.int32),
            pltpu.SMEM((device_count, 1, LANES), jnp.int32), pltpu.SemaphoreType.DMA,
        ],
    )


def solution(mesh):
    placed = (
        P("blk", None),
        P(("rep", "blk"), None),
        P(("rep", "blk"), None),
        P(("rep", "blk")),
        P(("rep", "blk")),
    )
    return jax.shard_map(
        on_device, mesh=mesh, in_specs=placed, out_specs=P(("rep", "blk"), None), check_vma=False
    )
```

```python
import functools
import math
import jax
import jax.numpy as jnp
from jax import lax
from jax.experimental import pallas as pl
from jax.experimental.pallas import tpu as pltpu
from jax.sharding import PartitionSpec as P

ITERS = 8
WIDE_ITERS = 1
TILE = 512
LANES = 128
SPARE_VMEM = 6 * 1024 * 1024

conf_scale = 6.0
ridge_term = 0.5


def dot32(left, right, dims=((1,), (0,))):
    return lax.dot_general(left, right, (dims, ((), ())), preferred_element_type=jnp.float32)


def halves(value):
    high = value.astype(jnp.bfloat16)
    low = (value - high.astype(jnp.float32)).astype(jnp.bfloat16)
    return high, low


def local_slots(core, per_panel):
    for side in range(2):
        parity = core if side == 0 else 1 - core
        for pick in range(per_panel):
            yield side, parity * per_panel + pick


def position(chips, back):
    blk = lax.axis_index("blk")
    return lax.rem(blk, 2), lax.rem(lax.div(blk, 2) + chips - back, chips)


def part_at(refs, reps, part, i, named):
    if part == reps - 1 and len(refs) > reps:
        return refs[part + i], 0
    return refs[part], i * named


def select_kernel(chips, reps, steps, batch_count, per_panel, *refs):
    ids_refs, refs = refs[:reps], refs[reps:]
    panel_refs, refs = refs[:2 * len(steps)], refs[2 * len(steps):]
    gram_refs = [ref for ref in refs if ref.dtype == jnp.float32]
    out_refs = refs[len(gram_refs):]
    slots = 2 * per_panel
    blocks, size, _ = panel_refs[0].shape
    named = batch_count * slots
    for part, ids_ref in enumerate(ids_refs):
        for i, back in enumerate(steps):
            core, chip = position(chips, back)
            out_ref, first = part_at(out_refs, reps, part, i, named)
            for batch in range(batch_count):
                for side, local in local_slots(core, per_panel):
                    block = ids_ref[batch, chip * slots + local]
                    out_ref[first + batch * slots + local] = panel_refs[2 * i + side][lax.rem(block, blocks)]
        for gram_ref in gram_refs:
            out_ref = out_refs[part]
            gram = jnp.concatenate(halves(gram_ref[...]), axis=0)
            out_ref[len(steps) * named:] = gram.reshape(-1, size, gram.shape[1])


def join_kernel(reps, inputs, steps, batch_count, per_panel, *refs):
    part_refs, (rows_ref, cols_ref, *gram_refs) = refs[:inputs], refs[inputs:]
    rep = lax.axis_index("rep")
    size = part_refs[0].shape[1]
    slots = 2 * per_panel
    named = batch_count * slots
    for part in range(reps):
        for i in range(len(steps)):
            ref, first = part_at(part_refs, reps, part, i, named)
            for batch in range(batch_count):
                for local in range(slots):
                    offset = (i * slots + local) * reps * size + (rep ^ part) * size
                    rows_ref[batch, pl.ds(pl.multiple_of(offset, size), size), :] = ref[
                        first + batch * slots + local
                    ]
        ref = part_refs[part]
        extra = ref.shape[0] - len(steps) * named
        half = extra // 2
        for i, gram_ref in enumerate(gram_refs):
            start = len(steps) * named + i * half
            offset = pl.multiple_of((rep ^ part) * size * half, size * half)
            gram_ref[pl.ds(offset, size * half), :] = ref[start:start + half].reshape(size * half, ref.shape[2])
    for batch in range(batch_count):
        cols_ref[batch] = rows_ref[batch].T


def pick_kernel(chips, batch_count, per_panel, ids_ref, own_ref, other_ref, rows_ref, cols_ref):
    core, chip = position(chips, 0)
    slots = 2 * per_panel
    blocks, block_size, _ = own_ref.shape
    for batch in range(batch_count):
        for side, local in local_slots(core, per_panel):
            block = ids_ref[batch, chip * slots + local]
            held = other_ref if side else own_ref
            offset = pl.multiple_of(local * block_size, block_size)
            rows_ref[batch, pl.ds(offset, block_size), :] = held[lax.rem(block, blocks)]
        cols_ref[batch] = rows_ref[batch].T


def weigh_kernel(chips, steps, block_size, batch_count, *refs):
    live_ref, ratings_ref = refs[:2]
    rows_refs, (weight, last, partial, early) = refs[2:-4], refs[-4:]
    users = ratings_ref.shape[0] // batch_count
    columns = ratings_ref.shape[1]
    span = columns // chips
    first_last = columns - last.shape[2]
    for column in range(0, columns, TILE):
        _, chip = position(chips, steps[column // span])
        start = pl.multiple_of(chip * span + column % span, TILE)
        index = start + lax.broadcasted_iota(jnp.int32, (users, TILE), 1)
        for batch in range(batch_count):
            rated = ratings_ref[batch * users:(batch + 1) * users, pl.ds(start, TILE)].astype(jnp.float32)
            live = index < live_ref[batch] * block_size
            scaled = jnp.where(live, conf_scale * rated, 0.0)
            weight[batch, :, column:column + TILE] = scaled
            high, low = halves(jnp.where(live, 1.0 + scaled, 0.0))
            target, at = (early, column) if column < first_last else (last, column - first_last)
            target[batch, :users, at:at + TILE] = high
            target[batch, users:, at:at + TILE] = low
    for batch in range(batch_count):
        total, start = None, 0
        for ref in rows_refs:
            term = dot32(early[batch, :, start:start + ref.shape[1]], ref[batch])
            total = term if total is None else total + term
            start += ref.shape[1]
        partial[batch] = total[:users] + total[users:]


def solve_kernel(users, batch_count, *refs):
    place_ref, slots_ref, gram_high, gram_low, weight, last, partial = refs[:7]
    refs = refs[7:]
    tables = (len(refs) - 6) // 2
    rows_refs, cols_refs, refs = refs[:tables], refs[tables:2 * tables], refs[2 * tables:]
    send_ref, back, x_s, r_s, p_s, n_s = refs
    batches = range(batch_count)
    tiles, starts = [], []
    for table, ref in enumerate(rows_refs):
        start = sum(other.shape[1] for other in rows_refs[:table])
        starts.append(start)
        tiles += [(table, first, start + first) for first in range(0, ref.shape[1], TILE)]

    def back_dot(batch, rows):
        total = None
        for table, start in enumerate(starts):
            size = rows_refs[table].shape[1]
            term = dot32(back[batch, :rows, start:start + size], rows_refs[table][batch])
            total = term if total is None else total + term
        return total

    def put_halves(batch, column, value):
        high, low = halves(value)
        back[batch, :users, column:column + TILE] = high
        back[batch, users:, column:column + TILE] = low

    for batch in batches:
        total = dot32(last[batch], rows_refs[-1][batch])
        target_proj = partial[batch] + total[:users] + total[users:]
        x_s[batch] = jnp.zeros_like(target_proj)
        r_s[batch] = target_proj
        p_s[batch] = target_proj
        n_s[batch] = jnp.sum(target_proj * target_proj, axis=1, keepdims=True)

    def advance(batch, wide, final):
        direction = p_s[batch]
        high, low = halves(direction)
        both = jnp.concatenate([high, low], axis=0)
        for table, first, column in tiles:
            projected = dot32(both if wide else high, cols_refs[table][batch, :, first:first + TILE])
            if wide:
                projected = projected[:users] + projected[users:]
            projected = projected * weight[batch, :, column:column + TILE]
            if wide:
                put_halves(batch, column, projected)
            else:
                back[batch, :users, column:column + TILE] = projected.astype(jnp.bfloat16)
        gram_part = dot32(both, gram_high[...])
        image = gram_part[:users] + gram_part[users:] + dot32(high, gram_low[...]) + ridge_term * direction
        total = back_dot(batch, 2 * users if wide else users)
        if wide:
            total = total[:users] + total[users:]
        image = image + total
        norm_now = n_s[batch]
        step_size = norm_now / jnp.sum(direction * image, axis=1, keepdims=True)
        x_s[batch] = x_s[batch] + step_size * direction
        if final:
            return
        residual = r_s[batch] - step_size * image
        r_s[batch] = residual
        norm_next = jnp.sum(residual * residual, axis=1, keepdims=True)
        p_s[batch] = residual + norm_next / norm_now * direction
        n_s[batch] = norm_next

    width = x_s.shape[2]
    quota = batch_count * users // send_ref.shape[0]
    send_ref[:, :, quota * width:] = slots_ref[...]
    for iteration in range(ITERS):
        for batch in batches:
            advance(batch, iteration < WIDE_ITERS, iteration == ITERS - 1)
            for user in range(users if iteration == ITERS - 1 else 0):
                row = batch * users + user
                lanes = pl.ds(pl.multiple_of(place_ref[1, row], width), width)
                send_ref[place_ref[0, row], :, lanes] = x_s[batch, user:user + 1, :]


def place_kernel(got_ref, out_ref, as_integers, slots, sem):
    width = out_ref.shape[1]
    quota = out_ref.shape[0] // got_ref.shape[0]
    as_integers[...] = got_ref[:, :, quota * width:].astype(jnp.int32)
    copy = pltpu.make_async_copy(as_integers, slots, sem)
    copy.start()
    copy.wait()
    for source in range(got_ref.shape[0]):
        for row in range(quota):
            out_ref[pl.ds(slots[source, 0, row], 1), :] = got_ref[source, :, row * width:(row + 1) * width]


def smem():
    return pl.BlockSpec(memory_space=pltpu.SMEM)


def vmem():
    return pl.BlockSpec(memory_space=pltpu.VMEM)


def call(body, name, small, large, out_shape, flops, scratch=()):
    operands = (*small, *large)
    moved = sum(array.size * array.dtype.itemsize for array in (*operands, *jax.tree.leaves(out_shape)))
    kept = sum(math.prod(array.shape) * 4 for array in scratch if hasattr(array, "shape"))
    return pl.pallas_call(
        body,
        out_shape=out_shape,
        in_specs=[smem()] * len(small) + [vmem()] * len(large),
        out_specs=jax.tree.map(lambda _: vmem(), out_shape),
        scratch_shapes=list(scratch),
        compiler_params=pltpu.CompilerParams(vmem_limit_bytes=moved + kept + SPARE_VMEM),
        cost_estimate=pl.CostEstimate(flops=flops, bytes_accessed=moved, transcendentals=0),
        name=name,
    )(*operands)


def on_device(item_factors, ratings, block_ids, live_counts, owner_rows):
    item_local, width = item_factors.shape
    users_here, columns = ratings.shape
    batch_count, slot_count = block_ids.shape
    batch_rows = users_here // batch_count
    block_size = columns // slot_count
    panel_count = lax.axis_size("blk")
    rep_count = lax.axis_size("rep")
    device_count = rep_count * panel_count
    quota = users_here // device_count
    chips = panel_count // 2
    per_panel = slot_count // panel_count
    blocks = item_local // block_size
    part_rows = block_size // rep_count
    span = 2 * per_panel * block_size
    rep = lax.axis_index("rep")

    def over_blk(array, target):
        return lax.ppermute(array, "blk", [(b, target(b)) for b in range(panel_count)])

    def over_rep(array, part):
        return lax.ppermute(array, "rep", [(r, r ^ part) for r in range(rep_count)])

    def other_core(array):
        return over_blk(array, lambda b: b ^ 1)

    whole = item_factors.reshape(blocks, block_size, width)
    piece = lax.dynamic_slice(whole, (0, rep * part_rows, 0), (blocks, part_rows, width))

    after = lax.optimization_barrier
    whole, piece = after((whole, piece))
    other_whole = other_core(whole)
    pieces = {0: piece}
    for hop in (1, chips - 1):
        pieces[hop] = over_blk(piece, lambda b: (b + 2 * hop) % panel_count)
    other_whole, wanted = after((other_whole, block_ids))
    ids = [wanted] + [over_rep(wanted, part) for part in range(1, rep_count)]

    gram_rows = width // rep_count
    gram = sum(
        dot32(lax.dynamic_slice(panel, (0, rep * gram_rows), (item_local, gram_rows)), panel, ((0,), (0,)))
        for panel in (item_factors, other_whole.reshape(item_local, width))
    )
    pieces[chips - 1], _ = after((pieces[chips - 1], ids))
    ids, gram = after((ids, gram))
    gram = gram + over_blk(gram, lambda b: b ^ 2)
    pieces[1], gram = after((pieces[1], gram))
    for k in range(2, chips - 1):
        pieces[k] = over_blk(pieces[k - 1], lambda b: (b + 2) % panel_count)

    before = (jnp.arange(users_here)[:, None] < jnp.arange(users_here)[None, :]).astype(jnp.bfloat16)
    target_dev = owner_rows // users_here
    goes = target_dev[None, :] == jnp.arange(device_count)[:, None]
    goes_rank = dot32(goes.astype(jnp.bfloat16), before).astype(jnp.int32)
    sent = goes[:, None, :] & (goes_rank[:, None, :] == jnp.arange(quota)[None, :, None])
    slots = jnp.sum(jnp.where(sent, (owner_rows % users_here)[None, None, :], 0), axis=2)
    slots = jnp.pad(slots.astype(jnp.float32), ((0, 0), (0, LANES - quota)))[:, None, :]
    place = jnp.stack([target_dev, width * jnp.sum(jnp.where(goes, goes_rank, 0), axis=0)])

    def table_shape(steps):
        rows = len(steps) * span
        return (
            jax.ShapeDtypeStruct((batch_count, rows, width), jnp.bfloat16),
            jax.ShapeDtypeStruct((batch_count, width, rows), jnp.bfloat16),
        )

    near_first = sorted(range(1, chips), key=lambda k: min(k, chips - k))
    stages = [near_first[i:i + 2] for i in range(0, chips - 1, 2)]
    chosen, tables = None, []
    for steps in stages:
        pairs = []
        if steps is stages[1]:
            chosen, home, gram = after((chosen, other_whole, gram))
            bit = 4
            while bit < panel_count:
                gram = gram + over_blk(gram, lambda b: b ^ bit)
                bit *= 2
        if chosen is not None:
            parts = [chosen[0]] + [
                over_rep(array, min(part, rep_count - 1)) for part, array in enumerate(chosen) if part
            ]
        if steps is stages[1]:
            tables = [call(
                functools.partial(pick_kernel, chips, batch_count, per_panel), "pick",
                [block_ids], [whole, home], table_shape([0]), 1 << 20,
            )]
        for k in steps:
            piece = pieces[k]
            if chosen is not None:
                near = [1, 2, rep_count - 1]
                piece, some, tables[0], gram = after((piece, [parts[part] for part in near], tables[0], gram))
                for part, array in zip(near, some):
                    parts[part] = array
            pairs += [piece, other_core(piece)]
        if chosen is not None:
            tables.append(call(
                functools.partial(join_kernel, rep_count, len(parts), held, batch_count, per_panel), "join",
                [], parts, table_shape(held), 1 << 20,
            ))
        last = steps is stages[-1]
        count = len(steps) * batch_count * 2 * per_panel + last * (2 * gram_rows // part_rows)
        counts = [count] * rep_count
        if steps is stages[0]:
            counts[-1:] = [batch_count * 2 * per_panel] * len(steps)
        picked = tuple(jax.ShapeDtypeStruct((n, part_rows, width), jnp.bfloat16) for n in counts)
        chosen = call(
            functools.partial(select_kernel, chips, rep_count, steps, batch_count, per_panel), "select",
            ids, pairs + [gram] * last, picked, 1 << 20,
        )
        held = steps
    parts = [chosen[0]] + [over_rep(chosen[part], part) for part in range(1, rep_count)]
    grams = (jax.ShapeDtypeStruct((width, width), jnp.bfloat16),) * 2
    *table, gram_high, gram_low = call(
        functools.partial(join_kernel, rep_count, len(parts), held, batch_count, per_panel), "join",
        [], parts, table_shape(held) + grams, 1 << 20,
    )
    tables.append(table)
    rows_list, cols_list = [table[0] for table in tables], [table[1] for table in tables]

    lanes = quota * width + LANES
    last_columns = rows_list[-1].shape[1]
    per_batch = functools.partial(jax.ShapeDtypeStruct, dtype=jnp.float32)
    weight, last_targets, partial = call(
        functools.partial(weigh_kernel, chips, [0] + near_first, block_size, batch_count), "weigh",
        [live_counts], [ratings, *rows_list[:-1]],
        (
            per_batch((batch_count, batch_rows, columns)),
            jax.ShapeDtypeStruct((batch_count, 2 * batch_rows, last_columns), jnp.bfloat16),
            per_batch((batch_count, batch_rows, width)),
        ),
        4 * users_here * columns * width,
        [pltpu.VMEM((batch_count, 2 * batch_rows, columns - last_columns), jnp.bfloat16)],
    )
    state = pltpu.VMEM((batch_count, batch_rows, width), jnp.float32)
    send_rows = call(
        functools.partial(solve_kernel, batch_rows, batch_count), "solve",
        [place], [slots, gram_high, gram_low, weight, last_targets, partial, *rows_list, *cols_list],
        jax.ShapeDtypeStruct((device_count, 1, lanes), jnp.float32),
        8 * 4 * users_here * columns * width,
        [
            pltpu.VMEM((batch_count, 2 * batch_rows, columns), jnp.bfloat16),
            state, state, state, pltpu.VMEM((batch_count, batch_rows, 1), jnp.float32),
        ],
    )
    got_rows = lax.all_to_all(send_rows, ("rep", "blk"), split_axis=0, concat_axis=0, tiled=True)
    return call(
        place_kernel, "place", [], [got_rows],
        jax.ShapeDtypeStruct((users_here, width), jnp.float32), 1 << 20,
        [
            pltpu.VMEM((device_count, 1, LANES), jnp.int32),
            pltpu.SMEM((device_count, 1, LANES), jnp.int32), pltpu.SemaphoreType.DMA,
        ],
    )


def solution(mesh):
    placed = (
        P("blk", None),
        P(("rep", "blk"), None),
        P(("rep", "blk"), None),
        P(("rep", "blk")),
        P(("rep", "blk")),
    )
    return jax.shard_map(
        on_device, mesh=mesh, in_specs=placed, out_specs=P(("rep", "blk"), None), check_vma=False
    )
```

```python
import functools
import math
import jax
import jax.numpy as jnp
from jax import lax
from jax.experimental import pallas as pl
from jax.experimental.pallas import tpu as pltpu
from jax.sharding import PartitionSpec as P

ITERS = 8
WIDE_ITERS = 1
EXACT_ITERS = 3
TILE = 256
LANES = 128
SPARE_VMEM = 6 * 1024 * 1024

conf_scale = 6.0
ridge_term = 0.5


def dot32(left, right, dims=((1,), (0,))):
    return lax.dot_general(left, right, (dims, ((), ())), preferred_element_type=jnp.float32)


def halves(value):
    high = value.astype(jnp.bfloat16)
    low = (value - high.astype(jnp.float32)).astype(jnp.bfloat16)
    return high, low


def local_slots(core, per_panel):
    for side in range(2):
        parity = core if side == 0 else 1 - core
        for pick in range(per_panel):
            yield side, parity * per_panel + pick


def position(chips, back):
    blk = lax.axis_index("blk")
    return lax.rem(blk, 2), lax.rem(lax.div(blk, 2) + chips - back, chips)


def part_at(refs, reps, part, i, named):
    if part == reps - 1 and len(refs) > reps:
        return refs[part + i], 0
    return refs[part], i * named


def select_kernel(chips, reps, steps, batch_count, per_panel, *refs):
    ids_refs, refs = refs[:reps], refs[reps:]
    panel_refs, refs = refs[:2 * len(steps)], refs[2 * len(steps):]
    gram_refs = [ref for ref in refs if ref.dtype == jnp.float32]
    out_refs = refs[len(gram_refs):]
    slots = 2 * per_panel
    blocks, size, _ = panel_refs[0].shape
    named = batch_count * slots
    for part, ids_ref in enumerate(ids_refs):
        for i, back in enumerate(steps):
            core, chip = position(chips, back)
            out_ref, first = part_at(out_refs, reps, part, i, named)
            for batch in range(batch_count):
                for side, local in local_slots(core, per_panel):
                    block = ids_ref[batch, chip * slots + local]
                    out_ref[first + batch * slots + local] = panel_refs[2 * i + side][lax.rem(block, blocks)]
        for gram_ref in gram_refs:
            out_ref = out_refs[part]
            gram = jnp.concatenate(halves(gram_ref[...]), axis=0)
            out_ref[len(steps) * named:] = gram.reshape(-1, size, gram.shape[1])


def join_kernel(reps, inputs, steps, batch_count, per_panel, *refs):
    part_refs, (rows_ref, cols_ref, *gram_refs) = refs[:inputs], refs[inputs:]
    rep = lax.axis_index("rep")
    size = part_refs[0].shape[1]
    slots = 2 * per_panel
    named = batch_count * slots
    for part in range(reps):
        for i in range(len(steps)):
            ref, first = part_at(part_refs, reps, part, i, named)
            for batch in range(batch_count):
                for local in range(slots):
                    offset = (i * slots + local) * reps * size + (rep ^ part) * size
                    rows_ref[batch, pl.ds(pl.multiple_of(offset, size), size), :] = ref[
                        first + batch * slots + local
                    ]
        ref = part_refs[part]
        extra = ref.shape[0] - len(steps) * named
        half = extra // 2
        for i, gram_ref in enumerate(gram_refs):
            start = len(steps) * named + i * half
            offset = pl.multiple_of((rep ^ part) * size * half, size * half)
            gram_ref[pl.ds(offset, size * half), :] = ref[start:start + half].reshape(size * half, ref.shape[2])
    for batch in range(batch_count):
        cols_ref[batch] = rows_ref[batch].T


def pick_kernel(chips, batch_count, per_panel, ids_ref, own_ref, other_ref, rows_ref, cols_ref):
    core, chip = position(chips, 0)
    slots = 2 * per_panel
    blocks, block_size, _ = own_ref.shape
    for batch in range(batch_count):
        for side, local in local_slots(core, per_panel):
            block = ids_ref[batch, chip * slots + local]
            held = other_ref if side else own_ref
            offset = pl.multiple_of(local * block_size, block_size)
            rows_ref[batch, pl.ds(offset, block_size), :] = held[lax.rem(block, blocks)]
        cols_ref[batch] = rows_ref[batch].T


def weigh_kernel(chips, steps, block_size, batch_count, *refs):
    live_ref, ratings_ref = refs[:2]
    rows_refs, (weight, last, partial, early) = refs[2:-4], refs[-4:]
    users = ratings_ref.shape[0] // batch_count
    columns = ratings_ref.shape[1]
    span = columns // chips
    first_last = columns - last.shape[2]
    for column in range(0, columns, TILE):
        _, chip = position(chips, steps[column // span])
        start = pl.multiple_of(chip * span + column % span, TILE)
        index = start + lax.broadcasted_iota(jnp.int32, (users, TILE), 1)
        for batch in range(batch_count):
            rated = ratings_ref[batch * users:(batch + 1) * users, pl.ds(start, TILE)].astype(jnp.float32)
            live = index < live_ref[batch] * block_size
            scaled = jnp.where(live, conf_scale * rated, 0.0)
            weight[batch, :, column:column + TILE] = scaled
            high, low = halves(jnp.where(live, 1.0 + scaled, 0.0))
            target, at = (early, column) if column < first_last else (last, column - first_last)
            target[batch, :users, at:at + TILE] = high
            target[batch, users:, at:at + TILE] = low
    for batch in range(batch_count):
        total, start = None, 0
        for ref in rows_refs:
            term = dot32(early[batch, :, start:start + ref.shape[1]], ref[batch])
            total = term if total is None else total + term
            start += ref.shape[1]
        partial[batch] = total[:users] + total[users:]


def solve_kernel(users, batch_count, *refs):
    place_ref, slots_ref, gram_high, gram_low, weight, last, partial = refs[:7]
    refs = refs[7:]
    tables = (len(refs) - 6) // 2
    rows_refs, cols_refs, refs = refs[:tables], refs[tables:2 * tables], refs[2 * tables:]
    send_ref, back, x_s, r_s, p_s, n_s = refs
    batches = range(batch_count)
    tiles, starts = [], []
    for table, ref in enumerate(rows_refs):
        start = sum(other.shape[1] for other in rows_refs[:table])
        starts.append(start)
        tiles += [(table, first, start + first) for first in range(0, ref.shape[1], TILE)]

    def back_dot(batch, rows):
        total = None
        for table, start in enumerate(starts):
            size = rows_refs[table].shape[1]
            term = dot32(back[batch, :rows, start:start + size], rows_refs[table][batch])
            total = term if total is None else total + term
        return total

    def put_halves(batch, column, value):
        high, low = halves(value)
        back[batch, :users, column:column + TILE] = high
        back[batch, users:, column:column + TILE] = low

    for batch in batches:
        total = dot32(last[batch], rows_refs[-1][batch])
        target_proj = partial[batch] + total[:users] + total[users:]
        x_s[batch] = jnp.zeros_like(target_proj)
        r_s[batch] = target_proj
        p_s[batch] = target_proj
        n_s[batch] = jnp.sum(target_proj * target_proj, axis=1, keepdims=True)

    def advance(batch, wide, exact, final):
        direction = p_s[batch]
        high, low = halves(direction)
        both = jnp.concatenate([high, low], axis=0)
        for table, first, column in tiles:
            projected = dot32(both if wide else high, cols_refs[table][batch, :, first:first + TILE])
            if wide:
                projected = projected[:users] + projected[users:]
            projected = projected * weight[batch, :, column:column + TILE]
            if wide:
                put_halves(batch, column, projected)
            else:
                back[batch, :users, column:column + TILE] = projected.astype(jnp.bfloat16)
        gram_part = dot32(both if exact else high, gram_high[...])
        if exact:
            gram_part = gram_part[:users] + gram_part[users:]
        image = gram_part + dot32(high, gram_low[...]) + ridge_term * direction
        total = back_dot(batch, 2 * users if wide else users)
        if wide:
            total = total[:users] + total[users:]
        image = image + total
        norm_now = n_s[batch]
        step_size = norm_now / jnp.sum(direction * image, axis=1, keepdims=True)
        x_s[batch] = x_s[batch] + step_size * direction
        if final:
            return
        residual = r_s[batch] - step_size * image
        r_s[batch] = residual
        norm_next = jnp.sum(residual * residual, axis=1, keepdims=True)
        p_s[batch] = residual + norm_next / norm_now * direction
        n_s[batch] = norm_next

    width = x_s.shape[2]
    quota = batch_count * users // send_ref.shape[0]
    send_ref[:, :, quota * width:] = slots_ref[...]
    for iteration in range(ITERS):
        for batch in batches:
            advance(batch, iteration < WIDE_ITERS, iteration < EXACT_ITERS, iteration == ITERS - 1)
            for user in range(users if iteration == ITERS - 1 else 0):
                row = batch * users + user
                lanes = pl.ds(pl.multiple_of(place_ref[1, row], width), width)
                send_ref[place_ref[0, row], :, lanes] = x_s[batch, user:user + 1, :]


def place_kernel(got_ref, out_ref, as_integers, slots, sem):
    width = out_ref.shape[1]
    quota = out_ref.shape[0] // got_ref.shape[0]
    as_integers[...] = got_ref[:, :, quota * width:].astype(jnp.int32)
    copy = pltpu.make_async_copy(as_integers, slots, sem)
    copy.start()
    copy.wait()
    for source in range(got_ref.shape[0]):
        for row in range(quota):
            out_ref[pl.ds(slots[source, 0, row], 1), :] = got_ref[source, :, row * width:(row + 1) * width]


def smem():
    return pl.BlockSpec(memory_space=pltpu.SMEM)


def vmem():
    return pl.BlockSpec(memory_space=pltpu.VMEM)


def call(body, name, small, large, out_shape, flops, scratch=()):
    operands = (*small, *large)
    moved = sum(array.size * array.dtype.itemsize for array in (*operands, *jax.tree.leaves(out_shape)))
    kept = sum(math.prod(array.shape) * 4 for array in scratch if hasattr(array, "shape"))
    return pl.pallas_call(
        body,
        out_shape=out_shape,
        in_specs=[smem()] * len(small) + [vmem()] * len(large),
        out_specs=jax.tree.map(lambda _: vmem(), out_shape),
        scratch_shapes=list(scratch),
        compiler_params=pltpu.CompilerParams(vmem_limit_bytes=moved + kept + SPARE_VMEM),
        cost_estimate=pl.CostEstimate(flops=flops, bytes_accessed=moved, transcendentals=0),
        name=name,
    )(*operands)


def on_device(item_factors, ratings, block_ids, live_counts, owner_rows):
    item_local, width = item_factors.shape
    users_here, columns = ratings.shape
    batch_count, slot_count = block_ids.shape
    batch_rows = users_here // batch_count
    block_size = columns // slot_count
    panel_count = lax.axis_size("blk")
    rep_count = lax.axis_size("rep")
    device_count = rep_count * panel_count
    quota = users_here // device_count
    chips = panel_count // 2
    per_panel = slot_count // panel_count
    blocks = item_local // block_size
    part_rows = block_size // rep_count
    span = 2 * per_panel * block_size
    rep = lax.axis_index("rep")

    def over_blk(array, target):
        return lax.ppermute(array, "blk", [(b, target(b)) for b in range(panel_count)])

    def over_rep(array, part):
        return lax.ppermute(array, "rep", [(r, r ^ part) for r in range(rep_count)])

    def other_core(array):
        return over_blk(array, lambda b: b ^ 1)

    whole = item_factors.reshape(blocks, block_size, width)
    piece = lax.dynamic_slice(whole, (0, rep * part_rows, 0), (blocks, part_rows, width))

    after = lax.optimization_barrier
    whole, piece = after((whole, piece))
    other_whole = other_core(whole)
    pieces = {0: piece}
    for hop in (1, chips - 1):
        pieces[hop] = over_blk(piece, lambda b: (b + 2 * hop) % panel_count)
    other_whole, wanted = after((other_whole, block_ids))
    ids = [wanted] + [over_rep(wanted, part) for part in range(1, rep_count)]

    gram_rows = width // rep_count
    gram = sum(
        dot32(lax.dynamic_slice(panel, (0, rep * gram_rows), (item_local, gram_rows)), panel, ((0,), (0,)))
        for panel in (item_factors, other_whole.reshape(item_local, width))
    )
    pieces[chips - 1], _ = after((pieces[chips - 1], ids))
    ids, gram = after((ids, gram))
    gram = gram + over_blk(gram, lambda b: b ^ 2)
    pieces[1], gram = after((pieces[1], gram))
    for k in range(2, chips - 1):
        pieces[k] = over_blk(pieces[k - 1], lambda b: (b + 2) % panel_count)

    before = (jnp.arange(users_here)[:, None] < jnp.arange(users_here)[None, :]).astype(jnp.bfloat16)
    target_dev = owner_rows // users_here
    goes = target_dev[None, :] == jnp.arange(device_count)[:, None]
    goes_rank = dot32(goes.astype(jnp.bfloat16), before).astype(jnp.int32)
    sent = goes[:, None, :] & (goes_rank[:, None, :] == jnp.arange(quota)[None, :, None])
    slots = jnp.sum(jnp.where(sent, (owner_rows % users_here)[None, None, :], 0), axis=2)
    slots = jnp.pad(slots.astype(jnp.float32), ((0, 0), (0, LANES - quota)))[:, None, :]
    place = jnp.stack([target_dev, width * jnp.sum(jnp.where(goes, goes_rank, 0), axis=0)])

    def table_shape(steps):
        rows = len(steps) * span
        return (
            jax.ShapeDtypeStruct((batch_count, rows, width), jnp.bfloat16),
            jax.ShapeDtypeStruct((batch_count, width, rows), jnp.bfloat16),
        )

    near_first = sorted(range(1, chips), key=lambda k: min(k, chips - k))
    stages = [near_first[i:i + 2] for i in range(0, chips - 1, 2)]
    chosen, tables = None, []
    for steps in stages:
        pairs = []
        if steps is stages[1]:
            chosen, home, gram = after((chosen, other_whole, gram))
            bit = 4
            while bit < panel_count:
                gram = gram + over_blk(gram, lambda b: b ^ bit)
                bit *= 2
        if chosen is not None:
            parts = [chosen[0]] + [
                over_rep(array, min(part, rep_count - 1)) for part, array in enumerate(chosen) if part
            ]
        if steps is stages[1]:
            tables = [call(
                functools.partial(pick_kernel, chips, batch_count, per_panel), "pick",
                [block_ids], [whole, home], table_shape([0]), 1 << 20,
            )]
        for k in steps:
            piece = pieces[k]
            if chosen is not None:
                near = [1, 2, rep_count - 1]
                piece, some, tables[0], gram = after((piece, [parts[part] for part in near], tables[0], gram))
                for part, array in zip(near, some):
                    parts[part] = array
            pairs += [piece, other_core(piece)]
        if chosen is not None:
            tables.append(call(
                functools.partial(join_kernel, rep_count, len(parts), held, batch_count, per_panel), "join",
                [], parts, table_shape(held), 1 << 20,
            ))
        last = steps is stages[-1]
        count = len(steps) * batch_count * 2 * per_panel + last * (2 * gram_rows // part_rows)
        counts = [count] * rep_count
        if steps is stages[0]:
            counts[-1:] = [batch_count * 2 * per_panel] * len(steps)
        picked = tuple(jax.ShapeDtypeStruct((n, part_rows, width), jnp.bfloat16) for n in counts)
        chosen = call(
            functools.partial(select_kernel, chips, rep_count, steps, batch_count, per_panel), "select",
            ids, pairs + [gram] * last, picked, 1 << 20,
        )
        held = steps
    parts = [chosen[0]] + [over_rep(chosen[part], part) for part in range(1, rep_count)]
    grams = (jax.ShapeDtypeStruct((width, width), jnp.bfloat16),) * 2
    *table, gram_high, gram_low = call(
        functools.partial(join_kernel, rep_count, len(parts), held, batch_count, per_panel), "join",
        [], parts, table_shape(held) + grams, 1 << 20,
    )
    tables.append(table)
    rows_list, cols_list = [table[0] for table in tables], [table[1] for table in tables]

    lanes = quota * width + LANES
    last_columns = rows_list[-1].shape[1]
    per_batch = functools.partial(jax.ShapeDtypeStruct, dtype=jnp.float32)
    weight, last_targets, partial = call(
        functools.partial(weigh_kernel, chips, [0] + near_first, block_size, batch_count), "weigh",
        [live_counts], [ratings, *rows_list[:-1]],
        (
            per_batch((batch_count, batch_rows, columns)),
            jax.ShapeDtypeStruct((batch_count, 2 * batch_rows, last_columns), jnp.bfloat16),
            per_batch((batch_count, batch_rows, width)),
        ),
        4 * users_here * columns * width,
        [pltpu.VMEM((batch_count, 2 * batch_rows, columns - last_columns), jnp.bfloat16)],
    )
    state = pltpu.VMEM((batch_count, batch_rows, width), jnp.float32)
    send_rows = call(
        functools.partial(solve_kernel, batch_rows, batch_count), "solve",
        [place], [slots, gram_high, gram_low, weight, last_targets, partial, *rows_list, *cols_list],
        jax.ShapeDtypeStruct((device_count, 1, lanes), jnp.float32),
        8 * 4 * users_here * columns * width,
        [
            pltpu.VMEM((batch_count, 2 * batch_rows, columns), jnp.bfloat16),
            state, state, state, pltpu.VMEM((batch_count, batch_rows, 1), jnp.float32),
        ],
    )
    got_rows = lax.all_to_all(send_rows, ("rep", "blk"), split_axis=0, concat_axis=0, tiled=True)
    return call(
        place_kernel, "place", [], [got_rows],
        jax.ShapeDtypeStruct((users_here, width), jnp.float32), 1 << 20,
        [
            pltpu.VMEM((device_count, 1, LANES), jnp.int32),
            pltpu.SMEM((device_count, 1, LANES), jnp.int32), pltpu.SemaphoreType.DMA,
        ],
    )


def solution(mesh):
    placed = (
        P("blk", None),
        P(("rep", "blk"), None),
        P(("rep", "blk"), None),
        P(("rep", "blk")),
        P(("rep", "blk")),
    )
    return jax.shard_map(
        on_device, mesh=mesh, in_specs=placed, out_specs=P(("rep", "blk"), None), check_vma=False
    )
```
